512 devices in a mesh: clip: 16 (over y_hi, z), seq: 32 (over y_lo, x, core).
Axes of the slice: x: 4, y: 8 (y_hi: 2, y_lo: 4; y = y_hi * 4 + y_lo), z: 8, core: 2. Of those that a mesh axis runs over, the one named last changes fastest.
Arguments:
- video_query: bfloat16 [131072, 1536], P(('clip', 'seq')), may hold values from -7 to 7
- audio_key: bfloat16 [65536, 1536], P(('clip', 'seq')), may hold values from -7 to 7
- audio_value: bfloat16 [65536, 1536], P(('clip', 'seq')), may hold values from -6 to 6
- null_kv: bfloat16 [2, 1536], replicated, may hold values from -4 to 4
- audio_keep: int32 [65536], P('clip'), may hold values 0 or 1
- clip_lengths: int32 [16, 4], P('clip'), may hold values from 1 to 2048, as said below
- out_grad: bfloat16 [131072, 1536], P(('clip', 'seq')), may hold values from -6 to 6
Outputs:
- attended: bfloat16 [131072, 1536], P(('clip', 'seq'))
- query_grad: bfloat16 [131072, 1536], P(('clip', 'seq'))
- key_grad: bfloat16 [65536, 1536], P(('clip', 'seq'))
- value_grad: bfloat16 [65536, 1536], P(('clip', 'seq'))
- null_grad: float32 [2, 1536], replicated
The draws below stay inside these ranges and needn't reach their ends.
Inputs may be any that keep to these rules, and one draw needn't show every extreme that they name: `clip_lengths`: each row holds 3 clip lengths in packing order and then the padding at the group's end; a row sums to 4096, its largest entry is 2048, and the padding is 1 to 256 tokens.
All inputs are finite; a program needn't handle non-finite values. No bound on the sum of `audio_keep` on one device may be relied on, other than what follows from the above.
Results may differ from the reference program's by a relative error of at most 0.035.
Values may be sent and summed in bfloat16 or wider, within the bound.
No kernel may reach another device: no remote copies, remote signals or barrier semaphores. Data moves between devices by JAX's collectives and lax.ppermute only.
A program may use at most 64 MiB of HBM per device.

```python
import jax
import jax.numpy as jnp
from jax import lax

HEADS = 12
HEAD = 128
AUD_DEV = 128
VID_DEV = 256
WIDTH = 1536
WINDOW = 128
ATOK = 4096
VTOK = 8192
MOST = 2048
AUDIO = 65536
VIDEO = 131072
N_CLIP = 16
N_SEQ = 32


def draw_video_query(key, part):
    key = jax.random.fold_in(key, 11)
    values = jax.random.truncated_normal(key, -6.0, 6.0, (VIDEO, HEADS, HEAD), jnp.float32)
    return values.reshape(VIDEO, HEADS * HEAD).astype(jnp.bfloat16)


def draw_audio_key(key, part):
    key = jax.random.fold_in(key, 23)
    values = jax.random.truncated_normal(key, -6.0, 6.0, (AUDIO, HEADS, HEAD), jnp.float32)
    return values.reshape(AUDIO, HEADS * HEAD).astype(jnp.bfloat16)


def draw_clip_lengths(key, part):
    key = jax.random.fold_in(key, 37)
    first, second, third = jax.random.split(key, 3)
    padding = jax.random.randint(first, (N_CLIP,), 1, ATOK // 16 + 1).astype(jnp.int32)
    remain = ATOK - MOST - padding
    share = jax.random.randint(second, (N_CLIP,), 0, 1 << 20).astype(jnp.int32)
    lowest = remain // 4
    span = remain - 2 * lowest + 1
    first_clip = lowest + share % span
    place = jax.random.randint(third, (N_CLIP,), 0, 3).astype(jnp.int32)
    slots = jnp.arange(3, dtype=jnp.int32)
    order = (slots[None, :] - place[:, None] - 1) % 3
    clips = jnp.where(order == 2, MOST, jnp.where(order == 0, first_clip[:, None], (remain - first_clip)[:, None]))
    return jnp.concatenate([clips, padding[:, None]], axis=1).astype(jnp.int32)


def touch_ends(result, own_key, smallest, largest):
    longest = result.shape.index(max(result.shape))
    spots = []
    for shift in (0, 1):
        where = [jax.random.randint(jax.random.fold_in(own_key, axis), (), 0, length) for axis, length in enumerate(result.shape)]
        where[longest] = (where[longest] + shift) % result.shape[longest]
        spots.append(tuple(where))
    return result.at[spots[0]].set(smallest).at[spots[1]].set(largest)


def steps_of(key, extent, shards, low, largest):
    def one(dim, blocks):
        steps = jax.random.uniform(jax.random.fold_in(jax.random.fold_in(key, 6), dim), (blocks,), jnp.float32, low / len(shards), largest / len(shards))
        return jnp.repeat(jnp.exp(steps), extent[dim] // blocks).reshape((-1,) + (1,) * (len(extent) - dim - 1))

    factor_of = one(*shards[0])
    for cut in shards[1:]:
        factor_of = factor_of * one(*cut)
    return factor_of


def centred(own_key, extent, spread, bound, cuts=(), held_as=jnp.bfloat16):
    result = jax.random.normal(own_key, extent, jnp.float32) * spread
    if len(cuts) > 0:
        result = steps_of(own_key, extent, cuts, -0.22, 0.18) * result
    return jnp.clip(result, min=-bound, max=bound).astype(held_as)


def setup_inputs(seed: int = 0) -> dict:
    arg_keys = jax.random.split(jax.random.key(seed), 8)
    video_query = draw_video_query(jax.random.fold_in(arg_keys[7], 71), 0)
    audio_key = draw_audio_key(jax.random.fold_in(arg_keys[7], 71), 0)
    audio_value = centred(arg_keys[2], (AUDIO, WIDTH), 1.0, 6.0, ((0, 512),))
    null_kv = centred(arg_keys[3], (2, WIDTH), 1.0, 4.0)
    audio_keep = touch_ends((jax.random.randint(arg_keys[4], (AUDIO,), 0, 8) < 7).astype(jnp.int32), jax.random.fold_in(arg_keys[4], 1), 0, 1)
    clip_lengths = draw_clip_lengths(jax.random.fold_in(arg_keys[7], 71), 0)
    out_grad = centred(arg_keys[6], (VIDEO, WIDTH), 1.0, 6.0, ((0, 512),))
    return dict(video_query=video_query, audio_key=audio_key, audio_value=audio_value, null_kv=null_kv, audio_keep=audio_keep, clip_lengths=clip_lengths, out_grad=out_grad)


def segment_of(positions, bounds):
    return jnp.sum((positions[:, None] >= bounds[None, :-1]).astype(jnp.int32), axis=1)


def allowed_pairs(query_pos, key_pos, bounds, keep_rows, total_audio, pad_segment, window):
    key_clip = jnp.clip(key_pos, 0, total_audio - 1)
    key_seg = segment_of(key_clip, bounds)
    query_seg = segment_of(jnp.clip(query_pos // 2, 0, total_audio - 1), bounds)
    key_inside = (key_pos >= 0) & (key_pos < total_audio) & (keep_rows == 1) & (key_seg < pad_segment)
    query_inside = (query_pos >= 0) & (query_pos < 2 * total_audio) & (query_seg < pad_segment)
    nearby = jnp.abs(query_pos[:, None] - 2 * key_pos[None, :]) <= 2 * window
    return key_inside[None, :] & query_inside[:, None] & (key_seg[None, :] == query_seg[:, None]) & nearby


def as_float(array):
    return array.astype(jnp.float32)


def forward_block(queries, key_rows, value_rows, allowed, row_valid, null_kv):
    row_count = queries.shape[0]
    factor = HEAD ** -0.5
    query_heads = as_float(queries.reshape(row_count, HEADS, HEAD))
    key_heads = as_float(key_rows.reshape(key_rows.shape[0], HEADS, HEAD))
    value_heads = as_float(value_rows.reshape(value_rows.shape[0], HEADS, HEAD))
    null_key = as_float(null_kv[0].reshape(HEADS, HEAD))
    null_value = as_float(null_kv[1].reshape(HEADS, HEAD))
    scores = jnp.einsum("ihd,jhd->hij", query_heads, key_heads) * factor
    null_score = jnp.einsum("ihd,hd->hi", query_heads, null_key) * factor
    masked = jnp.where(allowed[None], scores, -jnp.inf)
    row_top = jnp.maximum(jnp.max(masked, axis=2), null_score)
    exponent = jnp.where(allowed[None], jnp.exp(scores - row_top[:, :, None]), 0.0)
    null_exponent = jnp.exp(null_score - row_top)
    row_total = jnp.sum(exponent, axis=2) + null_exponent
    weights = (exponent / row_total[:, :, None]).astype(jnp.bfloat16)
    null_prob = (null_exponent / row_total).astype(jnp.bfloat16)
    mixed = jnp.einsum("hij,jhd->ihd", as_float(weights), value_heads)
    mixed = mixed + as_float(null_prob).T[:, :, None] * null_value[None]
    attended = (mixed * row_valid[:, None, None]).reshape(row_count, HEADS * HEAD).astype(jnp.bfloat16)
    return attended, weights, null_prob


def backward_block(queries, grad_rows, key_rows, value_rows, weights, null_prob, null_kv):
    row_count = queries.shape[0]
    factor = HEAD ** -0.5
    query_heads = as_float(queries.reshape(row_count, HEADS, HEAD))
    grad_heads = as_float(grad_rows.reshape(row_count, HEADS, HEAD))
    key_heads = as_float(key_rows.reshape(key_rows.shape[0], HEADS, HEAD))
    value_heads = as_float(value_rows.reshape(value_rows.shape[0], HEADS, HEAD))
    null_key = as_float(null_kv[0].reshape(HEADS, HEAD))
    null_value = as_float(null_kv[1].reshape(HEADS, HEAD))
    prob_grad = jnp.einsum("ihd,jhd->hij", grad_heads, value_heads)
    null_prob_grad = jnp.einsum("ihd,hd->hi", grad_heads, null_value)
    weight_float = as_float(weights)
    null_float = as_float(null_prob)
    row_delta = jnp.sum(weight_float * prob_grad, axis=2) + null_float * null_prob_grad
    score_grad = (weight_float * (prob_grad - row_delta[:, :, None]) * factor).astype(jnp.bfloat16)
    null_score_grad = (null_float * (null_prob_grad - row_delta) * factor).astype(jnp.bfloat16)
    query_grad = jnp.einsum("hij,jhd->ihd", as_float(score_grad), key_heads)
    query_grad = query_grad + as_float(null_score_grad).T[:, :, None] * null_key[None]
    query_grad = query_grad.reshape(row_count, HEADS * HEAD).astype(jnp.bfloat16)
    key_grad = jnp.einsum("hij,ihd->jhd", as_float(score_grad), query_heads).reshape(-1, HEADS * HEAD)
    value_grad = jnp.einsum("hij,ihd->jhd", weight_float, grad_heads).reshape(-1, HEADS * HEAD)
    null_grad = jnp.stack([jnp.einsum("hi,ihd->hd", as_float(null_score_grad), query_heads),
                           jnp.einsum("hi,ihd->hd", null_float, grad_heads)]).reshape(2, HEADS * HEAD)
    return query_grad, key_grad, value_grad, null_grad


def reference(video_query, audio_key, audio_value, null_kv, audio_keep, clip_lengths, out_grad):
    groups = clip_lengths.shape[0]
    width = video_query.shape[1]
    group_queries = video_query.reshape(groups, VTOK, width)
    group_keys = audio_key.reshape(groups, ATOK, width)
    group_values = audio_value.reshape(groups, ATOK, width)
    group_keep = audio_keep.reshape(groups, ATOK)
    group_grads = out_grad.reshape(groups, VTOK, width)

    def one_group(packed):
        queries, key_rows, value_rows, keep, lengths, grads = packed
        bounds = jnp.cumsum(lengths)
        pad_segment = lengths.shape[0] - 1
        key_padded = jnp.pad(key_rows, ((AUD_DEV, AUD_DEV), (0, 0)))
        value_padded = jnp.pad(value_rows, ((AUD_DEV, AUD_DEV), (0, 0)))
        keep_padded = jnp.pad(keep, (AUD_DEV, AUD_DEV))

        def block_step(carry, block):
            key_acc, value_acc, null_acc = carry
            start = block * AUD_DEV
            query_pos = block * VID_DEV + jnp.arange(VID_DEV, dtype=jnp.int32)
            key_pos = start - AUD_DEV + jnp.arange(3 * AUD_DEV, dtype=jnp.int32)
            block_keys = lax.dynamic_slice_in_dim(key_padded, start, 3 * AUD_DEV)
            block_values = lax.dynamic_slice_in_dim(value_padded, start, 3 * AUD_DEV)
            keep_rows = lax.dynamic_slice_in_dim(keep_padded, start, 3 * AUD_DEV)
            block_queries = lax.dynamic_slice_in_dim(queries, block * VID_DEV, VID_DEV)
            block_grads = lax.dynamic_slice_in_dim(grads, block * VID_DEV, VID_DEV)
            allowed = allowed_pairs(query_pos, key_pos, bounds, keep_rows, ATOK, pad_segment, WINDOW)
            row_valid = (segment_of(query_pos // 2, bounds) < pad_segment).astype(jnp.float32)
            attended, weights, null_prob = forward_block(block_queries, block_keys, block_values, allowed, row_valid, null_kv)
            grad_rows = block_grads * row_valid[:, None].astype(jnp.bfloat16)
            query_grad, key_part, value_part, null_part = backward_block(
                block_queries, grad_rows, block_keys, block_values, weights, null_prob, null_kv)
            key_acc = lax.dynamic_update_slice_in_dim(
                key_acc, lax.dynamic_slice_in_dim(key_acc, start, 3 * AUD_DEV) + key_part, start, 0)
            value_acc = lax.dynamic_update_slice_in_dim(
                value_acc, lax.dynamic_slice_in_dim(value_acc, start, 3 * AUD_DEV) + value_part, start, 0)
            return (key_acc, value_acc, null_acc + null_part), (attended, query_grad)

        initial = (jnp.zeros((ATOK + 2 * AUD_DEV, width), jnp.float32),
                   jnp.zeros((ATOK + 2 * AUD_DEV, width), jnp.float32),
                   jnp.zeros((2, width), jnp.float32))
        (key_acc, value_acc, null_acc), (attended, query_grad) = lax.scan(
            block_step, initial, jnp.arange(N_SEQ, dtype=jnp.int32))
        return (attended.reshape(VTOK, width), query_grad.reshape(VTOK, width),
                key_acc[AUD_DEV:AUD_DEV + ATOK].astype(jnp.bfloat16),
                value_acc[AUD_DEV:AUD_DEV + ATOK].astype(jnp.bfloat16), null_acc)

    attended, query_grad, key_grad, value_grad, null_all = lax.map(
        one_group, (group_queries, group_keys, group_values, group_keep, clip_lengths, group_grads))
    return (attended.reshape(VIDEO, width), query_grad.reshape(VIDEO, width),
            key_grad.reshape(AUDIO, width), value_grad.reshape(AUDIO, width), jnp.sum(null_all, axis=0))
```

```python
import numpy as np

import jax
import jax.numpy as jnp
from jax import lax
from jax.experimental import pallas as pl
from jax.experimental.pallas import tpu as pltpu
from jax.sharding import Mesh
from jax.sharding import PartitionSpec as P

HEADS = 12
HEAD = 128
NULL_ROWS = 16
MASKED = -1e30
FACTOR = HEAD**-0.5
LOG2E = 1.4426950408889634
CLIP_PARTS = (("yh", 2), ("z", 8))
SEQ_PARTS = (("yl", 4), ("x", 4), ("core", 2))
CLIP = tuple(name for name, _ in CLIP_PARTS)
SEQ = tuple(name for name, _ in SEQ_PARTS)
VMEM_LIMIT = 60 * 1024 * 1024
PER_STEP = 2
STEPS = HEADS // PER_STEP
WIDE = PER_STEP * HEAD


def swap_chip(block):
    count = lax.axis_size(SEQ)
    return lax.ppermute(block, SEQ, [(i, i ^ 1) for i in range(count)])


def swap_link(block):
    last = lax.axis_size(SEQ) - 1
    pairs = [(i, i + 1) for i in range(1, last, 2)]
    return lax.ppermute(block, SEQ, pairs + [(b, a) for a, b in pairs])


def segment_of(positions, bounds):
    return jnp.sum((positions[:, None] >= bounds[None, :-1]).astype(jnp.int32), axis=1)


def allowed_pairs(query_pos, key_pos, bounds, keep_rows, total_audio, pad_segment, window):
    key_clip = jnp.clip(key_pos, 0, total_audio - 1)
    key_seg = segment_of(key_clip, bounds)
    query_seg = segment_of(query_pos // 2, bounds)
    key_inside = (
        (key_pos >= 0) & (key_pos < total_audio) & (keep_rows == 1) & (key_seg < pad_segment)
    )
    nearby = jnp.abs(query_pos[None, :] - 2 * key_pos[:, None]) <= 2 * window
    return key_inside[:, None] & (key_seg[:, None] == query_seg[None, :]) & nearby


def dot(a, b, lhs_dim, rhs_dim):
    return lax.dot_general(
        a, b, (((lhs_dim,), (rhs_dim,)), ((), ())), preferred_element_type=jnp.float32
    )


def stack_kernel(key_ref, value_ref, out_ref, sems):
    rows = key_ref.shape[0]
    copies = [
        pltpu.make_async_copy(ref, out_ref.at[pl.ds(i * rows, rows)], sems.at[i])
        for i, ref in enumerate((key_ref, value_ref))
    ]
    for copy in copies:
        copy.start()
    for copy in copies:
        copy.wait()


def stack_call(keys, values):
    rows, width = keys.shape
    return pl.pallas_call(
        stack_kernel,
        in_specs=[pl.BlockSpec(memory_space=pl.ANY)] * 2,
        out_specs=pl.BlockSpec(memory_space=pltpu.VMEM),
        out_shape=jax.ShapeDtypeStruct((2 * rows, width), keys.dtype),
        scratch_shapes=[pltpu.SemaphoreType.DMA((2,))],
        compiler_params=pltpu.CompilerParams(vmem_limit_bytes=VMEM_LIMIT),
        name="stack",
    )(keys, values)


def columns(step):
    return pl.ds(pl.multiple_of(step * WIDE, WIDE), WIDE)


def wide_copies(refs, held, sems, step):
    return [
        pltpu.make_async_copy(ref.at[:, columns(step)], held.at[step, i], sems.at[step, i])
        for i, ref in enumerate(refs)
    ]


def start(copies):
    for copy in copies:
        copy.start()


def wait(copies):
    for copy in copies:
        copy.wait()


def gathered(blocks, null_ref, cols, index):
    rows = blocks.shape[1] // 2
    return jnp.concatenate(
        [blocks[i, index * rows : (index + 1) * rows, cols] for i in range(3)] + [null_ref[index]],
        axis=0,
    )


def heads_kernel(
    q_hbm, g_hbm, far_hbm, own_hbm, near_hbm, null_hbm, bias_hbm, valid_hbm,
    out_hbm, dq_hbm, far_grad_hbm, own_grad_hbm, near_grad_hbm, null_grad_ref,
    held, null_ref, bias_ref, valid_ref, results, ends, middle, null_sum,
    in_sems, rest_sems, out_sems,
):
    refs = (q_hbm, g_hbm, far_hbm, own_hbm, near_hbm)
    rows = middle.shape[2]
    rest = [
        pltpu.make_async_copy(src, dst, rest_sems.at[i])
        for i, (src, dst) in enumerate(
            ((bias_hbm, bias_ref), (valid_hbm, valid_ref), (null_hbm, null_ref))
        )
    ]
    start(wide_copies(refs, held, in_sems, 0))
    start(rest)
    for step in range(1, STEPS):
        start(wide_copies(refs, held, in_sems, step))
    wait(rest)

    def out_copies(step):
        pairs = [
            (results.at[step, 0], out_hbm.at[:, columns(step)]),
            (results.at[step, 1], dq_hbm.at[:, columns(step)]),
            (ends.at[step, 0], far_grad_hbm.at[:, :, columns(step)]),
            (middle.at[step], own_grad_hbm.at[:, :, columns(step)]),
            (ends.at[step, 1], near_grad_hbm.at[:, :, columns(step)]),
        ]
        return [
            pltpu.make_async_copy(src, dst, out_sems.at[step, i])
            for i, (src, dst) in enumerate(pairs)
        ]

    def one_step(step, carry):
        wait(wide_copies(refs, held, in_sems, step))
        for part in range(PER_STEP):
            head = step * PER_STEP + part
            cols = slice(part * HEAD, (part + 1) * HEAD)
            q = held[step, 0, :, cols]
            g = held[step, 1, :, cols]
            keys = gathered(held.at[step, 2:], null_ref.at[head], cols, 0)
            values = gathered(held.at[step, 2:], null_ref.at[head], cols, 1)
            scores = dot(keys, q, 1, 1) + bias_ref[...]
            top = jnp.max(scores, axis=0, keepdims=True)
            exponent = jnp.exp2((scores - top) * (FACTOR * LOG2E))
            total = jnp.sum(exponent, axis=0, keepdims=True)
            exponent = exponent.astype(jnp.bfloat16)
            share = valid_ref[...] / total
            g_flip = g.T.astype(jnp.float32)
            out_flip = dot(values, exponent, 0, 0) * share
            delta = jnp.sum(out_flip * g_flip, axis=0, keepdims=True)
            results[step, 0, :, cols] = out_flip.astype(jnp.bfloat16).T
            prob_grad = dot(values, g, 1, 1)
            score_grad = ((prob_grad - delta) * (share * FACTOR)).astype(jnp.bfloat16) * exponent
            results[step, 1, :, cols] = dot(keys, score_grad, 0, 0).astype(jnp.bfloat16).T
            key_term = dot(score_grad, q, 1, 0)
            value_term = dot(exponent, (g_flip * share).astype(jnp.bfloat16), 1, 1)
            for index, term in enumerate((key_term, value_term)):
                ends[step, 0, index, :, cols] = term[:rows].astype(jnp.bfloat16)
                middle[step, index, :, cols] = term[rows : 2 * rows]
                ends[step, 1, index, :, cols] = term[2 * rows : 3 * rows].astype(jnp.bfloat16)
                null_sum[pl.ds(index * HEADS + head, 1), :] = term[3 * rows : 3 * rows + 1]
        start(out_copies(step))
        return carry

    lax.fori_loop(0, STEPS, one_step, 0)
    null_grad_ref[...] = jnp.broadcast_to(
        null_sum[...].astype(jnp.bfloat16)[None], null_grad_ref.shape
    )
    for step in range(STEPS):
        wait(out_copies(step))


def heads_call(q, g, far, own, near, null_rows, bias, valid, peers):
    video_rows, width = q.shape
    audio_rows = video_rows // 2
    args = (q, g, far, own, near, null_rows, bias, valid)
    anywhere = pl.BlockSpec(memory_space=pl.ANY)
    wide = jax.ShapeDtypeStruct((video_rows, width), jnp.bfloat16)
    terms = [
        jax.ShapeDtypeStruct((2, audio_rows, width), dtype)
        for dtype in (jnp.bfloat16, jnp.float32, jnp.bfloat16)
    ]
    return pl.pallas_call(
        heads_kernel,
        in_specs=[anywhere] * len(args),
        out_specs=[anywhere] * 5 + [pl.BlockSpec(memory_space=pltpu.VMEM)],
        out_shape=[wide, wide, *terms, jax.ShapeDtypeStruct((peers, 2 * HEADS, HEAD), jnp.bfloat16)],
        scratch_shapes=[
            pltpu.VMEM((STEPS, 5, video_rows, WIDE), jnp.bfloat16),
            pltpu.VMEM(null_rows.shape, jnp.bfloat16),
            pltpu.VMEM(bias.shape, jnp.float32),
            pltpu.VMEM(valid.shape, jnp.float32),
            pltpu.VMEM((STEPS, 2, video_rows, WIDE), jnp.bfloat16),
            pltpu.VMEM((STEPS, 2, 2, audio_rows, WIDE), jnp.bfloat16),
            pltpu.VMEM((STEPS, 2, audio_rows, WIDE), jnp.float32),
            pltpu.VMEM((2 * HEADS, HEAD), jnp.float32),
            pltpu.SemaphoreType.DMA((STEPS, 5)),
            pltpu.SemaphoreType.DMA((3,)),
            pltpu.SemaphoreType.DMA((STEPS, 5)),
        ],
        compiler_params=pltpu.CompilerParams(vmem_limit_bytes=VMEM_LIMIT),
        cost_estimate=pl.CostEstimate(
            flops=12 * bias.size * width, bytes_accessed=9_000_000, transcendentals=bias.size * HEADS
        ),
        name="heads",
    )(*args)


def sum_peers(parts):
    return jnp.sum(parts.astype(jnp.float32), axis=0)


def body(video_query, audio_key, audio_value, null_kv, audio_keep, clip_lengths, out_grad):
    audio_rows = audio_key.shape[0]
    video_rows = video_query.shape[0]
    shards = lax.axis_size(SEQ)
    seq_index = lax.axis_index(SEQ)
    total_audio = audio_rows * shards

    stacked = stack_call(audio_key, audio_value)
    far = swap_link(stacked)

    bounds = jnp.cumsum(clip_lengths[0])
    pad_segment = clip_lengths.shape[1] - 1
    query_pos = seq_index * video_rows + jnp.arange(video_rows, dtype=jnp.int32)
    side = 1 - 2 * (seq_index % 2)
    starts = [(seq_index + move) * audio_rows for move in (-side, 0, side)]
    own_pos = jnp.arange(audio_rows, dtype=jnp.int32)
    key_pos = jnp.concatenate([start + own_pos for start in starts])
    keep_padded = jnp.pad(audio_keep, (audio_rows, audio_rows))
    keep_rows = jnp.concatenate(
        [lax.dynamic_slice_in_dim(keep_padded, start + audio_rows, audio_rows) for start in starts]
    )
    allowed = allowed_pairs(
        query_pos, key_pos, bounds, keep_rows, total_audio, pad_segment, audio_rows
    )
    null_allowed = jnp.arange(NULL_ROWS) == 0
    bias = jnp.where(
        jnp.concatenate([allowed, jnp.broadcast_to(null_allowed[:, None], (NULL_ROWS, video_rows))]),
        0.0,
        MASKED,
    ).astype(jnp.float32)
    valid = (segment_of(query_pos // 2, bounds) < pad_segment).astype(jnp.float32)[None]
    null_heads = null_kv.reshape(2, HEADS, 1, HEAD).swapaxes(0, 1)
    null_rows = jnp.pad(null_heads, ((0, 0), (0, 0), (0, NULL_ROWS - 1), (0, 0)))

    stacked, valid = lax.optimization_barrier((stacked, valid))
    near = swap_chip(stacked)

    wide_axes, deep_axes = ("yh", "yl", "x"), ("z", "core")
    attended, query_grad, far_grad, own_grad, near_grad, null_copies = heads_call(
        video_query, out_grad, far, stacked, near, null_rows, bias, valid, lax.axis_size(wide_axes)
    )
    far_back = swap_link(far_grad)
    first = lax.all_to_all(null_copies, wide_axes, 0, 0)
    first, near_grad = lax.optimization_barrier((first, near_grad))
    partial = sum_peers(first).astype(jnp.bfloat16)
    copies = jnp.broadcast_to(partial[None], (lax.axis_size(deep_axes), *partial.shape))
    second = lax.all_to_all(copies, deep_axes, 0, 0)
    near_back = swap_chip(near_grad)
    grads = [
        (own_grad[i] + far_back[i].astype(jnp.float32) + near_back[i].astype(jnp.float32)).astype(
            jnp.bfloat16
        )
        for i in range(2)
    ]
    second, *grads = lax.optimization_barrier((second, *grads))
    null_grad = sum_peers(second).reshape(null_kv.shape)
    return (attended, query_grad, grads[0], grads[1], null_grad)


def solution(mesh):
    parts = CLIP_PARTS + SEQ_PARTS
    fine = Mesh(
        np.asarray(mesh.devices).reshape([size for _, size in parts]), [name for name, _ in parts]
    )
    rows = P(CLIP + SEQ, None)
    return jax.shard_map(
        body,
        mesh=fine,
        in_specs=(rows, rows, rows, P(), P(CLIP), P(CLIP, None), rows),
        out_specs=(rows, rows, rows, rows, P()),
        check_vma=False,
    )
```

```python
import numpy as np

import jax
import jax.numpy as jnp
from jax import lax
from jax.experimental import pallas as pl
from jax.experimental.pallas import tpu as pltpu
from jax.sharding import Mesh
from jax.sharding import PartitionSpec as P

HEADS = 12
HEAD = 128
NULL_ROWS = 16
MASKED = -1e30
FACTOR = HEAD**-0.5
LOG2E = 1.4426950408889634
CLIP_PARTS = (("yh", 2), ("z", 8))
SEQ_PARTS = (("yl", 4), ("x", 4), ("core", 2))
CLIP = tuple(name for name, _ in CLIP_PARTS)
SEQ = tuple(name for name, _ in SEQ_PARTS)
VMEM_LIMIT = 60 * 1024 * 1024
PER_STEP = 4
STEPS = HEADS // PER_STEP
WIDE = PER_STEP * HEAD


def swap_chip(block):
    count = lax.axis_size(SEQ)
    return lax.ppermute(block, SEQ, [(i, i ^ 1) for i in range(count)])


def swap_link(block):
    last = lax.axis_size(SEQ) - 1
    pairs = [(i, i + 1) for i in range(1, last, 2)]
    return lax.ppermute(block, SEQ, pairs + [(b, a) for a, b in pairs])


def segment_of(positions, bounds):
    return jnp.sum((positions[:, None] >= bounds[None, :-1]).astype(jnp.int32), axis=1)


def allowed_pairs(query_pos, key_pos, bounds, keep_rows, total_audio, pad_segment, window):
    key_clip = jnp.clip(key_pos, 0, total_audio - 1)
    key_seg = segment_of(key_clip, bounds)
    query_seg = segment_of(query_pos // 2, bounds)
    key_inside = (
        (key_pos >= 0) & (key_pos < total_audio) & (keep_rows == 1) & (key_seg < pad_segment)
    )
    nearby = jnp.abs(query_pos[None, :] - 2 * key_pos[:, None]) <= 2 * window
    return key_inside[:, None] & (key_seg[:, None] == query_seg[None, :]) & nearby


def dot(a, b, lhs_dim, rhs_dim):
    return lax.dot_general(
        a, b, (((lhs_dim,), (rhs_dim,)), ((), ())), preferred_element_type=jnp.float32
    )


def start(copies):
    for copy in copies:
        copy.start()


def wait(copies):
    for copy in copies:
        copy.wait()


def stack_kernel(key_ref, value_ref, out_ref, held, in_sems, out_sems):
    rows = held.shape[1]
    pieces = [pl.ds(i * rows, rows) for i in range(key_ref.shape[0] // rows)]
    sources = [ref.at[piece] for ref in (key_ref, value_ref) for piece in pieces]
    arrive = [
        pltpu.make_async_copy(src, held.at[i], in_sems.at[i]) for i, src in enumerate(sources)
    ]
    leave = [
        pltpu.make_async_copy(held.at[i], out_ref.at[pl.ds(i * rows, rows)], out_sems.at[i])
        for i in range(len(sources))
    ]
    start(arrive)
    for first, second in zip(arrive, leave):
        first.wait()
        second.start()
    wait(leave)


def stack_call(keys, values):
    rows, width = keys.shape
    return pl.pallas_call(
        stack_kernel,
        in_specs=[pl.BlockSpec(memory_space=pl.ANY)] * 2,
        out_specs=pl.BlockSpec(memory_space=pl.ANY),
        out_shape=jax.ShapeDtypeStruct((2 * rows, width), keys.dtype),
        scratch_shapes=[
            pltpu.VMEM((4, rows // 2, width), keys.dtype),
            pltpu.SemaphoreType.DMA((4,)),
            pltpu.SemaphoreType.DMA((4,)),
        ],
        compiler_params=pltpu.CompilerParams(vmem_limit_bytes=VMEM_LIMIT),
        name="stack",
    )(keys, values)


def gathered(refs, null_ref, cols, index):
    rows = refs[0].shape[0] // 2
    return jnp.concatenate(
        [ref[index * rows : (index + 1) * rows, cols] for ref in refs] + [null_ref[index]], axis=0
    )


def heads_kernel(
    q_ref, g_ref, far_ref, own_ref, near_ref, null_ref, bias_ref, valid_ref,
    out_ref, dq_ref, far_grad_ref, own_grad_ref, near_grad_ref, null_grad_ref, null_sum,
):
    step = pl.program_id(0)
    rows = own_ref.shape[0] // 2
    refs = (far_ref, own_ref, near_ref)
    parts = range(PER_STEP)
    cols = [slice(i * HEAD, (i + 1) * HEAD) for i in parts]
    keys = [gathered(refs, null_ref.at[i], cols[i], 0) for i in parts]
    values = [gathered(refs, null_ref.at[i], cols[i], 1) for i in parts]
    scores = [dot(keys[i], q_ref[:, cols[i]], 1, 1) + bias_ref[...] for i in parts]
    tops = [jnp.max(x, axis=0, keepdims=True) for x in scores]
    exact = [jnp.exp2((x - top) * (FACTOR * LOG2E)) for x, top in zip(scores, tops)]
    shares = [valid_ref[...] / jnp.sum(x, axis=0, keepdims=True) for x in exact]
    exponents = [x.astype(jnp.bfloat16) for x in exact]
    flips = [g_ref[:, cols[i]].T.astype(jnp.float32) for i in parts]
    mixed = [dot(values[i], exponents[i], 0, 0) * shares[i] for i in parts]
    deltas = [jnp.sum(x * flip, axis=0, keepdims=True) for x, flip in zip(mixed, flips)]
    prob_grads = [dot(values[i], g_ref[:, cols[i]], 1, 1) for i in parts]
    score_grads = [
        ((x - delta) * (share * FACTOR)).astype(jnp.bfloat16) * exponent
        for x, delta, share, exponent in zip(prob_grads, deltas, shares, exponents)
    ]
    for i in parts:
        out_ref[:, cols[i]] = mixed[i].astype(jnp.bfloat16).T
        dq_ref[:, cols[i]] = dot(keys[i], score_grads[i], 0, 0).astype(jnp.bfloat16).T
        terms = (
            dot(score_grads[i], q_ref[:, cols[i]], 1, 0),
            dot(exponents[i], (flips[i] * shares[i]).astype(jnp.bfloat16), 1, 1),
        )
        for index, term in enumerate(terms):
            far_grad_ref[index, :, cols[i]] = term[:rows].astype(jnp.bfloat16)
            own_grad_ref[index, :, cols[i]] = term[rows : 2 * rows]
            near_grad_ref[index, :, cols[i]] = term[2 * rows : 3 * rows].astype(jnp.bfloat16)
            null_sum[pl.ds(index * HEADS + step * PER_STEP + i, 1), :] = term[3 * rows : 3 * rows + 1]

    @pl.when(step == STEPS - 1)
    def _():
        null_grad_ref[...] = jnp.broadcast_to(
            null_sum[...].astype(jnp.bfloat16)[None], null_grad_ref.shape
        )


def block(*lead):
    return pl.BlockSpec((*lead, WIDE), lambda i: (0,) * len(lead) + (i,))


def whole(shape):
    return pl.BlockSpec(shape, lambda i: (0,) * len(shape))


def heads_call(q, g, far, own, near, null_rows, bias, valid, peers):
    video_rows, width = q.shape
    audio_rows = video_rows // 2
    wide = jax.ShapeDtypeStruct((video_rows, width), jnp.bfloat16)
    terms = [
        jax.ShapeDtypeStruct((2, audio_rows, width), dtype)
        for dtype in (jnp.bfloat16, jnp.float32, jnp.bfloat16)
    ]
    null_shape = (peers, 2 * HEADS, HEAD)
    return pl.pallas_call(
        heads_kernel,
        grid=(STEPS,),
        in_specs=[block(video_rows)] * 5
        + [
            pl.BlockSpec((PER_STEP, *null_rows.shape[1:]), lambda i: (i, 0, 0, 0)),
            whole(bias.shape),
            whole(valid.shape),
        ],
        out_specs=[block(video_rows)] * 2 + [block(2, audio_rows)] * 3 + [whole(null_shape)],
        out_shape=[wide, wide, *terms, jax.ShapeDtypeStruct(null_shape, jnp.bfloat16)],
        scratch_shapes=[pltpu.VMEM((2 * HEADS, HEAD), jnp.float32)],
        compiler_params=pltpu.CompilerParams(vmem_limit_bytes=VMEM_LIMIT),
        cost_estimate=pl.CostEstimate(
            flops=12 * bias.size * width, bytes_accessed=9_000_000, transcendentals=bias.size * HEADS
        ),
        name="heads",
    )(q, g, far, own, near, null_rows, bias, valid)


def sum_peers(parts):
    return jnp.sum(parts.astype(jnp.float32), axis=0)


def body(video_query, audio_key, audio_value, null_kv, audio_keep, clip_lengths, out_grad):
    audio_rows = audio_key.shape[0]
    video_rows = video_query.shape[0]
    shards = lax.axis_size(SEQ)
    seq_index = lax.axis_index(SEQ)
    total_audio = audio_rows * shards

    stacked = stack_call(audio_key, audio_value)
    far = swap_link(stacked)

    bounds = jnp.cumsum(clip_lengths[0])
    pad_segment = clip_lengths.shape[1] - 1
    query_pos = seq_index * video_rows + jnp.arange(video_rows, dtype=jnp.int32)
    side = 1 - 2 * (seq_index % 2)
    starts = [(seq_index + move) * audio_rows for move in (-side, 0, side)]
    own_pos = jnp.arange(audio_rows, dtype=jnp.int32)
    key_pos = jnp.concatenate([start + own_pos for start in starts])
    keep_padded = jnp.pad(audio_keep, (audio_rows, audio_rows))
    keep_rows = jnp.concatenate(
        [lax.dynamic_slice_in_dim(keep_padded, start + audio_rows, audio_rows) for start in starts]
    )
    allowed = allowed_pairs(
        query_pos, key_pos, bounds, keep_rows, total_audio, pad_segment, audio_rows
    )
    null_allowed = jnp.arange(NULL_ROWS) == 0
    bias = jnp.where(
        jnp.concatenate([allowed, jnp.broadcast_to(null_allowed[:, None], (NULL_ROWS, video_rows))]),
        0.0,
        MASKED,
    ).astype(jnp.float32)
    valid = (segment_of(query_pos // 2, bounds) < pad_segment).astype(jnp.float32)[None]
    null_heads = null_kv.reshape(2, HEADS, 1, HEAD).swapaxes(0, 1)
    null_rows = jnp.pad(null_heads, ((0, 0), (0, 0), (0, NULL_ROWS - 1), (0, 0)))

    stacked, valid = lax.optimization_barrier((stacked, valid))
    near = swap_chip(stacked)

    wide_axes, deep_axes = ("yh", "yl", "x"), ("z", "core")
    attended, query_grad, far_grad, own_grad, near_grad, null_copies = heads_call(
        video_query, out_grad, far, stacked, near, null_rows, bias, valid, lax.axis_size(wide_axes)
    )
    far_back = swap_link(far_grad)
    first = lax.all_to_all(null_copies, wide_axes, 0, 0)
    partial = sum_peers(first).astype(jnp.bfloat16)
    copies = jnp.broadcast_to(partial[None], (lax.axis_size(deep_axes), *partial.shape))
    copies, near_grad = lax.optimization_barrier((copies, near_grad))
    second = lax.all_to_all(copies, deep_axes, 0, 0)
    near_back = swap_chip(near_grad)
    grads = [
        (own_grad[i] + far_back[i].astype(jnp.float32) + near_back[i].astype(jnp.float32)).astype(
            jnp.bfloat16
        )
        for i in range(2)
    ]
    second, *grads = lax.optimization_barrier((second, *grads))
    null_grad = sum_peers(second).reshape(null_kv.shape)
    return (attended, query_grad, grads[0], grads[1], null_grad)


def solution(mesh):
    parts = CLIP_PARTS + SEQ_PARTS
    fine = Mesh(
        np.asarray(mesh.devices).reshape([size for _, size in parts]), [name for name, _ in parts]
    )
    rows = P(CLIP + SEQ, None)
    return jax.shard_map(
        body,
        mesh=fine,
        in_specs=(rows, rows, rows, P(), P(CLIP), P(CLIP, None), rows),
        out_specs=(rows, rows, rows, rows, P()),
        check_vma=False,
    )
```

```python
import numpy as np

import jax
import jax.numpy as jnp
from jax import lax
from jax.experimental import pallas as pl
from jax.experimental.pallas import tpu as pltpu
from jax.sharding import Mesh
from jax.sharding import PartitionSpec as P

HEADS = 12
HEAD = 128
NULL_ROWS = 16
MASKED = -1e30
FACTOR = HEAD**-0.5
LOG2E = 1.4426950408889634
CLIP_PARTS = (("yh", 2), ("z", 8))
SEQ_PARTS = (("yl", 4), ("x", 4), ("core", 2))
CLIP = tuple(name for name, _ in CLIP_PARTS)
SEQ = tuple(name for name, _ in SEQ_PARTS)
VMEM_LIMIT = 60 * 1024 * 1024
HEADS_LIMIT = 56 * 1024 * 1024
ADD_LIMIT = 8 * 1024 * 1024
PER_STEP = 4
STEPS = HEADS // PER_STEP
WIDE = PER_STEP * HEAD


def swap_chip(block):
    count = lax.axis_size(SEQ)
    return lax.ppermute(block, SEQ, [(i, i ^ 1) for i in range(count)])


def swap_link(block):
    last = lax.axis_size(SEQ) - 1
    pairs = [(i, i + 1) for i in range(1, last, 2)]
    return lax.ppermute(block, SEQ, pairs + [(b, a) for a, b in pairs])


def segment_of(positions, bounds):
    return jnp.sum((positions[:, None] >= bounds[None, :-1]).astype(jnp.int32), axis=1)


def allowed_pairs(query_pos, key_pos, bounds, keep_rows, total_audio, pad_segment, window):
    key_clip = jnp.clip(key_pos, 0, total_audio - 1)
    key_seg = segment_of(key_clip, bounds)
    query_seg = segment_of(query_pos // 2, bounds)
    key_inside = (
        (key_pos >= 0) & (key_pos < total_audio) & (keep_rows == 1) & (key_seg < pad_segment)
    )
    nearby = jnp.abs(query_pos[None, :] - 2 * key_pos[:, None]) <= 2 * window
    return key_inside[:, None] & (key_seg[:, None] == query_seg[None, :]) & nearby


def dot(a, b, lhs_dim, rhs_dim):
    return lax.dot_general(
        a, b, (((lhs_dim,), (rhs_dim,)), ((), ())), preferred_element_type=jnp.float32
    )


def start(copies):
    for copy in copies:
        copy.start()


def wait(copies):
    for copy in copies:
        copy.wait()


def stack_kernel(key_ref, value_ref, out_ref, held, in_sems, out_sems):
    rows = held.shape[1]
    pieces = [pl.ds(i * rows, rows) for i in range(key_ref.shape[0] // rows)]
    sources = [ref.at[piece] for ref in (key_ref, value_ref) for piece in pieces]
    arrive = [
        pltpu.make_async_copy(src, held.at[i], in_sems.at[i]) for i, src in enumerate(sources)
    ]
    leave = [
        pltpu.make_async_copy(held.at[i], out_ref.at[pl.ds(i * rows, rows)], out_sems.at[i])
        for i in range(len(sources))
    ]
    start(arrive)
    for first, second in zip(arrive, leave):
        first.wait()
        second.start()
    wait(leave)


def stack_call(keys, values):
    rows, width = keys.shape
    return pl.pallas_call(
        stack_kernel,
        in_specs=[pl.BlockSpec(memory_space=pl.ANY)] * 2,
        out_specs=pl.BlockSpec(memory_space=pl.ANY),
        out_shape=jax.ShapeDtypeStruct((2 * rows, width), keys.dtype),
        scratch_shapes=[
            pltpu.VMEM((4, rows // 2, width), keys.dtype),
            pltpu.SemaphoreType.DMA((4,)),
            pltpu.SemaphoreType.DMA((4,)),
        ],
        compiler_params=pltpu.CompilerParams(vmem_limit_bytes=VMEM_LIMIT),
        name="stack",
    )(keys, values)


def prepare_kernel(q_hbm, g_hbm, own_hbm, q_ref, g_ref, own_ref, sems):
    pairs = ((q_hbm, q_ref), (g_hbm, g_ref), (own_hbm, own_ref))
    copies = [pltpu.make_async_copy(a, b, sems.at[i]) for i, (a, b) in enumerate(pairs)]
    start(copies)
    wait(copies)


def prepare_call(q, g, own):
    arrays = (q, g, own)
    return pl.pallas_call(
        prepare_kernel,
        in_specs=[pl.BlockSpec(memory_space=pl.ANY)] * 3,
        out_specs=[pl.BlockSpec(memory_space=pltpu.VMEM)] * 3,
        out_shape=[jax.ShapeDtypeStruct(x.shape, x.dtype) for x in arrays],
        scratch_shapes=[pltpu.SemaphoreType.DMA((3,))],
        compiler_params=pltpu.CompilerParams(vmem_limit_bytes=HEADS_LIMIT),
        name="prepare",
    )(*arrays)


def gathered(refs, null_ref, cols, index):
    rows = refs[0].shape[0] // 2
    return jnp.concatenate(
        [ref[index * rows : (index + 1) * rows, cols] for ref in refs] + [null_ref[index]], axis=0
    )


def heads_kernel(
    q_ref, g_ref, far_ref, own_ref, near_ref, null_ref, bias_ref, valid_ref,
    out_ref, dq_ref, far_grad_ref, own_grad_ref, near_grad_ref, null_grad_ref, null_sum,
):
    step = pl.program_id(0)
    rows = own_ref.shape[0] // 2
    refs = (far_ref, own_ref, near_ref)
    parts = range(PER_STEP)
    cols = [slice(i * HEAD, (i + 1) * HEAD) for i in parts]
    keys = [gathered(refs, null_ref.at[i], cols[i], 0) for i in parts]
    values = [gathered(refs, null_ref.at[i], cols[i], 1) for i in parts]
    scores = [dot(keys[i], q_ref[:, cols[i]], 1, 1) + bias_ref[...] for i in parts]
    tops = [jnp.max(x, axis=0, keepdims=True) for x in scores]
    exact = [jnp.exp2((x - top) * (FACTOR * LOG2E)) for x, top in zip(scores, tops)]
    shares = [valid_ref[...] / jnp.sum(x, axis=0, keepdims=True) for x in exact]
    exponents = [x.astype(jnp.bfloat16) for x in exact]
    flips = [g_ref[:, cols[i]].T.astype(jnp.float32) for i in parts]
    mixed = [dot(values[i], exponents[i], 0, 0) * shares[i] for i in parts]
    deltas = [jnp.sum(x * flip, axis=0, keepdims=True) for x, flip in zip(mixed, flips)]
    prob_grads = [dot(values[i], g_ref[:, cols[i]], 1, 1) for i in parts]
    score_grads = [
        ((x - delta) * (share * FACTOR)).astype(jnp.bfloat16) * exponent
        for x, delta, share, exponent in zip(prob_grads, deltas, shares, exponents)
    ]
    for i in parts:
        out_ref[:, cols[i]] = mixed[i].astype(jnp.bfloat16).T
        dq_ref[:, cols[i]] = dot(keys[i], score_grads[i], 0, 0).astype(jnp.bfloat16).T
        terms = (
            dot(score_grads[i], q_ref[:, cols[i]], 1, 0),
            dot(exponents[i], (flips[i] * shares[i]).astype(jnp.bfloat16), 1, 1),
        )
        for index, term in enumerate(terms):
            far_grad_ref[index, :, cols[i]] = term[:rows].astype(jnp.bfloat16)
            own_grad_ref[index, :, cols[i]] = term[rows : 2 * rows].astype(jnp.bfloat16)
            near_grad_ref[index, :, cols[i]] = term[2 * rows : 3 * rows].astype(jnp.bfloat16)
            null_sum[pl.ds(index * HEADS + step * PER_STEP + i, 1), :] = term[3 * rows : 3 * rows + 1]

    @pl.when(step == STEPS - 1)
    def _():
        null_grad_ref[...] = jnp.broadcast_to(
            null_sum[...].astype(jnp.bfloat16)[None], null_grad_ref.shape
        )


def block(*lead):
    return pl.BlockSpec((*lead, WIDE), lambda i: (0,) * len(lead) + (i,))


def whole(shape):
    return pl.BlockSpec(shape, lambda i: (0,) * len(shape))


def heads_call(q, g, far, own, near, null_rows, bias, valid, peers):
    video_rows, width = q.shape
    audio_rows = video_rows // 2
    wide = jax.ShapeDtypeStruct((video_rows, width), jnp.bfloat16)
    terms = [jax.ShapeDtypeStruct((2, audio_rows, width), jnp.bfloat16)] * 3
    null_shape = (peers, 2 * HEADS, HEAD)
    return pl.pallas_call(
        heads_kernel,
        grid=(STEPS,),
        in_specs=[block(video_rows)] * 5
        + [
            pl.BlockSpec((PER_STEP, *null_rows.shape[1:]), lambda i: (i, 0, 0, 0)),
            whole(bias.shape),
            whole(valid.shape),
        ],
        out_specs=[block(video_rows)] * 2 + [block(2, audio_rows)] * 3 + [whole(null_shape)],
        out_shape=[wide, wide, *terms, jax.ShapeDtypeStruct(null_shape, jnp.bfloat16)],
        scratch_shapes=[pltpu.VMEM((2 * HEADS, HEAD), jnp.float32)],
        compiler_params=pltpu.CompilerParams(vmem_limit_bytes=HEADS_LIMIT),
        cost_estimate=pl.CostEstimate(
            flops=12 * bias.size * width, bytes_accessed=9_000_000, transcendentals=bias.size * HEADS
        ),
        name="heads",
    )(q, g, far, own, near, null_rows, bias, valid)


def add_kernel(a_ref, b_ref, *out_refs):
    total = a_ref[...].astype(jnp.float32) + b_ref[...].astype(jnp.float32)
    if len(out_refs) == 1:
        out_refs[0][...] = total.astype(jnp.bfloat16)
    else:
        for i, ref in enumerate(out_refs):
            ref[...] = total[i].astype(jnp.bfloat16)


def add_call(a, b, split, work, name):
    _, rows, width = a.shape
    steps = 3
    both = pl.BlockSpec((2, rows, width // steps), lambda i: (0, 0, i))
    one = pl.BlockSpec((rows, width // steps), lambda i: (0, i))
    single = jax.ShapeDtypeStruct((rows, width), jnp.bfloat16)
    return pl.pallas_call(
        add_kernel,
        grid=(steps,),
        in_specs=[both, both],
        out_specs=[one, one] if split else both,
        out_shape=[single, single] if split else jax.ShapeDtypeStruct(a.shape, jnp.bfloat16),
        compiler_params=pltpu.CompilerParams(vmem_limit_bytes=ADD_LIMIT),
        cost_estimate=pl.CostEstimate(flops=a.size, bytes_accessed=work, transcendentals=0),
        name=name,
    )(a, b)


def sum_peers(parts):
    return jnp.sum(parts.astype(jnp.float32), axis=0)


def body(video_query, audio_key, audio_value, null_kv, audio_keep, clip_lengths, out_grad):
    audio_rows = audio_key.shape[0]
    video_rows = video_query.shape[0]
    shards = lax.axis_size(SEQ)
    seq_index = lax.axis_index(SEQ)
    total_audio = audio_rows * shards

    stacked = stack_call(audio_key, audio_value)
    far = swap_link(stacked)

    bounds = jnp.cumsum(clip_lengths[0])
    pad_segment = clip_lengths.shape[1] - 1
    query_pos = seq_index * video_rows + jnp.arange(video_rows, dtype=jnp.int32)
    side = 1 - 2 * (seq_index % 2)
    starts = [(seq_index + move) * audio_rows for move in (-side, 0, side)]
    own_pos = jnp.arange(audio_rows, dtype=jnp.int32)
    key_pos = jnp.concatenate([start + own_pos for start in starts])
    keep_padded = jnp.pad(audio_keep, (audio_rows, audio_rows))
    keep_rows = jnp.concatenate(
        [lax.dynamic_slice_in_dim(keep_padded, start + audio_rows, audio_rows) for start in starts]
    )
    allowed = allowed_pairs(
        query_pos, key_pos, bounds, keep_rows, total_audio, pad_segment, audio_rows
    )
    null_allowed = jnp.arange(NULL_ROWS) == 0
    bias = jnp.where(
        jnp.concatenate([allowed, jnp.broadcast_to(null_allowed[:, None], (NULL_ROWS, video_rows))]),
        0.0,
        MASKED,
    ).astype(jnp.float32)
    valid = (segment_of(query_pos // 2, bounds) < pad_segment).astype(jnp.float32)[None]
    null_heads = null_kv.reshape(2, HEADS, 1, HEAD).swapaxes(0, 1)
    null_rows = jnp.pad(null_heads, ((0, 0), (0, 0), (0, NULL_ROWS - 1), (0, 0)))

    stacked, valid = lax.optimization_barrier((stacked, valid))
    near = swap_chip(stacked)

    wide_axes, deep_axes = ("yh", "yl", "x"), ("z", "core")
    q_held, g_held, own = prepare_call(video_query, out_grad, stacked)
    attended, query_grad, far_grad, own_grad, near_grad, null_copies = heads_call(
        q_held, g_held, far, own, near, null_rows, bias, valid, lax.axis_size(wide_axes)
    )
    far_back = swap_link(far_grad)
    first = lax.all_to_all(null_copies, wide_axes, 0, 0)
    partial = sum_peers(first).astype(jnp.bfloat16)
    copies = jnp.broadcast_to(partial[None], (lax.axis_size(deep_axes), *partial.shape))
    copies, near_grad = lax.optimization_barrier((copies, near_grad))
    second = lax.all_to_all(copies, deep_axes, 0, 0)
    near_back = swap_chip(near_grad)
    part = add_call(own_grad, far_back, False, 40_000_000, "add_far")
    grads = add_call(part, near_back, True, 2_400_000, "add_near")
    second, *grads = lax.optimization_barrier((second, *grads))
    null_grad = sum_peers(second).reshape(null_kv.shape)
    return (attended, query_grad, grads[0], grads[1], null_grad)


def solution(mesh):
    parts = CLIP_PARTS + SEQ_PARTS
    fine = Mesh(
        np.asarray(mesh.devices).reshape([size for _, size in parts]), [name for name, _ in parts]
    )
    rows = P(CLIP + SEQ, None)
    return jax.shard_map(
        body,
        mesh=fine,
        in_specs=(rows, rows, rows, P(), P(CLIP), P(CLIP, None), rows),
        out_specs=(rows, rows, rows, rows, P()),
        check_vma=False,
    )
```

```python
import numpy as np

import jax
import jax.numpy as jnp
from jax import lax
from jax.experimental import pallas as pl
from jax.experimental.pallas import tpu as pltpu
from jax.sharding import Mesh
from jax.sharding import PartitionSpec as P

HEADS = 12
HEAD = 128
NULL_ROWS = 16
MASKED = -1e30
FACTOR = HEAD**-0.5
LOG2E = 1.4426950408889634
CLIP_PARTS = (("yh", 2), ("z", 8))
SEQ_PARTS = (("yl", 4), ("x", 4), ("core", 2))
CLIP = tuple(name for name, _ in CLIP_PARTS)
SEQ = tuple(name for name, _ in SEQ_PARTS)
VMEM_LIMIT = 60 * 1024 * 1024
HEADS_LIMIT = 48 * 1024 * 1024
ADD_LIMIT = 8 * 1024 * 1024
PER_STEP = 6
STEPS = HEADS // PER_STEP
WIDE = PER_STEP * HEAD


def swap_chip(block):
    count = lax.axis_size(SEQ)
    return lax.ppermute(block, SEQ, [(i, i ^ 1) for i in range(count)])


def swap_link(block):
    last = lax.axis_size(SEQ) - 1
    pairs = [(i, i + 1) for i in range(1, last, 2)]
    return lax.ppermute(block, SEQ, pairs + [(b, a) for a, b in pairs])


def segment_of(positions, bounds):
    return jnp.sum((positions[:, None] >= bounds[None, :-1]).astype(jnp.int32), axis=1)


def allowed_pairs(query_pos, key_pos, bounds, keep_rows, total_audio, pad_segment, window):
    key_clip = jnp.clip(key_pos, 0, total_audio - 1)
    key_seg = segment_of(key_clip, bounds)
    query_seg = segment_of(query_pos // 2, bounds)
    key_inside = (
        (key_pos >= 0) & (key_pos < total_audio) & (keep_rows == 1) & (key_seg < pad_segment)
    )
    nearby = jnp.abs(query_pos[None, :] - 2 * key_pos[:, None]) <= 2 * window
    return key_inside[:, None] & (key_seg[:, None] == query_seg[None, :]) & nearby


def dot(a, b, lhs_dim, rhs_dim):
    return lax.dot_general(
        a, b, (((lhs_dim,), (rhs_dim,)), ((), ())), preferred_element_type=jnp.float32
    )


def start(copies):
    for copy in copies:
        copy.start()


def wait(copies):
    for copy in copies:
        copy.wait()


def stack_kernel(key_ref, value_ref, out_ref, held, in_sems, out_sems):
    rows = held.shape[1]
    pieces = [pl.ds(i * rows, rows) for i in range(key_ref.shape[0] // rows)]
    sources = [ref.at[piece] for ref in (key_ref, value_ref) for piece in pieces]
    arrive = [
        pltpu.make_async_copy(src, held.at[i], in_sems.at[i]) for i, src in enumerate(sources)
    ]
    leave = [
        pltpu.make_async_copy(held.at[i], out_ref.at[pl.ds(i * rows, rows)], out_sems.at[i])
        for i in range(len(sources))
    ]
    start(arrive)
    for first, second in zip(arrive, leave):
        first.wait()
        second.start()
    wait(leave)


def stack_call(keys, values):
    rows, width = keys.shape
    return pl.pallas_call(
        stack_kernel,
        in_specs=[pl.BlockSpec(memory_space=pl.ANY)] * 2,
        out_specs=pl.BlockSpec(memory_space=pl.ANY),
        out_shape=jax.ShapeDtypeStruct((2 * rows, width), keys.dtype),
        scratch_shapes=[
            pltpu.VMEM((4, rows // 2, width), keys.dtype),
            pltpu.SemaphoreType.DMA((4,)),
            pltpu.SemaphoreType.DMA((4,)),
        ],
        compiler_params=pltpu.CompilerParams(vmem_limit_bytes=VMEM_LIMIT),
        name="stack",
    )(keys, values)


def prepare_kernel(q_hbm, g_hbm, own_hbm, q_ref, g_ref, own_ref, sems):
    pairs = ((q_hbm, q_ref), (g_hbm, g_ref), (own_hbm, own_ref))
    copies = [pltpu.make_async_copy(a, b, sems.at[i]) for i, (a, b) in enumerate(pairs)]
    start(copies)
    wait(copies)


def prepare_call(q, g, own):
    arrays = (q, g, own)
    return pl.pallas_call(
        prepare_kernel,
        in_specs=[pl.BlockSpec(memory_space=pl.ANY)] * 3,
        out_specs=[pl.BlockSpec(memory_space=pltpu.VMEM)] * 3,
        out_shape=[jax.ShapeDtypeStruct(x.shape, x.dtype) for x in arrays],
        scratch_shapes=[pltpu.SemaphoreType.DMA((3,))],
        compiler_params=pltpu.CompilerParams(vmem_limit_bytes=HEADS_LIMIT),
        name="prepare",
    )(*arrays)


def gathered(refs, null_ref, cols, index):
    rows = refs[0].shape[0] // 2
    return jnp.concatenate(
        [ref[index * rows : (index + 1) * rows, cols] for ref in refs] + [null_ref[index]], axis=0
    )


def heads_kernel(
    q_ref, g_ref, far_ref, own_ref, near_ref, null_ref, bias_ref, valid_ref,
    out_ref, dq_ref, far_grad_ref, own_grad_ref, near_grad_ref, null_grad_ref, null_sum,
):
    step = pl.program_id(0)
    rows = own_ref.shape[0] // 2
    refs = (far_ref, own_ref, near_ref)
    parts = range(PER_STEP)
    cols = [slice(i * HEAD, (i + 1) * HEAD) for i in parts]
    keys = [gathered(refs, null_ref.at[i], cols[i], 0) for i in parts]
    values = [gathered(refs, null_ref.at[i], cols[i], 1) for i in parts]
    scores = [dot(keys[i], q_ref[:, cols[i]], 1, 1) + bias_ref[...] for i in parts]
    tops = [jnp.max(x, axis=0, keepdims=True) for x in scores]
    exact = [jnp.exp2((x - top) * (FACTOR * LOG2E)) for x, top in zip(scores, tops)]
    shares = [valid_ref[...] / jnp.sum(x, axis=0, keepdims=True) for x in exact]
    exponents = [x.astype(jnp.bfloat16) for x in exact]
    flips = [g_ref[:, cols[i]].T.astype(jnp.float32) for i in parts]
    mixed = [dot(values[i], exponents[i], 0, 0) * shares[i] for i in parts]
    deltas = [jnp.sum(x * flip, axis=0, keepdims=True) for x, flip in zip(mixed, flips)]
    prob_grads = [dot(values[i], g_ref[:, cols[i]], 1, 1) for i in parts]
    score_grads = [
        ((x - delta) * (share * FACTOR)).astype(jnp.bfloat16) * exponent
        for x, delta, share, exponent in zip(prob_grads, deltas, shares, exponents)
    ]
    for i in parts:
        out_ref[:, cols[i]] = mixed[i].astype(jnp.bfloat16).T
        dq_ref[:, cols[i]] = dot(keys[i], score_grads[i], 0, 0).astype(jnp.bfloat16).T
        terms = (
            dot(score_grads[i], q_ref[:, cols[i]], 1, 0),
            dot(exponents[i], (flips[i] * shares[i]).astype(jnp.bfloat16), 1, 1),
        )
        for index, term in enumerate(terms):
            far_grad_ref[index, :, cols[i]] = term[:rows].astype(jnp.bfloat16)
            own_grad_ref[index, :, cols[i]] = term[rows : 2 * rows].astype(jnp.bfloat16)
            near_grad_ref[index, :, cols[i]] = term[2 * rows : 3 * rows].astype(jnp.bfloat16)
            null_sum[pl.ds(index * HEADS + step * PER_STEP + i, 1), :] = term[3 * rows : 3 * rows + 1]

    @pl.when(step == STEPS - 1)
    def _():
        null_grad_ref[...] = jnp.broadcast_to(
            null_sum[...].astype(jnp.bfloat16)[None], null_grad_ref.shape
        )


def block(*lead):
    return pl.BlockSpec((*lead, WIDE), lambda i: (0,) * len(lead) + (i,))


def whole(shape):
    return pl.BlockSpec(shape, lambda i: (0,) * len(shape))


def heads_call(q, g, far, own, near, null_rows, bias, valid, peers):
    video_rows, width = q.shape
    audio_rows = video_rows // 2
    wide = jax.ShapeDtypeStruct((video_rows, width), jnp.bfloat16)
    terms = [jax.ShapeDtypeStruct((2, audio_rows, width), jnp.bfloat16)] * 3
    null_shape = (peers, 2 * HEADS, HEAD)
    return pl.pallas_call(
        heads_kernel,
        grid=(STEPS,),
        in_specs=[block(video_rows)] * 5
        + [
            pl.BlockSpec((PER_STEP, *null_rows.shape[1:]), lambda i: (i, 0, 0, 0)),
            whole(bias.shape),
            whole(valid.shape),
        ],
        out_specs=[block(video_rows)] * 2 + [block(2, audio_rows)] * 3 + [whole(null_shape)],
        out_shape=[wide, wide, *terms, jax.ShapeDtypeStruct(null_shape, jnp.bfloat16)],
        scratch_shapes=[pltpu.VMEM((2 * HEADS, HEAD), jnp.float32)],
        compiler_params=pltpu.CompilerParams(vmem_limit_bytes=HEADS_LIMIT),
        cost_estimate=pl.CostEstimate(
            flops=12 * bias.size * width, bytes_accessed=9_000_000, transcendentals=bias.size * HEADS
        ),
        name="heads",
    )(q, g, far, own, near, null_rows, bias, valid)


def add_kernel(a_ref, b_ref, *out_refs):
    total = a_ref[...].astype(jnp.float32) + b_ref[...].astype(jnp.float32)
    if len(out_refs) == 1:
        out_refs[0][...] = total.astype(jnp.bfloat16)
    else:
        for i, ref in enumerate(out_refs):
            ref[...] = total[i].astype(jnp.bfloat16)


def add_call(a, b, split, work, name):
    _, rows, width = a.shape
    steps = 3
    both = pl.BlockSpec((2, rows, width // steps), lambda i: (0, 0, i))
    one = pl.BlockSpec((rows, width // steps), lambda i: (0, i))
    single = jax.ShapeDtypeStruct((rows, width), jnp.bfloat16)
    return pl.pallas_call(
        add_kernel,
        grid=(steps,),
        in_specs=[both, both],
        out_specs=[one, one] if split else both,
        out_shape=[single, single] if split else jax.ShapeDtypeStruct(a.shape, jnp.bfloat16),
        compiler_params=pltpu.CompilerParams(vmem_limit_bytes=ADD_LIMIT),
        cost_estimate=pl.CostEstimate(flops=a.size, bytes_accessed=work, transcendentals=0),
        name=name,
    )(a, b)


def sum_peers(parts):
    return jnp.sum(parts.astype(jnp.float32), axis=0)


def body(video_query, audio_key, audio_value, null_kv, audio_keep, clip_lengths, out_grad):
    audio_rows = audio_key.shape[0]
    video_rows = video_query.shape[0]
    shards = lax.axis_size(SEQ)
    seq_index = lax.axis_index(SEQ)
    total_audio = audio_rows * shards

    stacked = stack_call(audio_key, audio_value)
    far = swap_link(stacked)

    bounds = jnp.cumsum(clip_lengths[0])
    pad_segment = clip_lengths.shape[1] - 1
    query_pos = seq_index * video_rows + jnp.arange(video_rows, dtype=jnp.int32)
    side = 1 - 2 * (seq_index % 2)
    starts = [(seq_index + move) * audio_rows for move in (-side, 0, side)]
    own_pos = jnp.arange(audio_rows, dtype=jnp.int32)
    key_pos = jnp.concatenate([start + own_pos for start in starts])
    keep_padded = jnp.pad(audio_keep, (audio_rows, audio_rows))
    keep_rows = jnp.concatenate(
        [lax.dynamic_slice_in_dim(keep_padded, start + audio_rows, audio_rows) for start in starts]
    )
    allowed = allowed_pairs(
        query_pos, key_pos, bounds, keep_rows, total_audio, pad_segment, audio_rows
    )
    null_allowed = jnp.arange(NULL_ROWS) == 0
    bias = jnp.where(
        jnp.concatenate([allowed, jnp.broadcast_to(null_allowed[:, None], (NULL_ROWS, video_rows))]),
        0.0,
        MASKED,
    ).astype(jnp.float32)
    valid = (segment_of(query_pos // 2, bounds) < pad_segment).astype(jnp.float32)[None]
    null_heads = null_kv.reshape(2, HEADS, 1, HEAD).swapaxes(0, 1)
    null_rows = jnp.pad(null_heads, ((0, 0), (0, 0), (0, NULL_ROWS - 1), (0, 0)))

    stacked, valid = lax.optimization_barrier((stacked, valid))
    near = swap_chip(stacked)

    wide_axes, deep_axes = ("yh", "yl", "x"), ("z", "core")
    q_held, g_held, own = prepare_call(video_query, out_grad, stacked)
    attended, query_grad, far_grad, own_grad, near_grad, null_copies = heads_call(
        q_held, g_held, far, own, near, null_rows, bias, valid, lax.axis_size(wide_axes)
    )
    far_back = swap_link(far_grad)
    first = lax.all_to_all(null_copies, wide_axes, 0, 0)
    partial = sum_peers(first).astype(jnp.bfloat16)
    copies = jnp.broadcast_to(partial[None], (lax.axis_size(deep_axes), *partial.shape))
    copies, near_grad = lax.optimization_barrier((copies, near_grad))
    near_back = swap_chip(near_grad)
    second = lax.all_to_all(copies, deep_axes, 0, 0)
    part = add_call(own_grad, far_back, False, 40_000_000, "add_far")
    grads = add_call(part, near_back, True, 2_400_000, "add_near")
    second, *grads = lax.optimization_barrier((second, *grads))
    null_grad = sum_peers(second).reshape(null_kv.shape)
    return (attended, query_grad, grads[0], grads[1], null_grad)


def solution(mesh):
    parts = CLIP_PARTS + SEQ_PARTS
    fine = Mesh(
        np.asarray(mesh.devices).reshape([size for _, size in parts]), [name for name, _ in parts]
    )
    rows = P(CLIP + SEQ, None)
    return jax.shard_map(
        body,
        mesh=fine,
        in_specs=(rows, rows, rows, P(), P(CLIP), P(CLIP, None), rows),
        out_specs=(rows, rows, rows, rows, P()),
        check_vma=False,
    )
```

```python
import numpy as np

import jax
import jax.numpy as jnp
from jax import lax
from jax.experimental import pallas as pl
from jax.experimental.pallas import tpu as pltpu
from jax.sharding import Mesh
from jax.sharding import PartitionSpec as P

HEADS = 12
HEAD = 128
NULL_ROWS = 16
MASKED = -1e30
FACTOR = HEAD**-0.5
LOG2E = 1.4426950408889634
CLIP_PARTS = (("yh", 2), ("z", 8))
SEQ_PARTS = (("yl", 4), ("x", 4), ("core", 2))
CLIP = tuple(name for name, _ in CLIP_PARTS)
SEQ = tuple(name for name, _ in SEQ_PARTS)
VMEM_LIMIT = 60 * 1024 * 1024
HEADS_LIMIT = 36 * 1024 * 1024
PREPARE_LIMIT = 24 * 1024 * 1024
ADD_LIMIT = 8 * 1024 * 1024
PER_STEP = 6
STEPS = HEADS // PER_STEP
WIDE = PER_STEP * HEAD


def swap_chip(block):
    count = lax.axis_size(SEQ)
    return lax.ppermute(block, SEQ, [(i, i ^ 1) for i in range(count)])


def swap_link(block):
    last = lax.axis_size(SEQ) - 1
    pairs = [(i, i + 1) for i in range(1, last, 2)]
    return lax.ppermute(block, SEQ, pairs + [(b, a) for a, b in pairs])


def segment_of(positions, bounds):
    return jnp.sum((positions[:, None] >= bounds[None, :-1]).astype(jnp.int32), axis=1)


def allowed_pairs(query_pos, key_pos, bounds, keep_rows, total_audio, pad_segment, window):
    key_clip = jnp.clip(key_pos, 0, total_audio - 1)
    key_seg = segment_of(key_clip, bounds)
    query_seg = segment_of(query_pos // 2, bounds)
    key_inside = (
        (key_pos >= 0) & (key_pos < total_audio) & (keep_rows == 1) & (key_seg < pad_segment)
    )
    nearby = jnp.abs(query_pos[None, :] - 2 * key_pos[:, None]) <= 2 * window
    return key_inside[:, None] & (key_seg[:, None] == query_seg[None, :]) & nearby


def dot(a, b, lhs_dim, rhs_dim):
    return lax.dot_general(
        a, b, (((lhs_dim,), (rhs_dim,)), ((), ())), preferred_element_type=jnp.float32
    )


def start(copies):
    for copy in copies:
        copy.start()


def wait(copies):
    for copy in copies:
        copy.wait()


def stack_kernel(key_ref, value_ref, out_ref, held, in_sems, out_sems):
    rows = held.shape[1]
    pieces = [pl.ds(i * rows, rows) for i in range(key_ref.shape[0] // rows)]
    sources = [ref.at[piece] for ref in (key_ref, value_ref) for piece in pieces]
    arrive = [
        pltpu.make_async_copy(src, held.at[i], in_sems.at[i]) for i, src in enumerate(sources)
    ]
    leave = [
        pltpu.make_async_copy(held.at[i], out_ref.at[pl.ds(i * rows, rows)], out_sems.at[i])
        for i in range(len(sources))
    ]
    start(arrive)
    for first, second in zip(arrive, leave):
        first.wait()
        second.start()
    wait(leave)


def stack_call(keys, values):
    rows, width = keys.shape
    return pl.pallas_call(
        stack_kernel,
        in_specs=[pl.BlockSpec(memory_space=pl.ANY)] * 2,
        out_specs=pl.BlockSpec(memory_space=pl.ANY),
        out_shape=jax.ShapeDtypeStruct((2 * rows, width), keys.dtype),
        scratch_shapes=[
            pltpu.VMEM((4, rows // 2, width), keys.dtype),
            pltpu.SemaphoreType.DMA((4,)),
            pltpu.SemaphoreType.DMA((4,)),
        ],
        compiler_params=pltpu.CompilerParams(vmem_limit_bytes=VMEM_LIMIT),
        name="stack",
    )(keys, values)


def prepare_kernel(
    q_hbm, g_hbm, own_hbm, near_hbm, q_ref, g_ref, own_ref, near_ref,
    g_flip, own_flip, near_flip, sems,
):
    pairs = ((g_hbm, g_ref), (own_hbm, own_ref), (near_hbm, near_ref), (q_hbm, q_ref))
    copies = [pltpu.make_async_copy(a, b, sems.at[i]) for i, (a, b) in enumerate(pairs)]
    start(copies)
    wait(copies)
    for head in range(HEADS):
        span = slice(head * HEAD, (head + 1) * HEAD)
        for ref, flip in ((g_ref, g_flip), (own_ref, own_flip), (near_ref, near_flip)):
            flip[span, :] = ref[:, span].T


def prepare_call(q, g, own, near):
    arrays = (q, g, own, near)
    inside = pl.BlockSpec(memory_space=pltpu.VMEM)
    flips = [jax.ShapeDtypeStruct(x.shape[::-1], x.dtype) for x in (g, own, near)]
    return pl.pallas_call(
        prepare_kernel,
        in_specs=[pl.BlockSpec(memory_space=pl.ANY)] * 4,
        out_specs=[inside] * 7,
        out_shape=[jax.ShapeDtypeStruct(x.shape, x.dtype) for x in arrays] + flips,
        scratch_shapes=[pltpu.SemaphoreType.DMA((4,))],
        compiler_params=pltpu.CompilerParams(vmem_limit_bytes=PREPARE_LIMIT),
        name="prepare",
    )(*arrays)


def gathered(refs, null_ref, cols, index):
    rows = refs[0].shape[0] // 2
    return jnp.concatenate(
        [ref[index * rows : (index + 1) * rows, cols] for ref in refs] + [null_ref[index]], axis=0
    )


def flipped(far_ref, own_flip, near_flip, null_flip, cols, index):
    rows = far_ref.shape[0] // 2
    span = slice(index * rows, (index + 1) * rows)
    far = far_ref[span, cols].T
    return jnp.concatenate([far, own_flip[cols, span], near_flip[cols, span], null_flip[index]], axis=1)


def heads_kernel(
    q_ref, g_ref, far_ref, own_ref, near_ref, g_flip, own_flip, near_flip,
    null_ref, null_flip, bias_ref, valid_ref,
    out_ref, dq_ref, far_grad_ref, own_grad_ref, near_grad_ref, null_grad_ref, null_sum,
):
    step = pl.program_id(0)
    rows = own_ref.shape[0] // 2
    refs = (far_ref, own_ref, near_ref)
    parts = range(PER_STEP)
    cols = [slice(i * HEAD, (i + 1) * HEAD) for i in parts]
    keys = [gathered(refs, null_ref.at[i], cols[i], 0) for i in parts]
    values = [gathered(refs, null_ref.at[i], cols[i], 1) for i in parts]
    scores = [dot(keys[i], q_ref[:, cols[i]], 1, 1) + bias_ref[...] for i in parts]
    tops = [jnp.max(x, axis=0, keepdims=True) for x in scores]
    exact = [jnp.exp2((x - top) * (FACTOR * LOG2E)) for x, top in zip(scores, tops)]
    shares = [valid_ref[...] / jnp.sum(x, axis=0, keepdims=True) for x in exact]
    exponents = [x.astype(jnp.bfloat16) for x in exact]
    flips = [g_flip[cols[i], :].astype(jnp.float32) for i in parts]
    keys_flip, values_flip = [
        [flipped(far_ref, own_flip, near_flip, null_flip.at[i], cols[i], index) for i in parts]
        for index in range(2)
    ]
    mixed = [dot(values_flip[i], exponents[i], 1, 0) * shares[i] for i in parts]
    deltas = [jnp.sum(x * flip, axis=0, keepdims=True) for x, flip in zip(mixed, flips)]
    prob_grads = [dot(values[i], g_ref[:, cols[i]], 1, 1) for i in parts]
    score_grads = [
        ((x - delta) * (share * FACTOR)).astype(jnp.bfloat16) * exponent
        for x, delta, share, exponent in zip(prob_grads, deltas, shares, exponents)
    ]
    for i in parts:
        out_ref[:, cols[i]] = mixed[i].astype(jnp.bfloat16).T
        dq_ref[:, cols[i]] = dot(keys_flip[i], score_grads[i], 1, 0).astype(jnp.bfloat16).T
        terms = (
            dot(score_grads[i], q_ref[:, cols[i]], 1, 0),
            dot(exponents[i], (flips[i] * shares[i]).astype(jnp.bfloat16), 1, 1),
        )
        for index, term in enumerate(terms):
            far_grad_ref[index, :, cols[i]] = term[:rows].astype(jnp.bfloat16)
            own_grad_ref[index, :, cols[i]] = term[rows : 2 * rows].astype(jnp.bfloat16)
            near_grad_ref[index, :, cols[i]] = term[2 * rows : 3 * rows].astype(jnp.bfloat16)
            null_sum[pl.ds(index * HEADS + step * PER_STEP + i, 1), :] = term[3 * rows : 3 * rows + 1]

    @pl.when(step == STEPS - 1)
    def _():
        null_grad_ref[...] = jnp.broadcast_to(
            null_sum[...].astype(jnp.bfloat16)[None], null_grad_ref.shape
        )


def block(*lead):
    return pl.BlockSpec((*lead, WIDE), lambda i: (0,) * len(lead) + (i,))


def whole(shape):
    return pl.BlockSpec(shape, lambda i: (0,) * len(shape))


def heads_call(q, g, far, own, near, flips, null_rows, null_flip, bias, valid, peers):
    video_rows, width = q.shape
    audio_rows = video_rows // 2
    wide = jax.ShapeDtypeStruct((video_rows, width), jnp.bfloat16)
    terms = [jax.ShapeDtypeStruct((2, audio_rows, width), jnp.bfloat16)] * 3
    null_shape = (peers, 2 * HEADS, HEAD)
    return pl.pallas_call(
        heads_kernel,
        grid=(STEPS,),
        in_specs=[block(video_rows)] * 5
        + [pl.BlockSpec((WIDE, video_rows), lambda i: (i, 0))] * 3
        + [
            pl.BlockSpec((PER_STEP, *null_rows.shape[1:]), lambda i: (i, 0, 0, 0)),
            pl.BlockSpec((PER_STEP, *null_flip.shape[1:]), lambda i: (i, 0, 0, 0)),
            whole(bias.shape),
            whole(valid.shape),
        ],
        out_specs=[block(video_rows)] * 2 + [block(2, audio_rows)] * 3 + [whole(null_shape)],
        out_shape=[wide, wide, *terms, jax.ShapeDtypeStruct(null_shape, jnp.bfloat16)],
        scratch_shapes=[pltpu.VMEM((2 * HEADS, HEAD), jnp.float32)],
        compiler_params=pltpu.CompilerParams(vmem_limit_bytes=HEADS_LIMIT),
        cost_estimate=pl.CostEstimate(
            flops=12 * bias.size * width, bytes_accessed=9_000_000, transcendentals=bias.size * HEADS
        ),
        name="heads",
    )(q, g, far, own, near, *flips, null_rows, null_flip, bias, valid)


def add_kernel(a_ref, b_ref, *out_refs):
    total = a_ref[...].astype(jnp.float32) + b_ref[...].astype(jnp.float32)
    if len(out_refs) == 1:
        out_refs[0][...] = total.astype(jnp.bfloat16)
    else:
        for i, ref in enumerate(out_refs):
            ref[...] = total[i].astype(jnp.bfloat16)


def add_call(a, b, split, work, name):
    _, rows, width = a.shape
    steps = 3
    both = pl.BlockSpec((2, rows, width // steps), lambda i: (0, 0, i))
    one = pl.BlockSpec((rows, width // steps), lambda i: (0, i))
    single = jax.ShapeDtypeStruct((rows, width), jnp.bfloat16)
    return pl.pallas_call(
        add_kernel,
        grid=(steps,),
        in_specs=[both, both],
        out_specs=[one, one] if split else both,
        out_shape=[single, single] if split else jax.ShapeDtypeStruct(a.shape, jnp.bfloat16),
        compiler_params=pltpu.CompilerParams(vmem_limit_bytes=ADD_LIMIT),
        cost_estimate=pl.CostEstimate(flops=a.size, bytes_accessed=work, transcendentals=0),
        name=name,
    )(a, b)


def sum_peers(parts):
    return jnp.sum(parts.astype(jnp.float32), axis=0)


def body(video_query, audio_key, audio_value, null_kv, audio_keep, clip_lengths, out_grad):
    audio_rows = audio_key.shape[0]
    video_rows = video_query.shape[0]
    shards = lax.axis_size(SEQ)
    seq_index = lax.axis_index(SEQ)
    total_audio = audio_rows * shards

    stacked = stack_call(audio_key, audio_value)
    far = swap_link(stacked)

    bounds = jnp.cumsum(clip_lengths[0])
    pad_segment = clip_lengths.shape[1] - 1
    query_pos = seq_index * video_rows + jnp.arange(video_rows, dtype=jnp.int32)
    side = 1 - 2 * (seq_index % 2)
    starts = [(seq_index + move) * audio_rows for move in (-side, 0, side)]
    own_pos = jnp.arange(audio_rows, dtype=jnp.int32)
    key_pos = jnp.concatenate([start + own_pos for start in starts])
    keep_padded = jnp.pad(audio_keep, (audio_rows, audio_rows))
    keep_rows = jnp.concatenate(
        [lax.dynamic_slice_in_dim(keep_padded, start + audio_rows, audio_rows) for start in starts]
    )
    allowed = allowed_pairs(
        query_pos, key_pos, bounds, keep_rows, total_audio, pad_segment, audio_rows
    )
    null_allowed = jnp.arange(NULL_ROWS) == 0
    bias = jnp.where(
        jnp.concatenate([allowed, jnp.broadcast_to(null_allowed[:, None], (NULL_ROWS, video_rows))]),
        0.0,
        MASKED,
    ).astype(jnp.float32)
    valid = (segment_of(query_pos // 2, bounds) < pad_segment).astype(jnp.float32)[None]
    null_heads = null_kv.reshape(2, HEADS, HEAD).swapaxes(0, 1)
    first_only = jnp.arange(NULL_ROWS) == 0
    null_rows = jnp.where(first_only[:, None], null_heads[:, :, None], jnp.bfloat16(0))
    null_flip = jnp.where(first_only, null_heads[..., None], jnp.bfloat16(0))

    stacked, valid = lax.optimization_barrier((stacked, valid))
    near = swap_chip(stacked)

    wide_axes, deep_axes = ("yh", "yl", "x"), ("z", "core")
    q_held, g_held, own, near, *flips = prepare_call(video_query, out_grad, stacked, near)
    attended, query_grad, far_grad, own_grad, near_grad, null_copies = heads_call(
        q_held, g_held, far, own, near, flips, null_rows, null_flip, bias, valid,
        lax.axis_size(wide_axes),
    )
    far_back = swap_link(far_grad)
    first = lax.all_to_all(null_copies, wide_axes, 0, 0)
    partial = sum_peers(first).astype(jnp.bfloat16)
    copies = jnp.broadcast_to(partial[None], (lax.axis_size(deep_axes), *partial.shape))
    copies, near_grad = lax.optimization_barrier((copies, near_grad))
    near_back = swap_chip(near_grad)
    second = lax.all_to_all(copies, deep_axes, 0, 0)
    part = add_call(own_grad, far_back, False, 400_000_000, "add_far")
    grads = add_call(part, near_back, True, 2_400_000, "add_near")
    second, *grads = lax.optimization_barrier((second, *grads))
    null_grad = sum_peers(second).reshape(null_kv.shape)
    return (attended, query_grad, grads[0], grads[1], null_grad)


def solution(mesh):
    parts = CLIP_PARTS + SEQ_PARTS
    fine = Mesh(
        np.asarray(mesh.devices).reshape([size for _, size in parts]), [name for name, _ in parts]
    )
    rows = P(CLIP + SEQ, None)
    return jax.shard_map(
        body,
        mesh=fine,
        in_specs=(rows, rows, rows, P(), P(CLIP), P(CLIP, None), rows),
        out_specs=(rows, rows, rows, rows, P()),
        check_vma=False,
    )
```

```python
import numpy as np

import jax
import jax.numpy as jnp
from jax import lax
from jax.experimental import pallas as pl
from jax.experimental.pallas import tpu as pltpu
from jax.sharding import Mesh
from jax.sharding import PartitionSpec as P

HEADS = 12
HEAD = 128
NULL_ROWS = 16
MASKED = -1e30
FACTOR = HEAD**-0.5
LOG2E = 1.4426950408889634
CLIP_PARTS = (("yh", 2), ("z", 8))
SEQ_PARTS = (("yl", 4), ("x", 4), ("core", 2))
CLIP = tuple(name for name, _ in CLIP_PARTS)
SEQ = tuple(name for name, _ in SEQ_PARTS)
VMEM_LIMIT = 60 * 1024 * 1024
HEADS_LIMIT = 36 * 1024 * 1024
PREPARE_LIMIT = 24 * 1024 * 1024
ADD_LIMIT = 8 * 1024 * 1024
PER_STEP = 6
STEPS = HEADS // PER_STEP
WIDE = PER_STEP * HEAD


def swap_chip(block):
    count = lax.axis_size(SEQ)
    return lax.ppermute(block, SEQ, [(i, i ^ 1) for i in range(count)])


def swap_link(block):
    last = lax.axis_size(SEQ) - 1
    pairs = [(i, i + 1) for i in range(1, last, 2)]
    return lax.ppermute(block, SEQ, pairs + [(b, a) for a, b in pairs])


def segment_of(positions, bounds):
    return jnp.sum((positions[:, None] >= bounds[None, :-1]).astype(jnp.int32), axis=1)


def allowed_pairs(query_pos, key_pos, bounds, keep_rows, total_audio, pad_segment, window):
    key_clip = jnp.clip(key_pos, 0, total_audio - 1)
    key_seg = segment_of(key_clip, bounds)
    query_seg = segment_of(query_pos // 2, bounds)
    key_inside = (
        (key_pos >= 0) & (key_pos < total_audio) & (keep_rows == 1) & (key_seg < pad_segment)
    )
    nearby = jnp.abs(query_pos[None, :] - 2 * key_pos[:, None]) <= 2 * window
    return key_inside[:, None] & (key_seg[:, None] == query_seg[None, :]) & nearby


def dot(a, b, lhs_dim, rhs_dim):
    return lax.dot_general(
        a, b, (((lhs_dim,), (rhs_dim,)), ((), ())), preferred_element_type=jnp.float32
    )


def start(copies):
    for copy in copies:
        copy.start()


def wait(copies):
    for copy in copies:
        copy.wait()


def stack_kernel(key_ref, value_ref, out_ref, held, in_sems, out_sems):
    rows = held.shape[1]
    pieces = [pl.ds(i * rows, rows) for i in range(key_ref.shape[0] // rows)]
    sources = [ref.at[piece] for ref in (key_ref, value_ref) for piece in pieces]
    arrive = [
        pltpu.make_async_copy(src, held.at[i], in_sems.at[i]) for i, src in enumerate(sources)
    ]
    leave = [
        pltpu.make_async_copy(held.at[i], out_ref.at[pl.ds(i * rows, rows)], out_sems.at[i])
        for i in range(len(sources))
    ]
    start(arrive)
    for first, second in zip(arrive, leave):
        first.wait()
        second.start()
    wait(leave)


def stack_call(keys, values):
    rows, width = keys.shape
    return pl.pallas_call(
        stack_kernel,
        in_specs=[pl.BlockSpec(memory_space=pl.ANY)] * 2,
        out_specs=pl.BlockSpec(memory_space=pl.ANY),
        out_shape=jax.ShapeDtypeStruct((2 * rows, width), keys.dtype),
        scratch_shapes=[
            pltpu.VMEM((4, rows // 2, width), keys.dtype),
            pltpu.SemaphoreType.DMA((4,)),
            pltpu.SemaphoreType.DMA((4,)),
        ],
        compiler_params=pltpu.CompilerParams(vmem_limit_bytes=VMEM_LIMIT),
        name="stack",
    )(keys, values)


def prepare_kernel(
    q_in, g_in, own_ref, near_ref, bias_ref,
    q_ref, g_ref, g_flip, keys_flip, exponent_ref, prob_grad_ref, mixed_ref, stats_ref,
):
    rows = own_ref.shape[0] // 2
    parts = range(PER_STEP)
    cols = [slice(i * HEAD, (i + 1) * HEAD) for i in parts]
    sides = (own_ref, near_ref)
    keys, values = [
        [jnp.concatenate([ref[span, cols[i]] for ref in sides], axis=0) for i in parts]
        for span in (slice(0, rows), slice(rows, 2 * rows))
    ]
    scores = [dot(keys[i], q_in[:, cols[i]], 1, 1) + bias_ref[...] for i in parts]
    tops = [jnp.max(x, axis=0, keepdims=True) for x in scores]
    exact = [jnp.exp2((x - top) * (FACTOR * LOG2E)) for x, top in zip(scores, tops)]
    exponents = [x.astype(jnp.bfloat16) for x in exact]
    for i in parts:
        stats_ref[i, 0:1] = tops[i]
        stats_ref[i, 1:2] = jnp.sum(exact[i], axis=0, keepdims=True)
        exponent_ref[i] = exponents[i]
        prob_grad_ref[i] = dot(values[i], g_in[:, cols[i]], 1, 1)
        mixed_ref[cols[i], :] = dot(values[i].T, exponents[i], 1, 0)
        keys_flip[cols[i], :] = keys[i].T
        g_flip[cols[i], :] = g_in[:, cols[i]].T
    q_ref[...] = q_in[...]
    g_ref[...] = g_in[...]


def prepare_call(q, g, own, near, bias):
    video_rows, width = q.shape
    local_rows = bias.shape[0]
    deep = pl.BlockSpec((WIDE, video_rows), lambda i: (i, 0))
    deep_shape = (width, video_rows)
    pairs = pl.BlockSpec((PER_STEP, local_rows, video_rows), lambda i: (i, 0, 0))
    pair_shape = (HEADS, local_rows, video_rows)
    outs = [
        (block(video_rows), q.shape, jnp.bfloat16),
        (block(video_rows), g.shape, jnp.bfloat16),
        (deep, deep_shape, jnp.bfloat16),
        (deep, deep_shape, jnp.bfloat16),
        (pairs, pair_shape, jnp.bfloat16),
        (pairs, pair_shape, jnp.float32),
        (deep, deep_shape, jnp.float32),
        (pl.BlockSpec((PER_STEP, 8, video_rows), lambda i: (i, 0, 0)), (HEADS, 8, video_rows), jnp.float32),
    ]
    return pl.pallas_call(
        prepare_kernel,
        grid=(STEPS,),
        in_specs=[block(video_rows)] * 4 + [whole(bias.shape)],
        out_specs=[spec for spec, _, _ in outs],
        out_shape=[jax.ShapeDtypeStruct(shape, dtype) for _, shape, dtype in outs],
        compiler_params=pltpu.CompilerParams(vmem_limit_bytes=PREPARE_LIMIT),
        cost_estimate=pl.CostEstimate(
            flops=6 * bias.size * width, bytes_accessed=9_000_000, transcendentals=bias.size * HEADS
        ),
        name="prepare",
    )(q, g, own, near, bias)


def heads_kernel(
    q_ref, g_ref, far_ref, g_flip, near_keys_flip, near_exponent, near_prob_grad, near_mixed, stats,
    null_ref, null_flip, bias_ref, valid_ref,
    out_ref, dq_ref, far_grad_ref, own_grad_ref, near_grad_ref, null_grad_ref, null_sum,
):
    step = pl.program_id(0)
    rows = far_ref.shape[0] // 2
    parts = range(PER_STEP)
    cols = [slice(i * HEAD, (i + 1) * HEAD) for i in parts]
    spans = (slice(0, rows), slice(rows, 2 * rows))
    keys, values = [
        [jnp.concatenate([far_ref[span, cols[i]], null_ref[i, index]], axis=0) for i in parts]
        for index, span in enumerate(spans)
    ]
    keys_flip, values_flip = [
        [jnp.concatenate([far_ref[span, cols[i]].T, null_flip[i, index]], axis=1) for i in parts]
        for index, span in enumerate(spans)
    ]
    scale = FACTOR * LOG2E
    scores = [dot(keys[i], q_ref[:, cols[i]], 1, 1) + bias_ref[...] for i in parts]
    tops = [
        jnp.maximum(jnp.max(x, axis=0, keepdims=True), stats[i, 0:1]) for i, x in enumerate(scores)
    ]
    exact = [jnp.exp2((x - top) * scale) for x, top in zip(scores, tops)]
    joins = [jnp.exp2((stats[i, 0:1] - tops[i]) * scale) for i in parts]
    totals = [
        jnp.sum(x, axis=0, keepdims=True) + joins[i] * stats[i, 1:2] for i, x in enumerate(exact)
    ]
    shares = [valid_ref[...] / total for total in totals]
    near_shares = [share * join for share, join in zip(shares, joins)]
    exponents = [x.astype(jnp.bfloat16) for x in exact]
    flips = [g_flip[cols[i], :].astype(jnp.float32) for i in parts]
    mixed = [
        dot(values_flip[i], exponents[i], 1, 0) * shares[i] + near_mixed[cols[i], :] * near_shares[i]
        for i in parts
    ]
    deltas = [jnp.sum(x * flip, axis=0, keepdims=True) for x, flip in zip(mixed, flips)]
    prob_grads = [dot(values[i], g_ref[:, cols[i]], 1, 1) for i in parts]
    score_grads = [
        ((prob_grads[i] - deltas[i]) * (shares[i] * FACTOR)).astype(jnp.bfloat16) * exponents[i]
        for i in parts
    ]
    near_score_grads = [
        ((near_prob_grad[i] - deltas[i]) * (near_shares[i] * FACTOR)).astype(jnp.bfloat16)
        * near_exponent[i]
        for i in parts
    ]
    for i in parts:
        out_ref[:, cols[i]] = mixed[i].astype(jnp.bfloat16).T
        query_grad = dot(keys_flip[i], score_grads[i], 1, 0)
        query_grad = query_grad + dot(near_keys_flip[cols[i], :], near_score_grads[i], 1, 0)
        dq_ref[:, cols[i]] = query_grad.astype(jnp.bfloat16).T
        q = q_ref[:, cols[i]]
        terms = (
            (dot(score_grads[i], q, 1, 0), dot(near_score_grads[i], q, 1, 0)),
            (
                dot(exponents[i], (flips[i] * shares[i]).astype(jnp.bfloat16), 1, 1),
                dot(near_exponent[i], (flips[i] * near_shares[i]).astype(jnp.bfloat16), 1, 1),
            ),
        )
        for index, (term, near_term) in enumerate(terms):
            far_grad_ref[index, :, cols[i]] = term[:rows].astype(jnp.bfloat16)
            own_grad_ref[index, :, cols[i]] = near_term[:rows].astype(jnp.bfloat16)
            near_grad_ref[index, :, cols[i]] = near_term[rows:].astype(jnp.bfloat16)
            null_sum[pl.ds(index * HEADS + step * PER_STEP + i, 1), :] = term[rows : rows + 1]

    @pl.when(step == STEPS - 1)
    def _():
        null_grad_ref[...] = jnp.broadcast_to(
            null_sum[...].astype(jnp.bfloat16)[None], null_grad_ref.shape
        )


def block(*lead):
    return pl.BlockSpec((*lead, WIDE), lambda i: (0,) * len(lead) + (i,))


def whole(shape):
    return pl.BlockSpec(shape, lambda i: (0,) * len(shape))


def heads_call(q, g, far, near_parts, null_rows, null_flip, bias, valid, peers):
    video_rows, width = q.shape
    audio_rows = video_rows // 2
    wide = jax.ShapeDtypeStruct((video_rows, width), jnp.bfloat16)
    terms = [jax.ShapeDtypeStruct((2, audio_rows, width), jnp.bfloat16)] * 3
    null_shape = (peers, 2 * HEADS, HEAD)
    deep = pl.BlockSpec((WIDE, video_rows), lambda i: (i, 0))
    pairs = pl.BlockSpec((PER_STEP, 2 * audio_rows, video_rows), lambda i: (i, 0, 0))
    return pl.pallas_call(
        heads_kernel,
        grid=(STEPS,),
        in_specs=[block(video_rows)] * 3
        + [deep, deep, pairs, pairs, deep]
        + [
            pl.BlockSpec((PER_STEP, 8, video_rows), lambda i: (i, 0, 0)),
            pl.BlockSpec((PER_STEP, *null_rows.shape[1:]), lambda i: (i, 0, 0, 0)),
            pl.BlockSpec((PER_STEP, *null_flip.shape[1:]), lambda i: (i, 0, 0, 0)),
            whole(bias.shape),
            whole(valid.shape),
        ],
        out_specs=[block(video_rows)] * 2 + [block(2, audio_rows)] * 3 + [whole(null_shape)],
        out_shape=[wide, wide, *terms, jax.ShapeDtypeStruct(null_shape, jnp.bfloat16)],
        scratch_shapes=[pltpu.VMEM((2 * HEADS, HEAD), jnp.float32)],
        compiler_params=pltpu.CompilerParams(vmem_limit_bytes=HEADS_LIMIT),
        cost_estimate=pl.CostEstimate(
            flops=12 * bias.size * width, bytes_accessed=9_000_000, transcendentals=bias.size * HEADS
        ),
        name="heads",
    )(q, g, far, *near_parts, null_rows, null_flip, bias, valid)


def add_kernel(a_ref, b_ref, *out_refs):
    total = a_ref[...].astype(jnp.float32) + b_ref[...].astype(jnp.float32)
    if len(out_refs) == 1:
        out_refs[0][...] = total.astype(jnp.bfloat16)
    else:
        for i, ref in enumerate(out_refs):
            ref[...] = total[i].astype(jnp.bfloat16)


def add_call(a, b, split, work, name):
    _, rows, width = a.shape
    steps = 3
    both = pl.BlockSpec((2, rows, width // steps), lambda i: (0, 0, i))
    one = pl.BlockSpec((rows, width // steps), lambda i: (0, i))
    single = jax.ShapeDtypeStruct((rows, width), jnp.bfloat16)
    return pl.pallas_call(
        add_kernel,
        grid=(steps,),
        in_specs=[both, both],
        out_specs=[one, one] if split else both,
        out_shape=[single, single] if split else jax.ShapeDtypeStruct(a.shape, jnp.bfloat16),
        compiler_params=pltpu.CompilerParams(vmem_limit_bytes=ADD_LIMIT),
        cost_estimate=pl.CostEstimate(flops=a.size, bytes_accessed=work, transcendentals=0),
        name=name,
    )(a, b)


def sum_peers(parts):
    return jnp.sum(parts.astype(jnp.float32), axis=0)


def body(video_query, audio_key, audio_value, null_kv, audio_keep, clip_lengths, out_grad):
    audio_rows = audio_key.shape[0]
    video_rows = video_query.shape[0]
    shards = lax.axis_size(SEQ)
    seq_index = lax.axis_index(SEQ)
    total_audio = audio_rows * shards

    stacked = stack_call(audio_key, audio_value)
    far = swap_link(stacked)

    bounds = jnp.cumsum(clip_lengths[0])
    pad_segment = clip_lengths.shape[1] - 1
    query_pos = seq_index * video_rows + jnp.arange(video_rows, dtype=jnp.int32)
    side = 1 - 2 * (seq_index % 2)
    starts = [(seq_index + move) * audio_rows for move in (-side, 0, side)]
    own_pos = jnp.arange(audio_rows, dtype=jnp.int32)
    key_pos = jnp.concatenate([start + own_pos for start in starts])
    keep_padded = jnp.pad(audio_keep, (audio_rows, audio_rows))
    keep_rows = jnp.concatenate(
        [lax.dynamic_slice_in_dim(keep_padded, start + audio_rows, audio_rows) for start in starts]
    )
    allowed = allowed_pairs(
        query_pos, key_pos, bounds, keep_rows, total_audio, pad_segment, audio_rows
    )
    near_bias = jnp.where(allowed[audio_rows:], 0.0, MASKED).astype(jnp.float32)
    null_allowed = jnp.broadcast_to(jnp.arange(NULL_ROWS)[:, None] == 0, (NULL_ROWS, video_rows))
    far_allowed = jnp.concatenate([allowed[:audio_rows], null_allowed])
    bias = jnp.where(far_allowed, 0.0, MASKED).astype(jnp.float32)
    valid = (segment_of(query_pos // 2, bounds) < pad_segment).astype(jnp.float32)[None]
    null_heads = null_kv.reshape(2, HEADS, HEAD).swapaxes(0, 1)
    first_only = jnp.arange(NULL_ROWS) == 0
    null_rows = jnp.where(first_only[:, None], null_heads[:, :, None], jnp.bfloat16(0))
    null_flip = jnp.where(first_only, null_heads[..., None], jnp.bfloat16(0))

    stacked, valid = lax.optimization_barrier((stacked, valid))
    near = swap_chip(stacked)

    wide_axes, deep_axes = ("yh", "yl", "x"), ("z", "core")
    q_held, g_held, *near_parts = prepare_call(video_query, out_grad, stacked, near, near_bias)
    attended, query_grad, far_grad, own_grad, near_grad, null_copies = heads_call(
        q_held, g_held, far, near_parts, null_rows, null_flip, bias, valid, lax.axis_size(wide_axes)
    )
    far_back = swap_link(far_grad)
    first = lax.all_to_all(null_copies, wide_axes, 0, 0)
    partial = sum_peers(first).astype(jnp.bfloat16)
    copies = jnp.broadcast_to(partial[None], (lax.axis_size(deep_axes), *partial.shape))
    copies, near_grad = lax.optimization_barrier((copies, near_grad))
    near_back = swap_chip(near_grad)
    second = lax.all_to_all(copies, deep_axes, 0, 0)
    part = add_call(own_grad, far_back, False, 4_000_000, "add_far")
    grads = add_call(part, near_back, True, 2_400_000, "add_near")
    second, *grads = lax.optimization_barrier((second, *grads))
    null_grad = sum_peers(second).reshape(null_kv.shape)
    return (attended, query_grad, grads[0], grads[1], null_grad)


def solution(mesh):
    parts = CLIP_PARTS + SEQ_PARTS
    fine = Mesh(
        np.asarray(mesh.devices).reshape([size for _, size in parts]), [name for name, _ in parts]
    )
    rows = P(CLIP + SEQ, None)
    return jax.shard_map(
        body,
        mesh=fine,
        in_specs=(rows, rows, rows, P(), P(CLIP), P(CLIP, None), rows),
        out_specs=(rows, rows, rows, rows, P()),
        check_vma=False,
    )
```

```python
import numpy as np

import jax
import jax.numpy as jnp
from jax import lax
from jax.experimental import pallas as pl
from jax.experimental.pallas import tpu as pltpu
from jax.sharding import Mesh
from jax.sharding import PartitionSpec as P

HEADS = 12
HEAD = 128
NULL_ROWS = 16
MASKED = -1e30
FACTOR = HEAD**-0.5
LOG2E = 1.4426950408889634
CLIP_PARTS = (("yh", 2), ("z", 8))
SEQ_PARTS = (("yl", 4), ("x", 4), ("core", 2))
CLIP = tuple(name for name, _ in CLIP_PARTS)
SEQ = tuple(name for name, _ in SEQ_PARTS)
STACK_LIMIT = 4 * 1024 * 1024
HEADS_LIMIT = 36 * 1024 * 1024
PREPARE_LIMIT = 24 * 1024 * 1024
ADD_LIMIT = 8 * 1024 * 1024
PER_STEP = 6
STEPS = HEADS // PER_STEP
WIDE = PER_STEP * HEAD


def swap_chip(block):
    count = lax.axis_size(SEQ)
    return lax.ppermute(block, SEQ, [(i, i ^ 1) for i in range(count)])


def swap_link(block):
    last = lax.axis_size(SEQ) - 1
    pairs = [(i, i + 1) for i in range(1, last, 2)]
    return lax.ppermute(block, SEQ, pairs + [(b, a) for a, b in pairs])


def segment_of(positions, bounds):
    return jnp.sum((positions[:, None] >= bounds[None, :-1]).astype(jnp.int32), axis=1)


def allowed_pairs(query_pos, key_pos, bounds, keep_rows, total_audio, pad_segment, window):
    key_clip = jnp.clip(key_pos, 0, total_audio - 1)
    key_seg = segment_of(key_clip, bounds)
    query_seg = segment_of(query_pos // 2, bounds)
    key_inside = (
        (key_pos >= 0) & (key_pos < total_audio) & (keep_rows == 1) & (key_seg < pad_segment)
    )
    nearby = jnp.abs(query_pos[None, :] - 2 * key_pos[:, None]) <= 2 * window
    return key_inside[:, None] & (key_seg[:, None] == query_seg[None, :]) & nearby


def dot(a, b, lhs_dim, rhs_dim):
    return lax.dot_general(
        a, b, (((lhs_dim,), (rhs_dim,)), ((), ())), preferred_element_type=jnp.float32
    )


def start(copies):
    for copy in copies:
        copy.start()


def wait(copies):
    for copy in copies:
        copy.wait()


def stack_kernel(key_ref, value_ref, out_ref, sems):
    rows = key_ref.shape[0]
    copies = [
        pltpu.make_async_copy(ref, out_ref.at[pl.ds(i * rows, rows)], sems.at[i])
        for i, ref in enumerate((key_ref, value_ref))
    ]
    start(copies)
    wait(copies)


def stack_call(keys, values):
    rows, width = keys.shape
    return pl.pallas_call(
        stack_kernel,
        in_specs=[pl.BlockSpec(memory_space=pl.ANY)] * 2,
        out_specs=pl.BlockSpec(memory_space=pltpu.VMEM),
        out_shape=jax.ShapeDtypeStruct((2 * rows, width), keys.dtype),
        scratch_shapes=[pltpu.SemaphoreType.DMA((2,))],
        compiler_params=pltpu.CompilerParams(vmem_limit_bytes=STACK_LIMIT),
        name="stack",
    )(keys, values)


def prepare_kernel(
    q_in, g_in, own_ref, near_ref, bias_ref,
    q_ref, g_ref, g_flip, keys_flip, exponent_ref, prob_grad_ref, mixed_ref, stats_ref,
):
    rows = own_ref.shape[0] // 2
    parts = range(PER_STEP)
    cols = [slice(i * HEAD, (i + 1) * HEAD) for i in parts]
    sides = (own_ref, near_ref)
    keys, values = [
        [jnp.concatenate([ref[span, cols[i]] for ref in sides], axis=0) for i in parts]
        for span in (slice(0, rows), slice(rows, 2 * rows))
    ]
    scores = [dot(keys[i], q_in[:, cols[i]], 1, 1) + bias_ref[...] for i in parts]
    tops = [jnp.max(x, axis=0, keepdims=True) for x in scores]
    exact = [jnp.exp2((x - top) * (FACTOR * LOG2E)) for x, top in zip(scores, tops)]
    exponents = [x.astype(jnp.bfloat16) for x in exact]
    for i in parts:
        stats_ref[i, 0:1] = tops[i]
        stats_ref[i, 1:2] = jnp.sum(exact[i], axis=0, keepdims=True)
        exponent_ref[i] = exponents[i]
        prob_grad_ref[i] = dot(values[i], g_in[:, cols[i]], 1, 1)
        mixed_ref[cols[i], :] = dot(values[i].T, exponents[i], 1, 0)
        keys_flip[cols[i], :] = keys[i].T
        g_flip[cols[i], :] = g_in[:, cols[i]].T
    q_ref[...] = q_in[...]
    g_ref[...] = g_in[...]


def prepare_call(q, g, own, near, bias):
    video_rows, width = q.shape
    local_rows = bias.shape[0]
    deep = pl.BlockSpec((WIDE, video_rows), lambda i: (i, 0))
    deep_shape = (width, video_rows)
    pairs = pl.BlockSpec((PER_STEP, local_rows, video_rows), lambda i: (i, 0, 0))
    pair_shape = (HEADS, local_rows, video_rows)
    outs = [
        (block(video_rows), q.shape, jnp.bfloat16),
        (block(video_rows), g.shape, jnp.bfloat16),
        (deep, deep_shape, jnp.bfloat16),
        (deep, deep_shape, jnp.bfloat16),
        (pairs, pair_shape, jnp.bfloat16),
        (pairs, pair_shape, jnp.float32),
        (deep, deep_shape, jnp.float32),
        (pl.BlockSpec((PER_STEP, 8, video_rows), lambda i: (i, 0, 0)), (HEADS, 8, video_rows), jnp.float32),
    ]
    return pl.pallas_call(
        prepare_kernel,
        grid=(STEPS,),
        in_specs=[block(video_rows)] * 4 + [whole(bias.shape)],
        out_specs=[spec for spec, _, _ in outs],
        out_shape=[jax.ShapeDtypeStruct(shape, dtype) for _, shape, dtype in outs],
        compiler_params=pltpu.CompilerParams(vmem_limit_bytes=PREPARE_LIMIT),
        cost_estimate=pl.CostEstimate(
            flops=6 * bias.size * width, bytes_accessed=9_000_000, transcendentals=bias.size * HEADS
        ),
        name="prepare",
    )(q, g, own, near, bias)


def heads_kernel(
    q_ref, g_ref, far_ref, g_flip, near_keys_flip, near_exponent, near_prob_grad, near_mixed, stats,
    null_ref, null_flip, bias_ref, valid_ref,
    out_ref, dq_ref, far_grad_ref, own_grad_ref, near_grad_ref, null_grad_ref, null_sum,
):
    step = pl.program_id(0)
    rows = far_ref.shape[0] // 2
    parts = range(PER_STEP)
    cols = [slice(i * HEAD, (i + 1) * HEAD) for i in parts]
    spans = (slice(0, rows), slice(rows, 2 * rows))
    keys, values = [
        [jnp.concatenate([far_ref[span, cols[i]], null_ref[i, index]], axis=0) for i in parts]
        for index, span in enumerate(spans)
    ]
    keys_flip, values_flip = [
        [jnp.concatenate([far_ref[span, cols[i]].T, null_flip[i, index]], axis=1) for i in parts]
        for index, span in enumerate(spans)
    ]
    scale = FACTOR * LOG2E
    scores = [dot(keys[i], q_ref[:, cols[i]], 1, 1) + bias_ref[...] for i in parts]
    tops = [
        jnp.maximum(jnp.max(x, axis=0, keepdims=True), stats[i, 0:1]) for i, x in enumerate(scores)
    ]
    exact = [jnp.exp2((x - top) * scale) for x, top in zip(scores, tops)]
    joins = [jnp.exp2((stats[i, 0:1] - tops[i]) * scale) for i in parts]
    totals = [
        jnp.sum(x, axis=0, keepdims=True) + joins[i] * stats[i, 1:2] for i, x in enumerate(exact)
    ]
    shares = [valid_ref[...] / total for total in totals]
    near_shares = [share * join for share, join in zip(shares, joins)]
    exponents = [x.astype(jnp.bfloat16) for x in exact]
    flips = [g_flip[cols[i], :].astype(jnp.float32) for i in parts]
    mixed = [
        dot(values_flip[i], exponents[i], 1, 0) * shares[i] + near_mixed[cols[i], :] * near_shares[i]
        for i in parts
    ]
    deltas = [jnp.sum(x * flip, axis=0, keepdims=True) for x, flip in zip(mixed, flips)]
    prob_grads = [dot(values[i], g_ref[:, cols[i]], 1, 1) for i in parts]
    score_grads = [
        ((prob_grads[i] - deltas[i]) * (shares[i] * FACTOR)).astype(jnp.bfloat16) * exponents[i]
        for i in parts
    ]
    near_score_grads = [
        ((near_prob_grad[i] - deltas[i]) * (near_shares[i] * FACTOR)).astype(jnp.bfloat16)
        * near_exponent[i]
        for i in parts
    ]
    for i in parts:
        out_ref[:, cols[i]] = mixed[i].astype(jnp.bfloat16).T
        query_grad = dot(keys_flip[i], score_grads[i], 1, 0)
        query_grad = query_grad + dot(near_keys_flip[cols[i], :], near_score_grads[i], 1, 0)
        dq_ref[:, cols[i]] = query_grad.astype(jnp.bfloat16).T
        q = q_ref[:, cols[i]]
        terms = (
            (dot(score_grads[i], q, 1, 0), dot(near_score_grads[i], q, 1, 0)),
            (
                dot(exponents[i], (flips[i] * shares[i]).astype(jnp.bfloat16), 1, 1),
                dot(near_exponent[i], (flips[i] * near_shares[i]).astype(jnp.bfloat16), 1, 1),
            ),
        )
        for index, (term, near_term) in enumerate(terms):
            far_grad_ref[index, :, cols[i]] = term[:rows].astype(jnp.bfloat16)
            own_grad_ref[index, :, cols[i]] = near_term[:rows].astype(jnp.bfloat16)
            near_grad_ref[index, :, cols[i]] = near_term[rows:].astype(jnp.bfloat16)
            null_sum[pl.ds(index * HEADS + step * PER_STEP + i, 1), :] = term[rows : rows + 1]

    @pl.when(step == STEPS - 1)
    def _():
        null_grad_ref[...] = jnp.broadcast_to(
            null_sum[...].astype(jnp.bfloat16)[None], null_grad_ref.shape
        )


def block(*lead):
    return pl.BlockSpec((*lead, WIDE), lambda i: (0,) * len(lead) + (i,))


def whole(shape):
    return pl.BlockSpec(shape, lambda i: (0,) * len(shape))


def heads_call(q, g, far, near_parts, null_rows, null_flip, bias, valid, peers):
    video_rows, width = q.shape
    audio_rows = video_rows // 2
    wide = jax.ShapeDtypeStruct((video_rows, width), jnp.bfloat16)
    terms = [jax.ShapeDtypeStruct((2, audio_rows, width), jnp.bfloat16)] * 3
    null_shape = (peers, 2 * HEADS, HEAD)
    deep = pl.BlockSpec((WIDE, video_rows), lambda i: (i, 0))
    pairs = pl.BlockSpec((PER_STEP, 2 * audio_rows, video_rows), lambda i: (i, 0, 0))
    return pl.pallas_call(
        heads_kernel,
        grid=(STEPS,),
        in_specs=[block(video_rows)] * 3
        + [deep, deep, pairs, pairs, deep]
        + [
            pl.BlockSpec((PER_STEP, 8, video_rows), lambda i: (i, 0, 0)),
            pl.BlockSpec((PER_STEP, *null_rows.shape[1:]), lambda i: (i, 0, 0, 0)),
            pl.BlockSpec((PER_STEP, *null_flip.shape[1:]), lambda i: (i, 0, 0, 0)),
            whole(bias.shape),
            whole(valid.shape),
        ],
        out_specs=[block(video_rows)] * 2 + [block(2, audio_rows)] * 3 + [whole(null_shape)],
        out_shape=[wide, wide, *terms, jax.ShapeDtypeStruct(null_shape, jnp.bfloat16)],
        scratch_shapes=[pltpu.VMEM((2 * HEADS, HEAD), jnp.float32)],
        compiler_params=pltpu.CompilerParams(vmem_limit_bytes=HEADS_LIMIT),
        cost_estimate=pl.CostEstimate(
            flops=12 * bias.size * width, bytes_accessed=9_000_000, transcendentals=bias.size * HEADS
        ),
        name="heads",
    )(q, g, far, *near_parts, null_rows, null_flip, bias, valid)


def add_kernel(a_ref, b_ref, *out_refs):
    total = a_ref[...].astype(jnp.float32) + b_ref[...].astype(jnp.float32)
    if len(out_refs) == 1:
        out_refs[0][...] = total.astype(jnp.bfloat16)
    else:
        for i, ref in enumerate(out_refs):
            ref[...] = total[i].astype(jnp.bfloat16)


def add_call(a, b, split, work, name):
    _, rows, width = a.shape
    steps = 3
    both = pl.BlockSpec((2, rows, width // steps), lambda i: (0, 0, i))
    one = pl.BlockSpec((rows, width // steps), lambda i: (0, i))
    single = jax.ShapeDtypeStruct((rows, width), jnp.bfloat16)
    return pl.pallas_call(
        add_kernel,
        grid=(steps,),
        in_specs=[both, both],
        out_specs=[one, one] if split else both,
        out_shape=[single, single] if split else jax.ShapeDtypeStruct(a.shape, jnp.bfloat16),
        compiler_params=pltpu.CompilerParams(vmem_limit_bytes=ADD_LIMIT),
        cost_estimate=pl.CostEstimate(flops=a.size, bytes_accessed=work, transcendentals=0),
        name=name,
    )(a, b)


def sum_peers(parts):
    return jnp.sum(parts.astype(jnp.float32), axis=0)


def body(video_query, audio_key, audio_value, null_kv, audio_keep, clip_lengths, out_grad):
    audio_rows = audio_key.shape[0]
    video_rows = video_query.shape[0]
    shards = lax.axis_size(SEQ)
    seq_index = lax.axis_index(SEQ)
    total_audio = audio_rows * shards

    stacked = stack_call(audio_key, audio_value)
    far = swap_link(stacked)

    bounds = jnp.cumsum(clip_lengths[0])
    pad_segment = clip_lengths.shape[1] - 1
    query_pos = seq_index * video_rows + jnp.arange(video_rows, dtype=jnp.int32)
    side = 1 - 2 * (seq_index % 2)
    starts = [(seq_index + move) * audio_rows for move in (-side, 0, side)]
    own_pos = jnp.arange(audio_rows, dtype=jnp.int32)
    key_pos = jnp.concatenate([start + own_pos for start in starts])
    keep_padded = jnp.pad(audio_keep, (audio_rows, audio_rows))
    keep_rows = jnp.concatenate(
        [lax.dynamic_slice_in_dim(keep_padded, start + audio_rows, audio_rows) for start in starts]
    )
    allowed = allowed_pairs(
        query_pos, key_pos, bounds, keep_rows, total_audio, pad_segment, audio_rows
    )
    near_bias = jnp.where(allowed[audio_rows:], 0.0, MASKED).astype(jnp.float32)
    null_allowed = jnp.broadcast_to(jnp.arange(NULL_ROWS)[:, None] == 0, (NULL_ROWS, video_rows))
    far_allowed = jnp.concatenate([allowed[:audio_rows], null_allowed])
    bias = jnp.where(far_allowed, 0.0, MASKED).astype(jnp.float32)
    valid = (segment_of(query_pos // 2, bounds) < pad_segment).astype(jnp.float32)[None]
    null_heads = null_kv.reshape(2, HEADS, HEAD).swapaxes(0, 1)
    first_only = jnp.arange(NULL_ROWS) == 0
    null_rows = jnp.where(first_only[:, None], null_heads[:, :, None], jnp.bfloat16(0))
    null_flip = jnp.where(first_only, null_heads[..., None], jnp.bfloat16(0))

    stacked, valid = lax.optimization_barrier((stacked, valid))
    near = swap_chip(stacked)

    wide_axes, deep_axes = ("yh", "yl", "x"), ("z", "core")
    q_held, g_held, *near_parts = prepare_call(video_query, out_grad, stacked, near, near_bias)
    attended, query_grad, far_grad, own_grad, near_grad, null_copies = heads_call(
        q_held, g_held, far, near_parts, null_rows, null_flip, bias, valid, lax.axis_size(wide_axes)
    )
    far_back = swap_link(far_grad)
    first = lax.all_to_all(null_copies, wide_axes, 0, 0)
    partial = sum_peers(first).astype(jnp.bfloat16)
    copies = jnp.broadcast_to(partial[None], (lax.axis_size(deep_axes), *partial.shape))
    copies, near_grad = lax.optimization_barrier((copies, near_grad))
    near_back = swap_chip(near_grad)
    second = lax.all_to_all(copies, deep_axes, 0, 0)
    part = add_call(own_grad, far_back, False, 4_000_000, "add_far")
    grads = add_call(part, near_back, True, 2_400_000, "add_near")
    second, *grads = lax.optimization_barrier((second, *grads))
    null_grad = sum_peers(second).reshape(null_kv.shape)
    return (attended, query_grad, grads[0], grads[1], null_grad)


def solution(mesh):
    parts = CLIP_PARTS + SEQ_PARTS
    fine = Mesh(
        np.asarray(mesh.devices).reshape([size for _, size in parts]), [name for name, _ in parts]
    )
    rows = P(CLIP + SEQ, None)
    return jax.shard_map(
        body,
        mesh=fine,
        in_specs=(rows, rows, rows, P(), P(CLIP), P(CLIP, None), rows),
        out_specs=(rows, rows, rows, rows, P()),
        check_vma=False,
    )
```

```python
import numpy as np

import jax
import jax.numpy as jnp
from jax import lax
from jax.experimental import pallas as pl
from jax.experimental.pallas import tpu as pltpu
from jax.sharding import Mesh
from jax.sharding import PartitionSpec as P

HEADS = 12
HEAD = 128
NULL_ROWS = 16
MASKED = -1e30
FACTOR = HEAD**-0.5
LOG2E = 1.4426950408889634
CLIP_PARTS = (("yh", 2), ("z", 8))
SEQ_PARTS = (("yl", 4), ("x", 4), ("core", 2))
CLIP = tuple(name for name, _ in CLIP_PARTS)
SEQ = tuple(name for name, _ in SEQ_PARTS)
HEADS_LIMIT = 36 * 1024 * 1024
PREPARE_LIMIT = 24 * 1024 * 1024
ADD_LIMIT = 8 * 1024 * 1024
PER_STEP = 6
STEPS = HEADS // PER_STEP
WIDE = PER_STEP * HEAD


def swap_chip(block):
    count = lax.axis_size(SEQ)
    return lax.ppermute(block, SEQ, [(i, i ^ 1) for i in range(count)])


def swap_link(block):
    last = lax.axis_size(SEQ) - 1
    pairs = [(i, i + 1) for i in range(1, last, 2)]
    return lax.ppermute(block, SEQ, pairs + [(b, a) for a, b in pairs])


def segment_of(positions, bounds):
    return jnp.sum((positions[:, None] >= bounds[None, :-1]).astype(jnp.int32), axis=1)


def allowed_pairs(query_pos, key_pos, bounds, keep_rows, total_audio, pad_segment, window):
    key_clip = jnp.clip(key_pos, 0, total_audio - 1)
    key_seg = segment_of(key_clip, bounds)
    query_seg = segment_of(query_pos // 2, bounds)
    key_inside = (
        (key_pos >= 0) & (key_pos < total_audio) & (keep_rows == 1) & (key_seg < pad_segment)
    )
    nearby = jnp.abs(query_pos[None, :] - 2 * key_pos[:, None]) <= 2 * window
    return key_inside[:, None] & (key_seg[:, None] == query_seg[None, :]) & nearby


def dot(a, b, lhs_dim, rhs_dim):
    return lax.dot_general(
        a, b, (((lhs_dim,), (rhs_dim,)), ((), ())), preferred_element_type=jnp.float32
    )


def prepare_kernel(
    q_in, g_in, own_ref, near_ref, bias_ref,
    q_ref, g_ref, g_flip, keys_flip, exponent_ref, prob_grad_ref, mixed_ref, stats_ref,
):
    rows = own_ref.shape[0] // 2
    parts = range(PER_STEP)
    cols = [slice(i * HEAD, (i + 1) * HEAD) for i in parts]
    sides = (own_ref, near_ref)
    keys, values = [
        [jnp.concatenate([ref[span, cols[i]] for ref in sides], axis=0) for i in parts]
        for span in (slice(0, rows), slice(rows, 2 * rows))
    ]
    scores = [dot(keys[i], q_in[:, cols[i]], 1, 1) + bias_ref[...] for i in parts]
    tops = [jnp.max(x, axis=0, keepdims=True) for x in scores]
    exact = [jnp.exp2((x - top) * (FACTOR * LOG2E)) for x, top in zip(scores, tops)]
    exponents = [x.astype(jnp.bfloat16) for x in exact]
    for i in parts:
        stats_ref[i, 0:1] = tops[i]
        stats_ref[i, 1:2] = jnp.sum(exact[i], axis=0, keepdims=True)
        exponent_ref[i] = exponents[i]
        prob_grad_ref[i] = dot(values[i], g_in[:, cols[i]], 1, 1)
        mixed_ref[cols[i], :] = dot(values[i].T, exponents[i], 1, 0)
        keys_flip[cols[i], :] = keys[i].T
        g_flip[cols[i], :] = g_in[:, cols[i]].T
    q_ref[...] = q_in[...]
    g_ref[...] = g_in[...]


def prepare_call(q, g, own, near, bias):
    video_rows, width = q.shape
    local_rows = bias.shape[0]
    deep = pl.BlockSpec((WIDE, video_rows), lambda i: (i, 0))
    deep_shape = (width, video_rows)
    pairs = pl.BlockSpec((PER_STEP, local_rows, video_rows), lambda i: (i, 0, 0))
    pair_shape = (HEADS, local_rows, video_rows)
    outs = [
        (block(video_rows), q.shape, jnp.bfloat16),
        (block(video_rows), g.shape, jnp.bfloat16),
        (deep, deep_shape, jnp.bfloat16),
        (deep, deep_shape, jnp.bfloat16),
        (pairs, pair_shape, jnp.bfloat16),
        (pairs, pair_shape, jnp.float32),
        (deep, deep_shape, jnp.float32),
        (pl.BlockSpec((PER_STEP, 8, video_rows), lambda i: (i, 0, 0)), (HEADS, 8, video_rows), jnp.float32),
    ]
    return pl.pallas_call(
        prepare_kernel,
        grid=(STEPS,),
        in_specs=[block(video_rows)] * 4 + [whole(bias.shape)],
        out_specs=[spec for spec, _, _ in outs],
        out_shape=[jax.ShapeDtypeStruct(shape, dtype) for _, shape, dtype in outs],
        compiler_params=pltpu.CompilerParams(vmem_limit_bytes=PREPARE_LIMIT),
        cost_estimate=pl.CostEstimate(
            flops=6 * bias.size * width, bytes_accessed=9_000_000, transcendentals=bias.size * HEADS
        ),
        name="prepare",
    )(q, g, own, near, bias)


def heads_kernel(
    q_ref, g_ref, far_ref, g_flip, near_keys_flip, near_exponent, near_prob_grad, near_mixed, stats,
    null_ref, null_flip, bias_ref, valid_ref,
    out_ref, dq_ref, far_grad_ref, own_grad_ref, near_grad_ref, null_grad_ref, null_sum,
):
    step = pl.program_id(0)
    rows = far_ref.shape[0] // 2
    parts = range(PER_STEP)
    cols = [slice(i * HEAD, (i + 1) * HEAD) for i in parts]
    spans = (slice(0, rows), slice(rows, 2 * rows))
    keys, values = [
        [jnp.concatenate([far_ref[span, cols[i]], null_ref[i, index]], axis=0) for i in parts]
        for index, span in enumerate(spans)
    ]
    keys_flip, values_flip = [
        [jnp.concatenate([far_ref[span, cols[i]].T, null_flip[i, index]], axis=1) for i in parts]
        for index, span in enumerate(spans)
    ]
    scale = FACTOR * LOG2E
    scores = [dot(keys[i], q_ref[:, cols[i]], 1, 1) + bias_ref[...] for i in parts]
    tops = [
        jnp.maximum(jnp.max(x, axis=0, keepdims=True), stats[i, 0:1]) for i, x in enumerate(scores)
    ]
    exact = [jnp.exp2((x - top) * scale) for x, top in zip(scores, tops)]
    joins = [jnp.exp2((stats[i, 0:1] - tops[i]) * scale) for i in parts]
    totals = [
        jnp.sum(x, axis=0, keepdims=True) + joins[i] * stats[i, 1:2] for i, x in enumerate(exact)
    ]
    shares = [valid_ref[...] / total for total in totals]
    near_shares = [share * join for share, join in zip(shares, joins)]
    exponents = [x.astype(jnp.bfloat16) for x in exact]
    flips = [g_flip[cols[i], :].astype(jnp.float32) for i in parts]
    mixed = [
        dot(values_flip[i], exponents[i], 1, 0) * shares[i] + near_mixed[cols[i], :] * near_shares[i]
        for i in parts
    ]
    deltas = [jnp.sum(x * flip, axis=0, keepdims=True) for x, flip in zip(mixed, flips)]
    prob_grads = [dot(values[i], g_ref[:, cols[i]], 1, 1) for i in parts]
    score_grads = [
        ((prob_grads[i] - deltas[i]) * (shares[i] * FACTOR)).astype(jnp.bfloat16) * exponents[i]
        for i in parts
    ]
    near_score_grads = [
        ((near_prob_grad[i] - deltas[i]) * (near_shares[i] * FACTOR)).astype(jnp.bfloat16)
        * near_exponent[i]
        for i in parts
    ]
    for i in parts:
        out_ref[:, cols[i]] = mixed[i].astype(jnp.bfloat16).T
        query_grad = dot(keys_flip[i], score_grads[i], 1, 0)
        query_grad = query_grad + dot(near_keys_flip[cols[i], :], near_score_grads[i], 1, 0)
        dq_ref[:, cols[i]] = query_grad.astype(jnp.bfloat16).T
        q = q_ref[:, cols[i]]
        terms = (
            (dot(score_grads[i], q, 1, 0), dot(near_score_grads[i], q, 1, 0)),
            (
                dot(exponents[i], (flips[i] * shares[i]).astype(jnp.bfloat16), 1, 1),
                dot(near_exponent[i], (flips[i] * near_shares[i]).astype(jnp.bfloat16), 1, 1),
            ),
        )
        for index, (term, near_term) in enumerate(terms):
            far_grad_ref[index, :, cols[i]] = term[:rows].astype(jnp.bfloat16)
            own_grad_ref[index, :, cols[i]] = near_term[:rows].astype(jnp.bfloat16)
            near_grad_ref[index, :, cols[i]] = near_term[rows:].astype(jnp.bfloat16)
            null_sum[pl.ds(index * HEADS + step * PER_STEP + i, 1), :] = term[rows : rows + 1]

    @pl.when(step == STEPS - 1)
    def _():
        null_grad_ref[...] = jnp.broadcast_to(
            null_sum[...].astype(jnp.bfloat16)[None], null_grad_ref.shape
        )


def block(*lead):
    return pl.BlockSpec((*lead, WIDE), lambda i: (0,) * len(lead) + (i,))


def whole(shape):
    return pl.BlockSpec(shape, lambda i: (0,) * len(shape))


def heads_call(q, g, far, near_parts, null_rows, null_flip, bias, valid, peers):
    video_rows, width = q.shape
    audio_rows = video_rows // 2
    wide = jax.ShapeDtypeStruct((video_rows, width), jnp.bfloat16)
    terms = [jax.ShapeDtypeStruct((2, audio_rows, width), jnp.bfloat16)] * 3
    null_shape = (peers, 2 * HEADS, HEAD)
    deep = pl.BlockSpec((WIDE, video_rows), lambda i: (i, 0))
    pairs = pl.BlockSpec((PER_STEP, 2 * audio_rows, video_rows), lambda i: (i, 0, 0))
    return pl.pallas_call(
        heads_kernel,
        grid=(STEPS,),
        in_specs=[block(video_rows)] * 3
        + [deep, deep, pairs, pairs, deep]
        + [
            pl.BlockSpec((PER_STEP, 8, video_rows), lambda i: (i, 0, 0)),
            pl.BlockSpec((PER_STEP, *null_rows.shape[1:]), lambda i: (i, 0, 0, 0)),
            pl.BlockSpec((PER_STEP, *null_flip.shape[1:]), lambda i: (i, 0, 0, 0)),
            whole(bias.shape),
            whole(valid.shape),
        ],
        out_specs=[block(video_rows)] * 2 + [block(2, audio_rows)] * 3 + [whole(null_shape)],
        out_shape=[wide, wide, *terms, jax.ShapeDtypeStruct(null_shape, jnp.bfloat16)],
        scratch_shapes=[pltpu.VMEM((2 * HEADS, HEAD), jnp.float32)],
        compiler_params=pltpu.CompilerParams(vmem_limit_bytes=HEADS_LIMIT),
        cost_estimate=pl.CostEstimate(
            flops=12 * bias.size * width, bytes_accessed=9_000_000, transcendentals=bias.size * HEADS
        ),
        name="heads",
    )(q, g, far, *near_parts, null_rows, null_flip, bias, valid)


def add_kernel(a_ref, b_ref, *out_refs):
    total = a_ref[...].astype(jnp.float32) + b_ref[...].astype(jnp.float32)
    if len(out_refs) == 1:
        out_refs[0][...] = total.astype(jnp.bfloat16)
    else:
        for i, ref in enumerate(out_refs):
            ref[...] = total[i].astype(jnp.bfloat16)


def add_call(a, b, split, work, name):
    _, rows, width = a.shape
    steps = 3
    both = pl.BlockSpec((2, rows, width // steps), lambda i: (0, 0, i))
    one = pl.BlockSpec((rows, width // steps), lambda i: (0, i))
    single = jax.ShapeDtypeStruct((rows, width), jnp.bfloat16)
    return pl.pallas_call(
        add_kernel,
        grid=(steps,),
        in_specs=[both, both],
        out_specs=[one, one] if split else both,
        out_shape=[single, single] if split else jax.ShapeDtypeStruct(a.shape, jnp.bfloat16),
        compiler_params=pltpu.CompilerParams(vmem_limit_bytes=ADD_LIMIT),
        cost_estimate=pl.CostEstimate(flops=a.size, bytes_accessed=work, transcendentals=0),
        name=name,
    )(a, b)


def sum_peers(parts):
    return jnp.sum(parts.astype(jnp.float32), axis=0)


def body(video_query, audio_key, audio_value, null_kv, audio_keep, clip_lengths, out_grad):
    audio_rows = audio_key.shape[0]
    video_rows = video_query.shape[0]
    shards = lax.axis_size(SEQ)
    seq_index = lax.axis_index(SEQ)
    total_audio = audio_rows * shards

    stacked = jnp.stack([audio_key, audio_value]).reshape(2 * audio_rows, -1)
    far = swap_link(stacked)

    bounds = jnp.cumsum(clip_lengths[0])
    pad_segment = clip_lengths.shape[1] - 1
    query_pos = seq_index * video_rows + jnp.arange(video_rows, dtype=jnp.int32)
    side = 1 - 2 * (seq_index % 2)
    starts = [(seq_index + move) * audio_rows for move in (-side, 0, side)]
    own_pos = jnp.arange(audio_rows, dtype=jnp.int32)
    key_pos = jnp.concatenate([start + own_pos for start in starts])
    keep_padded = jnp.pad(audio_keep, (audio_rows, audio_rows))
    keep_rows = jnp.concatenate(
        [lax.dynamic_slice_in_dim(keep_padded, start + audio_rows, audio_rows) for start in starts]
    )
    allowed = allowed_pairs(
        query_pos, key_pos, bounds, keep_rows, total_audio, pad_segment, audio_rows
    )
    near_bias = jnp.where(allowed[audio_rows:], 0.0, MASKED).astype(jnp.float32)
    null_allowed = jnp.broadcast_to(jnp.arange(NULL_ROWS)[:, None] == 0, (NULL_ROWS, video_rows))
    far_allowed = jnp.concatenate([allowed[:audio_rows], null_allowed])
    bias = jnp.where(far_allowed, 0.0, MASKED).astype(jnp.float32)
    valid = (segment_of(query_pos // 2, bounds) < pad_segment).astype(jnp.float32)[None]
    null_heads = null_kv.reshape(2, HEADS, HEAD).swapaxes(0, 1)
    first_only = jnp.arange(NULL_ROWS) == 0
    null_rows = jnp.where(first_only[:, None], null_heads[:, :, None], jnp.bfloat16(0))
    null_flip = jnp.where(first_only, null_heads[..., None], jnp.bfloat16(0))

    stacked, valid = lax.optimization_barrier((stacked, valid))
    near = swap_chip(stacked)

    wide_axes, deep_axes = ("yh", "yl", "x"), ("z", "core")
    q_held, g_held, *near_parts = prepare_call(video_query, out_grad, stacked, near, near_bias)
    attended, query_grad, far_grad, own_grad, near_grad, null_copies = heads_call(
        q_held, g_held, far, near_parts, null_rows, null_flip, bias, valid, lax.axis_size(wide_axes)
    )
    far_back = swap_link(far_grad)
    first = lax.all_to_all(null_copies, wide_axes, 0, 0)
    partial = sum_peers(first).astype(jnp.bfloat16)
    copies = jnp.broadcast_to(partial[None], (lax.axis_size(deep_axes), *partial.shape))
    copies, near_grad = lax.optimization_barrier((copies, near_grad))
    near_back = swap_chip(near_grad)
    second = lax.all_to_all(copies, deep_axes, 0, 0)
    part = add_call(own_grad, far_back, False, 4_000_000, "add_far")
    grads = add_call(part, near_back, True, 2_400_000, "add_near")
    second, *grads = lax.optimization_barrier((second, *grads))
    null_grad = sum_peers(second).reshape(null_kv.shape)
    return (attended, query_grad, grads[0], grads[1], null_grad)


def solution(mesh):
    parts = CLIP_PARTS + SEQ_PARTS
    fine = Mesh(
        np.asarray(mesh.devices).reshape([size for _, size in parts]), [name for name, _ in parts]
    )
    rows = P(CLIP + SEQ, None)
    return jax.shard_map(
        body,
        mesh=fine,
        in_specs=(rows, rows, rows, P(), P(CLIP), P(CLIP, None), rows),
        out_specs=(rows, rows, rows, rows, P()),
        check_vma=False,
    )
```

```python
import numpy as np

import jax
import jax.numpy as jnp
from jax import lax
from jax.experimental import pallas as pl
from jax.experimental.pallas import tpu as pltpu
from jax.sharding import Mesh
from jax.sharding import PartitionSpec as P

HEADS = 12
HEAD = 128
NULL_ROWS = 16
MASKED = -1e30
FACTOR = HEAD**-0.5
LOG2E = 1.4426950408889634
CLIP_PARTS = (("yh", 2), ("z", 8))
SEQ_PARTS = (("yl", 4), ("x", 4), ("core", 2))
CLIP = tuple(name for name, _ in CLIP_PARTS)
SEQ = tuple(name for name, _ in SEQ_PARTS)
HEADS_LIMIT = 36 * 1024 * 1024
PREPARE_LIMIT = 24 * 1024 * 1024
ADD_LIMIT = 8 * 1024 * 1024
PER_STEP = 6
STEPS = HEADS // PER_STEP
WIDE = PER_STEP * HEAD


def swap_chip(block):
    count = lax.axis_size(SEQ)
    return lax.ppermute(block, SEQ, [(i, i ^ 1) for i in range(count)])


def swap_link(block):
    last = lax.axis_size(SEQ) - 1
    pairs = [(i, i + 1) for i in range(1, last, 2)]
    return lax.ppermute(block, SEQ, pairs + [(b, a) for a, b in pairs])


def segment_of(positions, bounds):
    return jnp.sum((positions[:, None] >= bounds[None, :-1]).astype(jnp.int32), axis=1)


def allowed_pairs(query_pos, key_pos, bounds, keep_rows, total_audio, pad_segment, window):
    key_clip = jnp.clip(key_pos, 0, total_audio - 1)
    key_seg = segment_of(key_clip, bounds)
    query_seg = segment_of(query_pos // 2, bounds)
    key_inside = (
        (key_pos >= 0) & (key_pos < total_audio) & (keep_rows == 1) & (key_seg < pad_segment)
    )
    nearby = jnp.abs(query_pos[None, :] - 2 * key_pos[:, None]) <= 2 * window
    return key_inside[:, None] & (key_seg[:, None] == query_seg[None, :]) & nearby


def dot(a, b, lhs_dim, rhs_dim):
    return lax.dot_general(
        a, b, (((lhs_dim,), (rhs_dim,)), ((), ())), preferred_element_type=jnp.float32
    )


def prepare_kernel(
    q_in, g_in, own_ref, near_ref, bias_ref,
    q_ref, g_ref, g_flip, keys_flip, exponent_ref, prob_grad_ref, mixed_ref, stats_ref,
):
    rows = own_ref.shape[0] // 2
    parts = range(PER_STEP)
    cols = [slice(i * HEAD, (i + 1) * HEAD) for i in parts]
    sides = (own_ref, near_ref)
    keys, values = [
        [jnp.concatenate([ref[span, cols[i]] for ref in sides], axis=0) for i in parts]
        for span in (slice(0, rows), slice(rows, 2 * rows))
    ]
    scores = [dot(keys[i], q_in[:, cols[i]], 1, 1) + bias_ref[...] for i in parts]
    tops = [jnp.max(x, axis=0, keepdims=True) for x in scores]
    exact = [jnp.exp2((x - top) * (FACTOR * LOG2E)) for x, top in zip(scores, tops)]
    exponents = [x.astype(jnp.bfloat16) for x in exact]
    for i in parts:
        stats_ref[i, 0:1] = tops[i]
        stats_ref[i, 1:2] = jnp.sum(exact[i], axis=0, keepdims=True)
        exponent_ref[i] = exponents[i]
        prob_grad_ref[i] = dot(values[i], g_in[:, cols[i]], 1, 1)
        mixed_ref[cols[i], :] = dot(values[i].T, exponents[i], 1, 0)
        keys_flip[cols[i], :] = keys[i].T
        g_flip[cols[i], :] = g_in[:, cols[i]].T
    q_ref[...] = q_in[...]
    g_ref[...] = g_in[...]


def prepare_call(q, g, own, near, bias):
    video_rows, width = q.shape
    local_rows = bias.shape[0]
    deep = pl.BlockSpec((WIDE, video_rows), lambda i: (i, 0))
    deep_shape = (width, video_rows)
    pairs = pl.BlockSpec((PER_STEP, local_rows, video_rows), lambda i: (i, 0, 0))
    pair_shape = (HEADS, local_rows, video_rows)
    outs = [
        (block(video_rows), q.shape, jnp.bfloat16),
        (block(video_rows), g.shape, jnp.bfloat16),
        (deep, deep_shape, jnp.bfloat16),
        (deep, deep_shape, jnp.bfloat16),
        (pairs, pair_shape, jnp.bfloat16),
        (pairs, pair_shape, jnp.float32),
        (deep, deep_shape, jnp.float32),
        (pl.BlockSpec((PER_STEP, 8, video_rows), lambda i: (i, 0, 0)), (HEADS, 8, video_rows), jnp.float32),
    ]
    return pl.pallas_call(
        prepare_kernel,
        grid=(STEPS,),
        in_specs=[block(video_rows)] * 4 + [whole(bias.shape)],
        out_specs=[spec for spec, _, _ in outs],
        out_shape=[jax.ShapeDtypeStruct(shape, dtype) for _, shape, dtype in outs],
        compiler_params=pltpu.CompilerParams(vmem_limit_bytes=PREPARE_LIMIT),
        cost_estimate=pl.CostEstimate(
            flops=6 * bias.size * width, bytes_accessed=9_000_000, transcendentals=bias.size * HEADS
        ),
        name="prepare",
    )(q, g, own, near, bias)


def heads_kernel(
    q_ref, g_ref, far_ref, g_flip, near_keys_flip, near_exponent, near_prob_grad, near_mixed, stats,
    null_ref, null_flip, bias_ref, valid_ref,
    out_ref, dq_ref, far_grad_ref, own_grad_ref, near_grad_ref, null_grad_ref, null_sum,
):
    step = pl.program_id(0)
    rows = far_ref.shape[0] // 2
    parts = range(PER_STEP)
    cols = [slice(i * HEAD, (i + 1) * HEAD) for i in parts]
    spans = (slice(0, rows), slice(rows, 2 * rows))
    keys, values = [
        [jnp.concatenate([far_ref[span, cols[i]], null_ref[i, index]], axis=0) for i in parts]
        for index, span in enumerate(spans)
    ]
    keys_flip, values_flip = [
        [jnp.concatenate([far_ref[span, cols[i]].T, null_flip[i, index]], axis=1) for i in parts]
        for index, span in enumerate(spans)
    ]
    scale = FACTOR * LOG2E
    scores = [dot(keys[i], q_ref[:, cols[i]], 1, 1) + bias_ref[...] for i in parts]
    tops = [
        jnp.maximum(jnp.max(x, axis=0, keepdims=True), stats[i, 0:1]) for i, x in enumerate(scores)
    ]
    exact = [jnp.exp2((x - top) * scale) for x, top in zip(scores, tops)]
    joins = [jnp.exp2((stats[i, 0:1] - tops[i]) * scale) for i in parts]
    totals = [
        jnp.sum(x, axis=0, keepdims=True) + joins[i] * stats[i, 1:2] for i, x in enumerate(exact)
    ]
    shares = [valid_ref[...] / total for total in totals]
    near_shares = [share * join for share, join in zip(shares, joins)]
    exponents = [x.astype(jnp.bfloat16) for x in exact]
    flips = [g_flip[cols[i], :].astype(jnp.float32) for i in parts]
    mixed = [
        dot(values_flip[i], exponents[i], 1, 0) * shares[i] + near_mixed[cols[i], :] * near_shares[i]
        for i in parts
    ]
    deltas = [jnp.sum(x * flip, axis=0, keepdims=True) for x, flip in zip(mixed, flips)]
    prob_grads = [dot(values[i], g_ref[:, cols[i]], 1, 1) for i in parts]
    score_grads = [
        ((prob_grads[i] - deltas[i]) * (shares[i] * FACTOR)).astype(jnp.bfloat16) * exponents[i]
        for i in parts
    ]
    near_score_grads = [
        ((near_prob_grad[i] - deltas[i]) * (near_shares[i] * FACTOR)).astype(jnp.bfloat16)
        * near_exponent[i]
        for i in parts
    ]
    for i in parts:
        out_ref[:, cols[i]] = mixed[i].astype(jnp.bfloat16).T
        query_grad = dot(keys_flip[i], score_grads[i], 1, 0)
        query_grad = query_grad + dot(near_keys_flip[cols[i], :], near_score_grads[i], 1, 0)
        dq_ref[:, cols[i]] = query_grad.astype(jnp.bfloat16).T
        both = jnp.concatenate([near_score_grads[i], score_grads[i]], axis=0)
        key_term = dot(both, q_ref[:, cols[i]], 1, 0)
        terms = (
            (key_term[2 * rows :], key_term[: 2 * rows]),
            (
                dot(exponents[i], (flips[i] * shares[i]).astype(jnp.bfloat16), 1, 1),
                dot(near_exponent[i], (flips[i] * near_shares[i]).astype(jnp.bfloat16), 1, 1),
            ),
        )
        for index, (term, near_term) in enumerate(terms):
            far_grad_ref[index, :, cols[i]] = term[:rows].astype(jnp.bfloat16)
            own_grad_ref[index, :, cols[i]] = near_term[:rows].astype(jnp.bfloat16)
            near_grad_ref[index, :, cols[i]] = near_term[rows:].astype(jnp.bfloat16)
            null_sum[pl.ds(index * HEADS + step * PER_STEP + i, 1), :] = term[rows : rows + 1]

    @pl.when(step == STEPS - 1)
    def _():
        null_grad_ref[...] = jnp.broadcast_to(
            null_sum[...].astype(jnp.bfloat16)[None], null_grad_ref.shape
        )


def block(*lead):
    return pl.BlockSpec((*lead, WIDE), lambda i: (0,) * len(lead) + (i,))


def whole(shape):
    return pl.BlockSpec(shape, lambda i: (0,) * len(shape))


def heads_call(q, g, far, near_parts, null_rows, null_flip, bias, valid, peers):
    video_rows, width = q.shape
    audio_rows = video_rows // 2
    wide = jax.ShapeDtypeStruct((video_rows, width), jnp.bfloat16)
    terms = [jax.ShapeDtypeStruct((2, audio_rows, width), jnp.bfloat16)] * 3
    null_shape = (peers, 2 * HEADS, HEAD)
    deep = pl.BlockSpec((WIDE, video_rows), lambda i: (i, 0))
    pairs = pl.BlockSpec((PER_STEP, 2 * audio_rows, video_rows), lambda i: (i, 0, 0))
    return pl.pallas_call(
        heads_kernel,
        grid=(STEPS,),
        in_specs=[block(video_rows)] * 3
        + [deep, deep, pairs, pairs, deep]
        + [
            pl.BlockSpec((PER_STEP, 8, video_rows), lambda i: (i, 0, 0)),
            pl.BlockSpec((PER_STEP, *null_rows.shape[1:]), lambda i: (i, 0, 0, 0)),
            pl.BlockSpec((PER_STEP, *null_flip.shape[1:]), lambda i: (i, 0, 0, 0)),
            whole(bias.shape),
            whole(valid.shape),
        ],
        out_specs=[block(video_rows)] * 2 + [block(2, audio_rows)] * 3 + [whole(null_shape)],
        out_shape=[wide, wide, *terms, jax.ShapeDtypeStruct(null_shape, jnp.bfloat16)],
        scratch_shapes=[pltpu.VMEM((2 * HEADS, HEAD), jnp.float32)],
        compiler_params=pltpu.CompilerParams(vmem_limit_bytes=HEADS_LIMIT),
        cost_estimate=pl.CostEstimate(
            flops=12 * bias.size * width, bytes_accessed=9_000_000, transcendentals=bias.size * HEADS
        ),
        name="heads",
    )(q, g, far, *near_parts, null_rows, null_flip, bias, valid)


def add_kernel(a_ref, b_ref, *out_refs):
    total = a_ref[...].astype(jnp.float32) + b_ref[...].astype(jnp.float32)
    if len(out_refs) == 1:
        out_refs[0][...] = total.astype(jnp.bfloat16)
    else:
        for i, ref in enumerate(out_refs):
            ref[...] = total[i].astype(jnp.bfloat16)


def add_call(a, b, split, work, name):
    _, rows, width = a.shape
    steps = 3
    both = pl.BlockSpec((2, rows, width // steps), lambda i: (0, 0, i))
    one = pl.BlockSpec((rows, width // steps), lambda i: (0, i))
    single = jax.ShapeDtypeStruct((rows, width), jnp.bfloat16)
    return pl.pallas_call(
        add_kernel,
        grid=(steps,),
        in_specs=[both, both],
        out_specs=[one, one] if split else both,
        out_shape=[single, single] if split else jax.ShapeDtypeStruct(a.shape, jnp.bfloat16),
        compiler_params=pltpu.CompilerParams(vmem_limit_bytes=ADD_LIMIT),
        cost_estimate=pl.CostEstimate(flops=a.size, bytes_accessed=work, transcendentals=0),
        name=name,
    )(a, b)


def sum_peers(parts):
    return jnp.sum(parts.astype(jnp.float32), axis=0)


def body(video_query, audio_key, audio_value, null_kv, audio_keep, clip_lengths, out_grad):
    audio_rows = audio_key.shape[0]
    video_rows = video_query.shape[0]
    shards = lax.axis_size(SEQ)
    seq_index = lax.axis_index(SEQ)
    total_audio = audio_rows * shards

    stacked = jnp.stack([audio_key, audio_value]).reshape(2 * audio_rows, -1)
    far = swap_link(stacked)

    bounds = jnp.cumsum(clip_lengths[0])
    pad_segment = clip_lengths.shape[1] - 1
    query_pos = seq_index * video_rows + jnp.arange(video_rows, dtype=jnp.int32)
    side = 1 - 2 * (seq_index % 2)
    starts = [(seq_index + move) * audio_rows for move in (-side, 0, side)]
    own_pos = jnp.arange(audio_rows, dtype=jnp.int32)
    key_pos = jnp.concatenate([start + own_pos for start in starts])
    keep_padded = jnp.pad(audio_keep, (audio_rows, audio_rows))
    keep_rows = jnp.concatenate(
        [lax.dynamic_slice_in_dim(keep_padded, start + audio_rows, audio_rows) for start in starts]
    )
    allowed = allowed_pairs(
        query_pos, key_pos, bounds, keep_rows, total_audio, pad_segment, audio_rows
    )
    near_bias = jnp.where(allowed[audio_rows:], 0.0, MASKED).astype(jnp.float32)
    null_allowed = jnp.broadcast_to(jnp.arange(NULL_ROWS)[:, None] == 0, (NULL_ROWS, video_rows))
    far_allowed = jnp.concatenate([allowed[:audio_rows], null_allowed])
    bias = jnp.where(far_allowed, 0.0, MASKED).astype(jnp.float32)
    valid = (segment_of(query_pos // 2, bounds) < pad_segment).astype(jnp.float32)[None]
    null_heads = null_kv.reshape(2, HEADS, HEAD).swapaxes(0, 1)
    first_only = jnp.arange(NULL_ROWS) == 0
    null_rows = jnp.where(first_only[:, None], null_heads[:, :, None], jnp.bfloat16(0))
    null_flip = jnp.where(first_only, null_heads[..., None], jnp.bfloat16(0))

    stacked, valid = lax.optimization_barrier((stacked, valid))
    near = swap_chip(stacked)

    wide_axes, deep_axes = ("yh", "yl", "x"), ("z", "core")
    q_held, g_held, *near_parts = prepare_call(video_query, out_grad, stacked, near, near_bias)
    attended, query_grad, far_grad, own_grad, near_grad, null_copies = heads_call(
        q_held, g_held, far, near_parts, null_rows, null_flip, bias, valid, lax.axis_size(wide_axes)
    )
    far_back = swap_link(far_grad)
    near_back = swap_chip(near_grad)
    first = lax.all_to_all(null_copies, wide_axes, 0, 0)
    partial = sum_peers(first).astype(jnp.bfloat16)
    copies = jnp.broadcast_to(partial[None], (lax.axis_size(deep_axes), *partial.shape))
    second = lax.all_to_all(copies, deep_axes, 0, 0)
    part = add_call(own_grad, far_back, False, 4_000_000, "add_far")
    grads = add_call(part, near_back, True, 2_400_000, "add_near")
    second, *grads = lax.optimization_barrier((second, *grads))
    null_grad = sum_peers(second).reshape(null_kv.shape)
    return (attended, query_grad, grads[0], grads[1], null_grad)


def solution(mesh):
    parts = CLIP_PARTS + SEQ_PARTS
    fine = Mesh(
        np.asarray(mesh.devices).reshape([size for _, size in parts]), [name for name, _ in parts]
    )
    rows = P(CLIP + SEQ, None)
    return jax.shard_map(
        body,
        mesh=fine,
        in_specs=(rows, rows, rows, P(), P(CLIP), P(CLIP, None), rows),
        out_specs=(rows, rows, rows, rows, P()),
        check_vma=False,
    )
```

```python
import numpy as np

import jax
import jax.numpy as jnp
from jax import lax
from jax.experimental import pallas as pl
from jax.experimental.pallas import tpu as pltpu
from jax.sharding import Mesh
from jax.sharding import PartitionSpec as P

HEADS = 12
HEAD = 128
NULL_ROWS = 16
MASKED = -1e30
FACTOR = HEAD**-0.5
LOG2E = 1.4426950408889634
CLIP_PARTS = (("yh", 2), ("z", 8))
SEQ_PARTS = (("yl", 4), ("x", 4), ("core", 2))
CLIP = tuple(name for name, _ in CLIP_PARTS)
SEQ = tuple(name for name, _ in SEQ_PARTS)
HEADS_LIMIT = 36 * 1024 * 1024
PREPARE_LIMIT = 24 * 1024 * 1024
ADD_LIMIT = 8 * 1024 * 1024
PER_STEP = 6
STEPS = HEADS // PER_STEP
WIDE = PER_STEP * HEAD


def swap_chip(block):
    count = lax.axis_size(SEQ)
    return lax.ppermute(block, SEQ, [(i, i ^ 1) for i in range(count)])


def swap_link(block):
    last = lax.axis_size(SEQ) - 1
    pairs = [(i, i + 1) for i in range(1, last, 2)]
    return lax.ppermute(block, SEQ, pairs + [(b, a) for a, b in pairs])


def segment_of(positions, bounds):
    return jnp.sum((positions[:, None] >= bounds[None, :-1]).astype(jnp.int32), axis=1)


def allowed_pairs(query_pos, key_pos, bounds, keep_rows, total_audio, pad_segment, window):
    key_clip = jnp.clip(key_pos, 0, total_audio - 1)
    key_seg = segment_of(key_clip, bounds)
    query_seg = segment_of(query_pos // 2, bounds)
    key_inside = (
        (key_pos >= 0) & (key_pos < total_audio) & (keep_rows == 1) & (key_seg < pad_segment)
    )
    nearby = jnp.abs(query_pos[None, :] - 2 * key_pos[:, None]) <= 2 * window
    return key_inside[:, None] & (key_seg[:, None] == query_seg[None, :]) & nearby


def dot(a, b, lhs_dim, rhs_dim):
    return lax.dot_general(
        a, b, (((lhs_dim,), (rhs_dim,)), ((), ())), preferred_element_type=jnp.float32
    )


def prepare_kernel(
    q_in, g_in, own_ref, near_ref, bias_ref,
    q_ref, g_ref, g_flip, keys_flip, exponent_ref, prob_grad_ref, mixed_ref, stats_ref,
):
    rows = own_ref.shape[0] // 2
    parts = range(PER_STEP)
    cols = [slice(i * HEAD, (i + 1) * HEAD) for i in parts]
    sides = (own_ref, near_ref)
    keys, values = [
        [jnp.concatenate([ref[span, cols[i]] for ref in sides], axis=0) for i in parts]
        for span in (slice(0, rows), slice(rows, 2 * rows))
    ]
    scores = [dot(keys[i], q_in[:, cols[i]], 1, 1) + bias_ref[...] for i in parts]
    tops = [jnp.max(x, axis=0, keepdims=True) for x in scores]
    exact = [jnp.exp2((x - top) * (FACTOR * LOG2E)) for x, top in zip(scores, tops)]
    exponents = [x.astype(jnp.bfloat16) for x in exact]
    for i in parts:
        stats_ref[i, 0:1] = tops[i]
        stats_ref[i, 1:2] = jnp.sum(exact[i], axis=0, keepdims=True)
        exponent_ref[i] = exponents[i]
        prob_grad_ref[i] = dot(values[i], g_in[:, cols[i]], 1, 1)
        mixed_ref[cols[i], :] = dot(values[i].T, exponents[i], 1, 0)
        keys_flip[cols[i], :] = keys[i].T
        g_flip[cols[i], :] = g_in[:, cols[i]].T
    q_ref[...] = q_in[...]
    g_ref[...] = g_in[...]


def prepare_call(q, g, own, near, bias):
    video_rows, width = q.shape
    local_rows = bias.shape[0]
    deep = pl.BlockSpec((WIDE, video_rows), lambda i: (i, 0))
    deep_shape = (width, video_rows)
    pairs = pl.BlockSpec((PER_STEP, local_rows, video_rows), lambda i: (i, 0, 0))
    pair_shape = (HEADS, local_rows, video_rows)
    outs = [
        (block(video_rows), q.shape, jnp.bfloat16),
        (block(video_rows), g.shape, jnp.bfloat16),
        (deep, deep_shape, jnp.bfloat16),
        (deep, deep_shape, jnp.bfloat16),
        (pairs, pair_shape, jnp.bfloat16),
        (pairs, pair_shape, jnp.float32),
        (deep, deep_shape, jnp.float32),
        (pl.BlockSpec((PER_STEP, 8, video_rows), lambda i: (i, 0, 0)), (HEADS, 8, video_rows), jnp.float32),
    ]
    return pl.pallas_call(
        prepare_kernel,
        grid=(STEPS,),
        in_specs=[block(video_rows)] * 4 + [whole(bias.shape)],
        out_specs=[spec for spec, _, _ in outs],
        out_shape=[jax.ShapeDtypeStruct(shape, dtype) for _, shape, dtype in outs],
        compiler_params=pltpu.CompilerParams(vmem_limit_bytes=PREPARE_LIMIT),
        cost_estimate=pl.CostEstimate(
            flops=6 * bias.size * width, bytes_accessed=9_000_000, transcendentals=bias.size * HEADS
        ),
        name="prepare",
    )(q, g, own, near, bias)


def heads_kernel(
    q_ref, g_ref, far_ref, g_flip, near_keys_flip, near_exponent, near_prob_grad, near_mixed, stats,
    null_ref, null_flip, bias_ref, valid_ref,
    out_ref, dq_ref, far_grad_ref, own_grad_ref, near_grad_ref, null_grad_ref, null_sum,
):
    step = pl.program_id(0)
    rows = far_ref.shape[0] // 2
    parts = range(PER_STEP)
    cols = [slice(i * HEAD, (i + 1) * HEAD) for i in parts]
    spans = (slice(0, rows), slice(rows, 2 * rows))
    keys, values = [
        [jnp.concatenate([far_ref[span, cols[i]], null_ref[i, index]], axis=0) for i in parts]
        for index, span in enumerate(spans)
    ]
    keys_flip, values_flip = [
        [jnp.concatenate([far_ref[span, cols[i]].T, null_flip[i, index]], axis=1) for i in parts]
        for index, span in enumerate(spans)
    ]
    scale = FACTOR * LOG2E
    scores = [dot(keys[i], q_ref[:, cols[i]], 1, 1) + bias_ref[...] for i in parts]
    tops = [
        jnp.maximum(jnp.max(x, axis=0, keepdims=True), stats[i, 0:1]) for i, x in enumerate(scores)
    ]
    exact = [jnp.exp2((x - top) * scale) for x, top in zip(scores, tops)]
    joins = [jnp.exp2((stats[i, 0:1] - tops[i]) * scale) for i in parts]
    totals = [
        jnp.sum(x, axis=0, keepdims=True) + joins[i] * stats[i, 1:2] for i, x in enumerate(exact)
    ]
    shares = [valid_ref[...] / total for total in totals]
    near_shares = [share * join for share, join in zip(shares, joins)]
    exponents = [x.astype(jnp.bfloat16) for x in exact]
    flips = [g_flip[cols[i], :].astype(jnp.float32) for i in parts]
    mixed = [
        dot(values_flip[i], exponents[i], 1, 0) * shares[i] + near_mixed[cols[i], :] * near_shares[i]
        for i in parts
    ]
    deltas = [jnp.sum(x * flip, axis=0, keepdims=True) for x, flip in zip(mixed, flips)]
    prob_grads = [dot(values[i], g_ref[:, cols[i]], 1, 1) for i in parts]
    score_grads = [
        ((prob_grads[i] - deltas[i]) * (shares[i] * FACTOR)).astype(jnp.bfloat16) * exponents[i]
        for i in parts
    ]
    near_score_grads = [
        ((near_prob_grad[i] - deltas[i]) * (near_shares[i] * FACTOR)).astype(jnp.bfloat16)
        * near_exponent[i]
        for i in parts
    ]
    for i in parts:
        out_ref[:, cols[i]] = mixed[i].astype(jnp.bfloat16).T
        query_grad = dot(keys_flip[i], score_grads[i], 1, 0)
        query_grad = query_grad + dot(near_keys_flip[cols[i], :], near_score_grads[i], 1, 0)
        dq_ref[:, cols[i]] = query_grad.astype(jnp.bfloat16).T
        q = q_ref[:, cols[i]]
        terms = (
            (dot(score_grads[i], q, 1, 0), dot(near_score_grads[i], q, 1, 0)),
            (
                dot(exponents[i], (flips[i] * shares[i]).astype(jnp.bfloat16), 1, 1),
                dot(near_exponent[i], (flips[i] * near_shares[i]).astype(jnp.bfloat16), 1, 1),
            ),
        )
        for index, (term, near_term) in enumerate(terms):
            far_grad_ref[index, :, cols[i]] = term[:rows].astype(jnp.bfloat16)
            own_grad_ref[index, :, cols[i]] = near_term[:rows].astype(jnp.bfloat16)
            near_grad_ref[index, :, cols[i]] = near_term[rows:].astype(jnp.bfloat16)
            null_sum[pl.ds(index * HEADS + step * PER_STEP + i, 1), :] = term[rows : rows + 1]

    @pl.when(step == STEPS - 1)
    def _():
        total = null_sum[...]
        peers = null_grad_ref.shape[0] // total.shape[0]
        copies = jnp.broadcast_to(total[None], (peers, *total.shape))
        null_grad_ref[...] = copies.reshape(null_grad_ref.shape).astype(jnp.bfloat16)


def block(*lead):
    return pl.BlockSpec((*lead, WIDE), lambda i: (0,) * len(lead) + (i,))


def whole(shape):
    return pl.BlockSpec(shape, lambda i: (0,) * len(shape))


def heads_call(q, g, far, near_parts, null_rows, null_flip, bias, valid, peers):
    video_rows, width = q.shape
    audio_rows = video_rows // 2
    wide = jax.ShapeDtypeStruct((video_rows, width), jnp.bfloat16)
    terms = [jax.ShapeDtypeStruct((2, audio_rows, width), jnp.bfloat16)] * 3
    null_shape = (peers * 2 * HEADS, HEAD)
    deep = pl.BlockSpec((WIDE, video_rows), lambda i: (i, 0))
    pairs = pl.BlockSpec((PER_STEP, 2 * audio_rows, video_rows), lambda i: (i, 0, 0))
    return pl.pallas_call(
        heads_kernel,
        grid=(STEPS,),
        in_specs=[block(video_rows)] * 3
        + [deep, deep, pairs, pairs, deep]
        + [
            pl.BlockSpec((PER_STEP, 8, video_rows), lambda i: (i, 0, 0)),
            pl.BlockSpec((PER_STEP, *null_rows.shape[1:]), lambda i: (i, 0, 0, 0)),
            pl.BlockSpec((PER_STEP, *null_flip.shape[1:]), lambda i: (i, 0, 0, 0)),
            whole(bias.shape),
            whole(valid.shape),
        ],
        out_specs=[block(video_rows)] * 2 + [block(2, audio_rows)] * 3 + [whole(null_shape)],
        out_shape=[wide, wide, *terms, jax.ShapeDtypeStruct(null_shape, jnp.bfloat16)],
        scratch_shapes=[pltpu.VMEM((2 * HEADS, HEAD), jnp.float32)],
        compiler_params=pltpu.CompilerParams(vmem_limit_bytes=HEADS_LIMIT),
        cost_estimate=pl.CostEstimate(
            flops=12 * bias.size * width, bytes_accessed=9_000_000, transcendentals=bias.size * HEADS
        ),
        name="heads",
    )(q, g, far, *near_parts, null_rows, null_flip, bias, valid)


def add_kernel(a_ref, b_ref, *out_refs):
    total = a_ref[...].astype(jnp.float32) + b_ref[...].astype(jnp.float32)
    if len(out_refs) == 1:
        out_refs[0][...] = total.astype(jnp.bfloat16)
    else:
        for i, ref in enumerate(out_refs):
            ref[...] = total[i].astype(jnp.bfloat16)


def add_call(a, b, split, work, name):
    _, rows, width = a.shape
    steps = 3
    both = pl.BlockSpec((2, rows, width // steps), lambda i: (0, 0, i))
    one = pl.BlockSpec((rows, width // steps), lambda i: (0, i))
    single = jax.ShapeDtypeStruct((rows, width), jnp.bfloat16)
    return pl.pallas_call(
        add_kernel,
        grid=(steps,),
        in_specs=[both, both],
        out_specs=[one, one] if split else both,
        out_shape=[single, single] if split else jax.ShapeDtypeStruct(a.shape, jnp.bfloat16),
        compiler_params=pltpu.CompilerParams(vmem_limit_bytes=ADD_LIMIT),
        cost_estimate=pl.CostEstimate(flops=a.size, bytes_accessed=work, transcendentals=0),
        name=name,
    )(a, b)


def sum_peers(parts):
    return jnp.sum(parts.astype(jnp.float32), axis=0)


def body(video_query, audio_key, audio_value, null_kv, audio_keep, clip_lengths, out_grad):
    audio_rows = audio_key.shape[0]
    video_rows = video_query.shape[0]
    shards = lax.axis_size(SEQ)
    seq_index = lax.axis_index(SEQ)
    total_audio = audio_rows * shards

    stacked = jnp.stack([audio_key, audio_value]).reshape(2 * audio_rows, -1)
    far = swap_link(stacked)

    bounds = jnp.cumsum(clip_lengths[0])
    pad_segment = clip_lengths.shape[1] - 1
    query_pos = seq_index * video_rows + jnp.arange(video_rows, dtype=jnp.int32)
    side = 1 - 2 * (seq_index % 2)
    starts = [(seq_index + move) * audio_rows for move in (-side, 0, side)]
    own_pos = jnp.arange(audio_rows, dtype=jnp.int32)
    key_pos = jnp.concatenate([start + own_pos for start in starts])
    keep_padded = jnp.pad(audio_keep, (audio_rows, audio_rows))
    keep_rows = jnp.concatenate(
        [lax.dynamic_slice_in_dim(keep_padded, start + audio_rows, audio_rows) for start in starts]
    )
    allowed = allowed_pairs(
        query_pos, key_pos, bounds, keep_rows, total_audio, pad_segment, audio_rows
    )
    near_bias = jnp.where(allowed[audio_rows:], 0.0, MASKED).astype(jnp.float32)
    null_allowed = jnp.broadcast_to(jnp.arange(NULL_ROWS)[:, None] == 0, (NULL_ROWS, video_rows))
    far_allowed = jnp.concatenate([allowed[:audio_rows], null_allowed])
    bias = jnp.where(far_allowed, 0.0, MASKED).astype(jnp.float32)
    valid = (segment_of(query_pos // 2, bounds) < pad_segment).astype(jnp.float32)[None]
    null_heads = null_kv.reshape(2, HEADS, HEAD).swapaxes(0, 1)
    first_only = jnp.arange(NULL_ROWS) == 0
    null_rows = jnp.where(first_only[:, None], null_heads[:, :, None], jnp.bfloat16(0))
    null_flip = jnp.where(first_only, null_heads[..., None], jnp.bfloat16(0))

    stacked, valid = lax.optimization_barrier((stacked, valid))
    near = swap_chip(stacked)

    wide_axes, deep_axes = ("yh", "yl", "x"), ("z", "core")
    q_held, g_held, *near_parts = prepare_call(video_query, out_grad, stacked, near, near_bias)
    attended, query_grad, far_grad, own_grad, near_grad, null_copies = heads_call(
        q_held, g_held, far, near_parts, null_rows, null_flip, bias, valid, lax.axis_size(wide_axes)
    )
    far_back = swap_link(far_grad)
    first = lax.all_to_all(null_copies.reshape(-1, 2 * HEADS, HEAD), wide_axes, 0, 0)
    partial = sum_peers(first).astype(jnp.bfloat16)
    copies = jnp.broadcast_to(partial[None], (lax.axis_size(deep_axes), *partial.shape))
    copies, near_grad = lax.optimization_barrier((copies, near_grad))
    near_back = swap_chip(near_grad)
    second = lax.all_to_all(copies, deep_axes, 0, 0)
    part = add_call(own_grad, far_back, False, 4_000_000, "add_far")
    grads = add_call(part, near_back, True, 2_400_000, "add_near")
    second, *grads = lax.optimization_barrier((second, *grads))
    null_grad = sum_peers(second).reshape(null_kv.shape)
    return (attended, query_grad, grads[0], grads[1], null_grad)


def solution(mesh):
    parts = CLIP_PARTS + SEQ_PARTS
    fine = Mesh(
        np.asarray(mesh.devices).reshape([size for _, size in parts]), [name for name, _ in parts]
    )
    rows = P(CLIP + SEQ, None)
    return jax.shard_map(
        body,
        mesh=fine,
        in_specs=(rows, rows, rows, P(), P(CLIP), P(CLIP, None), rows),
        out_specs=(rows, rows, rows, rows, P()),
        check_vma=False,
    )
```

```python
import numpy as np

import jax
import jax.numpy as jnp
from jax import lax
from jax.experimental import pallas as pl
from jax.experimental.pallas import tpu as pltpu
from jax.sharding import Mesh
from jax.sharding import PartitionSpec as P

HEADS = 12
HEAD = 128
NULL_ROWS = 16
MASKED = -1e30
FACTOR = HEAD**-0.5
LOG2E = 1.4426950408889634
CLIP_PARTS = (("yh", 2), ("z", 8))
SEQ_PARTS = (("yl", 4), ("x", 4), ("core", 2))
CLIP = tuple(name for name, _ in CLIP_PARTS)
SEQ = tuple(name for name, _ in SEQ_PARTS)
HEADS_LIMIT = 36 * 1024 * 1024
PREPARE_LIMIT = 24 * 1024 * 1024
ADD_LIMIT = 8 * 1024 * 1024
PER_STEP = 6
STEPS = HEADS // PER_STEP
WIDE = PER_STEP * HEAD


def swap_chip(block):
    count = lax.axis_size(SEQ)
    return lax.ppermute(block, SEQ, [(i, i ^ 1) for i in range(count)])


def swap_link(block):
    last = lax.axis_size(SEQ) - 1
    pairs = [(i, i + 1) for i in range(1, last, 2)]
    return lax.ppermute(block, SEQ, pairs + [(b, a) for a, b in pairs])


def segment_of(positions, bounds):
    return jnp.sum((positions[:, None] >= bounds[None, :-1]).astype(jnp.int32), axis=1)


def allowed_pairs(query_pos, key_pos, bounds, keep_rows, total_audio, pad_segment, window):
    key_clip = jnp.clip(key_pos, 0, total_audio - 1)
    key_seg = segment_of(key_clip, bounds)
    query_seg = segment_of(query_pos // 2, bounds)
    key_inside = (
        (key_pos >= 0) & (key_pos < total_audio) & (keep_rows == 1) & (key_seg < pad_segment)
    )
    nearby = jnp.abs(query_pos[None, :] - 2 * key_pos[:, None]) <= 2 * window
    return key_inside[:, None] & (key_seg[:, None] == query_seg[None, :]) & nearby


def dot(a, b, lhs_dim, rhs_dim):
    return lax.dot_general(
        a, b, (((lhs_dim,), (rhs_dim,)), ((), ())), preferred_element_type=jnp.float32
    )


def prepare_kernel(
    q_in, g_in, own_ref, near_ref, bias_ref,
    q_ref, g_ref, g_flip, keys_flip, exponent_ref, prob_grad_ref, mixed_ref, stats_ref,
):
    rows = own_ref.shape[0] // 2
    parts = range(PER_STEP)
    cols = [slice(i * HEAD, (i + 1) * HEAD) for i in parts]
    sides = (own_ref, near_ref)
    keys, values = [
        [jnp.concatenate([ref[span, cols[i]] for ref in sides], axis=0) for i in parts]
        for span in (slice(0, rows), slice(rows, 2 * rows))
    ]
    scores = [dot(keys[i], q_in[:, cols[i]], 1, 1) + bias_ref[...] for i in parts]
    tops = [jnp.max(x, axis=0, keepdims=True) for x in scores]
    exact = [jnp.exp2((x - top) * (FACTOR * LOG2E)) for x, top in zip(scores, tops)]
    exponents = [x.astype(jnp.bfloat16) for x in exact]
    for i in parts:
        stats_ref[i, 0:1] = tops[i]
        stats_ref[i, 1:2] = jnp.sum(exact[i], axis=0, keepdims=True)
        exponent_ref[i] = exponents[i]
        prob_grad_ref[i] = dot(values[i], g_in[:, cols[i]], 1, 1)
        mixed_ref[cols[i], :] = dot(values[i].T, exponents[i], 1, 0)
        keys_flip[cols[i], :] = keys[i].T
        g_flip[cols[i], :] = g_in[:, cols[i]].T
    q_ref[...] = q_in[...]
    g_ref[...] = g_in[...]


def prepare_call(q, g, own, near, bias):
    video_rows, width = q.shape
    local_rows = bias.shape[0]
    deep = pl.BlockSpec((WIDE, video_rows), lambda i: (i, 0))
    deep_shape = (width, video_rows)
    pairs = pl.BlockSpec((PER_STEP, local_rows, video_rows), lambda i: (i, 0, 0))
    pair_shape = (HEADS, local_rows, video_rows)
    outs = [
        (block(video_rows), q.shape, jnp.bfloat16),
        (block(video_rows), g.shape, jnp.bfloat16),
        (deep, deep_shape, jnp.bfloat16),
        (deep, deep_shape, jnp.bfloat16),
        (pairs, pair_shape, jnp.bfloat16),
        (pairs, pair_shape, jnp.float32),
        (deep, deep_shape, jnp.float32),
        (pl.BlockSpec((PER_STEP, 8, video_rows), lambda i: (i, 0, 0)), (HEADS, 8, video_rows), jnp.float32),
    ]
    return pl.pallas_call(
        prepare_kernel,
        grid=(STEPS,),
        in_specs=[block(video_rows)] * 4 + [whole(bias.shape)],
        out_specs=[spec for spec, _, _ in outs],
        out_shape=[jax.ShapeDtypeStruct(shape, dtype) for _, shape, dtype in outs],
        compiler_params=pltpu.CompilerParams(vmem_limit_bytes=PREPARE_LIMIT),
        cost_estimate=pl.CostEstimate(
            flops=6 * bias.size * width, bytes_accessed=9_000_000, transcendentals=bias.size * HEADS
        ),
        name="prepare",
    )(q, g, own, near, bias)


def heads_kernel(
    q_ref, g_ref, far_ref, g_flip, near_keys_flip, near_exponent, near_prob_grad, near_mixed, stats,
    null_ref, null_flip, bias_ref, valid_ref,
    out_ref, dq_ref, far_grad_ref, own_grad_ref, near_grad_ref, null_grad_ref, null_sum,
):
    step = pl.program_id(0)
    rows = far_ref.shape[0] // 2
    parts = range(PER_STEP)
    cols = [slice(i * HEAD, (i + 1) * HEAD) for i in parts]
    spans = (slice(0, rows), slice(rows, 2 * rows))
    keys, values = [
        [jnp.concatenate([far_ref[span, cols[i]], null_ref[i, index]], axis=0) for i in parts]
        for index, span in enumerate(spans)
    ]
    keys_flip, values_flip = [
        [jnp.concatenate([far_ref[span, cols[i]].T, null_flip[i, index]], axis=1) for i in parts]
        for index, span in enumerate(spans)
    ]
    scale = FACTOR * LOG2E
    scores = [dot(keys[i], q_ref[:, cols[i]], 1, 1) + bias_ref[...] for i in parts]
    tops = [
        jnp.maximum(jnp.max(x, axis=0, keepdims=True), stats[i, 0:1]) for i, x in enumerate(scores)
    ]
    exact = [jnp.exp2((x - top) * scale) for x, top in zip(scores, tops)]
    joins = [jnp.exp2((stats[i, 0:1] - tops[i]) * scale) for i in parts]
    totals = [
        jnp.sum(x, axis=0, keepdims=True) + joins[i] * stats[i, 1:2] for i, x in enumerate(exact)
    ]
    shares = [valid_ref[...] / total for total in totals]
    near_shares = [share * join for share, join in zip(shares, joins)]
    exponents = [x.astype(jnp.bfloat16) for x in exact]
    flips = [g_flip[cols[i], :].astype(jnp.float32) for i in parts]
    mixed = [
        dot(values_flip[i], exponents[i], 1, 0) * shares[i] + near_mixed[cols[i], :] * near_shares[i]
        for i in parts
    ]
    deltas = [jnp.sum(x * flip, axis=0, keepdims=True) for x, flip in zip(mixed, flips)]
    prob_grads = [dot(values[i], g_ref[:, cols[i]], 1, 1) for i in parts]
    score_grads = [
        ((prob_grads[i] - deltas[i]) * (shares[i] * FACTOR)).astype(jnp.bfloat16) * exponents[i]
        for i in parts
    ]
    near_score_grads = [
        ((near_prob_grad[i] - deltas[i]) * (near_shares[i] * FACTOR)).astype(jnp.bfloat16)
        * near_exponent[i]
        for i in parts
    ]
    for i in parts:
        out_ref[:, cols[i]] = mixed[i].astype(jnp.bfloat16).T
        query_grad = dot(keys_flip[i], score_grads[i], 1, 0)
        query_grad = query_grad + dot(near_keys_flip[cols[i], :], near_score_grads[i], 1, 0)
        dq_ref[:, cols[i]] = query_grad.astype(jnp.bfloat16).T
        q = q_ref[:, cols[i]]
        terms = (
            (dot(score_grads[i], q, 1, 0), dot(near_score_grads[i], q, 1, 0)),
            (
                dot(exponents[i], (flips[i] * shares[i]).astype(jnp.bfloat16), 1, 1),
                dot(near_exponent[i], (flips[i] * near_shares[i]).astype(jnp.bfloat16), 1, 1),
            ),
        )
        for index, (term, near_term) in enumerate(terms):
            far_grad_ref[index, :, cols[i]] = term[:rows].astype(jnp.bfloat16)
            own_grad_ref[index, :, cols[i]] = near_term[:rows].astype(jnp.bfloat16)
            near_grad_ref[index, :, cols[i]] = near_term[rows:].astype(jnp.bfloat16)
            null_sum[pl.ds(index * HEADS + step * PER_STEP + i, 1), :] = term[rows : rows + 1]

    @pl.when(step == STEPS - 1)
    def _():
        total = null_sum[...]
        peers = null_grad_ref.shape[0] // total.shape[0]
        copies = jnp.broadcast_to(total[None], (peers, *total.shape))
        null_grad_ref[...] = copies.reshape(null_grad_ref.shape).astype(jnp.bfloat16)


def block(*lead):
    return pl.BlockSpec((*lead, WIDE), lambda i: (0,) * len(lead) + (i,))


def whole(shape):
    return pl.BlockSpec(shape, lambda i: (0,) * len(shape))


def heads_call(q, g, far, near_parts, null_rows, null_flip, bias, valid, peers):
    video_rows, width = q.shape
    audio_rows = video_rows // 2
    wide = jax.ShapeDtypeStruct((video_rows, width), jnp.bfloat16)
    terms = [jax.ShapeDtypeStruct((2, audio_rows, width), jnp.bfloat16)] * 3
    null_shape = (peers * 2 * HEADS, HEAD)
    deep = pl.BlockSpec((WIDE, video_rows), lambda i: (i, 0))
    pairs = pl.BlockSpec((PER_STEP, 2 * audio_rows, video_rows), lambda i: (i, 0, 0))
    return pl.pallas_call(
        heads_kernel,
        grid=(STEPS,),
        in_specs=[block(video_rows)] * 3
        + [deep, deep, pairs, pairs, deep]
        + [
            pl.BlockSpec((PER_STEP, 8, video_rows), lambda i: (i, 0, 0)),
            pl.BlockSpec((PER_STEP, *null_rows.shape[1:]), lambda i: (i, 0, 0, 0)),
            pl.BlockSpec((PER_STEP, *null_flip.shape[1:]), lambda i: (i, 0, 0, 0)),
            whole(bias.shape),
            whole(valid.shape),
        ],
        out_specs=[block(video_rows)] * 2 + [block(2, audio_rows)] * 3 + [whole(null_shape)],
        out_shape=[wide, wide, *terms, jax.ShapeDtypeStruct(null_shape, jnp.bfloat16)],
        scratch_shapes=[pltpu.VMEM((2 * HEADS, HEAD), jnp.float32)],
        compiler_params=pltpu.CompilerParams(vmem_limit_bytes=HEADS_LIMIT),
        cost_estimate=pl.CostEstimate(
            flops=12 * bias.size * width, bytes_accessed=9_000_000, transcendentals=bias.size * HEADS
        ),
        name="heads",
    )(q, g, far, *near_parts, null_rows, null_flip, bias, valid)


def add_kernel(a_ref, b_ref, *out_refs):
    total = a_ref[...].astype(jnp.float32) + b_ref[...].astype(jnp.float32)
    if len(out_refs) == 1:
        out_refs[0][...] = total.astype(jnp.bfloat16)
    else:
        for i, ref in enumerate(out_refs):
            ref[...] = total[i].astype(jnp.bfloat16)


def add_call(a, b, split, work, name):
    _, rows, width = a.shape
    steps = 3
    both = pl.BlockSpec((2, rows, width // steps), lambda i: (0, 0, i))
    one = pl.BlockSpec((rows, width // steps), lambda i: (0, i))
    single = jax.ShapeDtypeStruct((rows, width), jnp.bfloat16)
    return pl.pallas_call(
        add_kernel,
        grid=(steps,),
        in_specs=[both, both],
        out_specs=[one, one] if split else both,
        out_shape=[single, single] if split else jax.ShapeDtypeStruct(a.shape, jnp.bfloat16),
        compiler_params=pltpu.CompilerParams(vmem_limit_bytes=ADD_LIMIT),
        cost_estimate=pl.CostEstimate(flops=a.size, bytes_accessed=work, transcendentals=0),
        name=name,
    )(a, b)


def sum_peers(parts):
    return jnp.sum(parts.astype(jnp.float32), axis=0)


def body(video_query, audio_key, audio_value, null_kv, audio_keep, clip_lengths, out_grad):
    audio_rows = audio_key.shape[0]
    video_rows = video_query.shape[0]
    shards = lax.axis_size(SEQ)
    seq_index = lax.axis_index(SEQ)
    total_audio = audio_rows * shards

    stacked = jnp.stack([audio_key, audio_value]).reshape(2 * audio_rows, -1)
    far = swap_link(stacked)

    bounds = jnp.cumsum(clip_lengths[0])
    pad_segment = clip_lengths.shape[1] - 1
    query_pos = seq_index * video_rows + jnp.arange(video_rows, dtype=jnp.int32)
    side = 1 - 2 * (seq_index % 2)
    starts = [(seq_index + move) * audio_rows for move in (-side, 0, side)]
    own_pos = jnp.arange(audio_rows, dtype=jnp.int32)
    key_pos = jnp.concatenate([start + own_pos for start in starts])
    keep_padded = jnp.pad(audio_keep, (audio_rows, audio_rows))
    keep_rows = jnp.concatenate(
        [lax.dynamic_slice_in_dim(keep_padded, start + audio_rows, audio_rows) for start in starts]
    )
    allowed = allowed_pairs(
        query_pos, key_pos, bounds, keep_rows, total_audio, pad_segment, audio_rows
    )
    near_bias = jnp.where(allowed[audio_rows:], 0.0, MASKED).astype(jnp.float32)
    null_allowed = jnp.broadcast_to(jnp.arange(NULL_ROWS)[:, None] == 0, (NULL_ROWS, video_rows))
    far_allowed = jnp.concatenate([allowed[:audio_rows], null_allowed])
    bias = jnp.where(far_allowed, 0.0, MASKED).astype(jnp.float32)
    valid = (segment_of(query_pos // 2, bounds) < pad_segment).astype(jnp.float32)[None]
    null_heads = null_kv.reshape(2, HEADS, HEAD).swapaxes(0, 1)
    first_only = jnp.arange(NULL_ROWS) == 0
    null_rows = jnp.where(first_only[:, None], null_heads[:, :, None], jnp.bfloat16(0))
    null_flip = jnp.where(first_only, null_heads[..., None], jnp.bfloat16(0))

    stacked, valid = lax.optimization_barrier((stacked, valid))
    near = swap_chip(stacked)

    wide_axes, deep_axes = ("z", "x"), ("yh", "yl", "core")
    q_held, g_held, *near_parts = prepare_call(video_query, out_grad, stacked, near, near_bias)
    attended, query_grad, far_grad, own_grad, near_grad, null_copies = heads_call(
        q_held, g_held, far, near_parts, null_rows, null_flip, bias, valid, lax.axis_size(wide_axes)
    )
    far_back = swap_link(far_grad)
    first = lax.all_to_all(null_copies.reshape(-1, 2 * HEADS, HEAD), wide_axes, 0, 0)
    partial = sum_peers(first).astype(jnp.bfloat16)
    copies = jnp.broadcast_to(partial[None], (lax.axis_size(deep_axes), *partial.shape))
    copies, near_grad = lax.optimization_barrier((copies, near_grad))
    near_back = swap_chip(near_grad)
    second = lax.all_to_all(copies, deep_axes, 0, 0)
    part = add_call(own_grad, far_back, False, 4_000_000, "add_far")
    grads = add_call(part, near_back, True, 2_400_000, "add_near")
    second, *grads = lax.optimization_barrier((second, *grads))
    null_grad = sum_peers(second).reshape(null_kv.shape)
    return (attended, query_grad, grads[0], grads[1], null_grad)


def solution(mesh):
    parts = CLIP_PARTS + SEQ_PARTS
    fine = Mesh(
        np.asarray(mesh.devices).reshape([size for _, size in parts]), [name for name, _ in parts]
    )
    rows = P(CLIP + SEQ, None)
    return jax.shard_map(
        body,
        mesh=fine,
        in_specs=(rows, rows, rows, P(), P(CLIP), P(CLIP, None), rows),
        out_specs=(rows, rows, rows, rows, P()),
        check_vma=False,
    )
```

```python
import numpy as np

import jax
import jax.numpy as jnp
from jax import lax
from jax.experimental import pallas as pl
from jax.experimental.pallas import tpu as pltpu
from jax.sharding import Mesh
from jax.sharding import PartitionSpec as P

HEADS = 12
HEAD = 128
NULL_ROWS = 16
MASKED = -1e30
FACTOR = HEAD**-0.5
LOG2E = 1.4426950408889634
CLIP_PARTS = (("yh", 2), ("z", 8))
SEQ_PARTS = (("yl", 4), ("x", 4), ("core", 2))
CLIP = tuple(name for name, _ in CLIP_PARTS)
SEQ = tuple(name for name, _ in SEQ_PARTS)
HEADS_LIMIT = 36 * 1024 * 1024
PREPARE_LIMIT = 24 * 1024 * 1024
ADD_LIMIT = 8 * 1024 * 1024
PER_STEP = 6
STEPS = HEADS // PER_STEP
WIDE = PER_STEP * HEAD


def swap_chip(block):
    count = lax.axis_size(SEQ)
    return lax.ppermute(block, SEQ, [(i, i ^ 1) for i in range(count)])


def swap_link(block):
    last = lax.axis_size(SEQ) - 1
    pairs = [(i, i + 1) for i in range(1, last, 2)]
    return lax.ppermute(block, SEQ, pairs + [(b, a) for a, b in pairs])


def segment_of(positions, bounds):
    return jnp.sum((positions[:, None] >= bounds[None, :-1]).astype(jnp.int32), axis=1)


def allowed_pairs(query_pos, key_pos, bounds, keep_rows, total_audio, pad_segment, window):
    key_clip = jnp.clip(key_pos, 0, total_audio - 1)
    key_seg = segment_of(key_clip, bounds)
    query_seg = segment_of(query_pos // 2, bounds)
    key_inside = (
        (key_pos >= 0) & (key_pos < total_audio) & (keep_rows == 1) & (key_seg < pad_segment)
    )
    nearby = jnp.abs(query_pos[None, :] - 2 * key_pos[:, None]) <= 2 * window
    return key_inside[:, None] & (key_seg[:, None] == query_seg[None, :]) & nearby


def dot(a, b, lhs_dim, rhs_dim):
    return lax.dot_general(
        a, b, (((lhs_dim,), (rhs_dim,)), ((), ())), preferred_element_type=jnp.float32
    )


def prepare_kernel(
    q_in, g_in, own_ref, near_ref, bias_ref,
    q_ref, g_ref, g_flip, keys_flip, exponent_ref, prob_grad_ref, mixed_ref, stats_ref,
):
    rows = own_ref.shape[0] // 2
    parts = range(PER_STEP)
    cols = [slice(i * HEAD, (i + 1) * HEAD) for i in parts]
    sides = (own_ref, near_ref)
    keys, values = [
        [jnp.concatenate([ref[span, cols[i]] for ref in sides], axis=0) for i in parts]
        for span in (slice(0, rows), slice(rows, 2 * rows))
    ]
    scores = [dot(keys[i], q_in[:, cols[i]], 1, 1) + bias_ref[...] for i in parts]
    tops = [jnp.max(x, axis=0, keepdims=True) for x in scores]
    exact = [jnp.exp2((x - top) * (FACTOR * LOG2E)) for x, top in zip(scores, tops)]
    exponents = [x.astype(jnp.bfloat16) for x in exact]
    for i in parts:
        stats_ref[i, 0:1] = tops[i]
        stats_ref[i, 1:2] = jnp.sum(exact[i], axis=0, keepdims=True)
        exponent_ref[i] = exponents[i]
        prob_grad_ref[i] = dot(values[i], g_in[:, cols[i]], 1, 1)
        mixed_ref[cols[i], :] = dot(values[i].T, exponents[i], 1, 0)
        keys_flip[cols[i], :] = keys[i].T
        g_flip[cols[i], :] = g_in[:, cols[i]].T
    q_ref[...] = q_in[...]
    g_ref[...] = g_in[...]


def prepare_call(q, g, own, near, bias):
    video_rows, width = q.shape
    local_rows = bias.shape[0]
    deep = pl.BlockSpec((WIDE, video_rows), lambda i: (i, 0))
    deep_shape = (width, video_rows)
    pairs = pl.BlockSpec((PER_STEP, local_rows, video_rows), lambda i: (i, 0, 0))
    pair_shape = (HEADS, local_rows, video_rows)
    outs = [
        (block(video_rows), q.shape, jnp.bfloat16),
        (block(video_rows), g.shape, jnp.bfloat16),
        (deep, deep_shape, jnp.bfloat16),
        (deep, deep_shape, jnp.bfloat16),
        (pairs, pair_shape, jnp.bfloat16),
        (pairs, pair_shape, jnp.float32),
        (deep, deep_shape, jnp.float32),
        (pl.BlockSpec((PER_STEP, 8, video_rows), lambda i: (i, 0, 0)), (HEADS, 8, video_rows), jnp.float32),
    ]
    return pl.pallas_call(
        prepare_kernel,
        grid=(STEPS,),
        in_specs=[block(video_rows)] * 4 + [whole(bias.shape)],
        out_specs=[spec for spec, _, _ in outs],
        out_shape=[jax.ShapeDtypeStruct(shape, dtype) for _, shape, dtype in outs],
        compiler_params=pltpu.CompilerParams(vmem_limit_bytes=PREPARE_LIMIT),
        cost_estimate=pl.CostEstimate(
            flops=6 * bias.size * width, bytes_accessed=9_000_000, transcendentals=bias.size * HEADS
        ),
        name="prepare",
    )(q, g, own, near, bias)


def heads_kernel(
    q_ref, g_ref, far_ref, g_flip, near_keys_flip, near_exponent, near_prob_grad, near_mixed, stats,
    null_ref, null_flip, bias_ref, valid_ref,
    out_ref, dq_ref, far_grad_ref, own_grad_ref, near_grad_ref, null_grad_ref, null_sum,
):
    step = pl.program_id(0)
    rows = far_ref.shape[0] // 2
    parts = range(PER_STEP)
    cols = [slice(i * HEAD, (i + 1) * HEAD) for i in parts]
    spans = (slice(0, rows), slice(rows, 2 * rows))
    keys, values = [
        [jnp.concatenate([far_ref[span, cols[i]], null_ref[i, index]], axis=0) for i in parts]
        for index, span in enumerate(spans)
    ]
    keys_flip, values_flip = [
        [jnp.concatenate([far_ref[span, cols[i]].T, null_flip[i, index]], axis=1) for i in parts]
        for index, span in enumerate(spans)
    ]
    scale = FACTOR * LOG2E
    scores = [dot(keys[i], q_ref[:, cols[i]], 1, 1) + bias_ref[...] for i in parts]
    tops = [
        jnp.maximum(jnp.max(x, axis=0, keepdims=True), stats[i, 0:1]) for i, x in enumerate(scores)
    ]
    exact = [jnp.exp2((x - top) * scale) for x, top in zip(scores, tops)]
    joins = [jnp.exp2((stats[i, 0:1] - tops[i]) * scale) for i in parts]
    totals = [
        jnp.sum(x, axis=0, keepdims=True) + joins[i] * stats[i, 1:2] for i, x in enumerate(exact)
    ]
    shares = [valid_ref[...] / total for total in totals]
    near_shares = [share * join for share, join in zip(shares, joins)]
    exponents = [x.astype(jnp.bfloat16) for x in exact]
    flips = [g_flip[cols[i], :].astype(jnp.float32) for i in parts]
    mixed = [
        dot(values_flip[i], exponents[i], 1, 0) * shares[i] + near_mixed[cols[i], :] * near_shares[i]
        for i in parts
    ]
    deltas = [jnp.sum(x * flip, axis=0, keepdims=True) for x, flip in zip(mixed, flips)]
    prob_grads = [dot(values[i], g_ref[:, cols[i]], 1, 1) for i in parts]
    score_grads = [
        ((prob_grads[i] - deltas[i]) * (shares[i] * FACTOR)).astype(jnp.bfloat16) * exponents[i]
        for i in parts
    ]
    near_score_grads = [
        ((near_prob_grad[i] - deltas[i]) * (near_shares[i] * FACTOR)).astype(jnp.bfloat16)
        * near_exponent[i]
        for i in parts
    ]
    for i in parts:
        out_ref[:, cols[i]] = mixed[i].astype(jnp.bfloat16).T
        query_grad = dot(keys_flip[i], score_grads[i], 1, 0)
        query_grad = query_grad + dot(near_keys_flip[cols[i], :], near_score_grads[i], 1, 0)
        dq_ref[:, cols[i]] = query_grad.astype(jnp.bfloat16).T
        q = q_ref[:, cols[i]]
        terms = (
            (dot(score_grads[i], q, 1, 0), dot(near_score_grads[i], q, 1, 0)),
            (
                dot(exponents[i], (flips[i] * shares[i]).astype(jnp.bfloat16), 1, 1),
                dot(near_exponent[i], (flips[i] * near_shares[i]).astype(jnp.bfloat16), 1, 1),
            ),
        )
        for index, (term, near_term) in enumerate(terms):
            far_grad_ref[index, :, cols[i]] = term[:rows].astype(jnp.bfloat16)
            own_grad_ref[index, :, cols[i]] = near_term[:rows].astype(jnp.bfloat16)
            near_grad_ref[index, :, cols[i]] = near_term[rows:].astype(jnp.bfloat16)
            null_sum[pl.ds(index * HEADS + step * PER_STEP + i, 1), :] = term[rows : rows + 1]

    @pl.when(step == STEPS - 1)
    def _():
        total = null_sum[...]
        peers = null_grad_ref.shape[0] // total.shape[0]
        copies = jnp.broadcast_to(total[None], (peers, *total.shape))
        null_grad_ref[...] = copies.reshape(null_grad_ref.shape).astype(jnp.bfloat16)


def block(*lead):
    return pl.BlockSpec((*lead, WIDE), lambda i: (0,) * len(lead) + (i,))


def whole(shape):
    return pl.BlockSpec(shape, lambda i: (0,) * len(shape))


def heads_call(q, g, far, near_parts, null_rows, null_flip, bias, valid, peers):
    video_rows, width = q.shape
    audio_rows = video_rows // 2
    wide = jax.ShapeDtypeStruct((video_rows, width), jnp.bfloat16)
    terms = [jax.ShapeDtypeStruct((2, audio_rows, width), jnp.bfloat16)] * 3
    null_shape = (peers * 2 * HEADS, HEAD)
    deep = pl.BlockSpec((WIDE, video_rows), lambda i: (i, 0))
    pairs = pl.BlockSpec((PER_STEP, 2 * audio_rows, video_rows), lambda i: (i, 0, 0))
    return pl.pallas_call(
        heads_kernel,
        grid=(STEPS,),
        in_specs=[block(video_rows)] * 3
        + [deep, deep, pairs, pairs, deep]
        + [
            pl.BlockSpec((PER_STEP, 8, video_rows), lambda i: (i, 0, 0)),
            pl.BlockSpec((PER_STEP, *null_rows.shape[1:]), lambda i: (i, 0, 0, 0)),
            pl.BlockSpec((PER_STEP, *null_flip.shape[1:]), lambda i: (i, 0, 0, 0)),
            whole(bias.shape),
            whole(valid.shape),
        ],
        out_specs=[block(video_rows)] * 2 + [block(2, audio_rows)] * 3 + [whole(null_shape)],
        out_shape=[wide, wide, *terms, jax.ShapeDtypeStruct(null_shape, jnp.bfloat16)],
        scratch_shapes=[pltpu.VMEM((2 * HEADS, HEAD), jnp.float32)],
        compiler_params=pltpu.CompilerParams(vmem_limit_bytes=HEADS_LIMIT),
        cost_estimate=pl.CostEstimate(
            flops=12 * bias.size * width, bytes_accessed=9_000_000, transcendentals=bias.size * HEADS
        ),
        name="heads",
    )(q, g, far, *near_parts, null_rows, null_flip, bias, valid)


def add_kernel(own_ref, far_ref, near_ref, *out_refs):
    for i, ref in enumerate(out_refs):
        total = own_ref[i].astype(jnp.float32) + far_ref[i].astype(jnp.float32)
        ref[...] = (total + near_ref[i].astype(jnp.float32)).astype(jnp.bfloat16)


def add_call(own, far, near):
    _, rows, width = own.shape
    steps = 3
    both = pl.BlockSpec((2, rows, width // steps), lambda i: (0, 0, i))
    one = pl.BlockSpec((rows, width // steps), lambda i: (0, i))
    single = jax.ShapeDtypeStruct((rows, width), jnp.bfloat16)
    return pl.pallas_call(
        add_kernel,
        grid=(steps,),
        in_specs=[both] * 3,
        out_specs=[one, one],
        out_shape=[single, single],
        compiler_params=pltpu.CompilerParams(vmem_limit_bytes=ADD_LIMIT),
        cost_estimate=pl.CostEstimate(flops=2 * own.size, bytes_accessed=3_200_000, transcendentals=0),
        name="add",
    )(own, far, near)


def sum_peers(parts):
    return jnp.sum(parts.astype(jnp.float32), axis=0)


def body(video_query, audio_key, audio_value, null_kv, audio_keep, clip_lengths, out_grad):
    audio_rows = audio_key.shape[0]
    video_rows = video_query.shape[0]
    shards = lax.axis_size(SEQ)
    seq_index = lax.axis_index(SEQ)
    total_audio = audio_rows * shards

    stacked = jnp.stack([audio_key, audio_value]).reshape(2 * audio_rows, -1)
    far = swap_link(stacked)

    bounds = jnp.cumsum(clip_lengths[0])
    pad_segment = clip_lengths.shape[1] - 1
    query_pos = seq_index * video_rows + jnp.arange(video_rows, dtype=jnp.int32)
    side = 1 - 2 * (seq_index % 2)
    starts = [(seq_index + move) * audio_rows for move in (-side, 0, side)]
    own_pos = jnp.arange(audio_rows, dtype=jnp.int32)
    key_pos = jnp.concatenate([start + own_pos for start in starts])
    keep_padded = jnp.pad(audio_keep, (audio_rows, audio_rows))
    keep_rows = jnp.concatenate(
        [lax.dynamic_slice_in_dim(keep_padded, start + audio_rows, audio_rows) for start in starts]
    )
    allowed = allowed_pairs(
        query_pos, key_pos, bounds, keep_rows, total_audio, pad_segment, audio_rows
    )
    near_bias = jnp.where(allowed[audio_rows:], 0.0, MASKED).astype(jnp.float32)
    null_allowed = jnp.broadcast_to(jnp.arange(NULL_ROWS)[:, None] == 0, (NULL_ROWS, video_rows))
    far_allowed = jnp.concatenate([allowed[:audio_rows], null_allowed])
    bias = jnp.where(far_allowed, 0.0, MASKED).astype(jnp.float32)
    valid = (segment_of(query_pos // 2, bounds) < pad_segment).astype(jnp.float32)[None]
    null_heads = null_kv.reshape(2, HEADS, HEAD).swapaxes(0, 1)
    first_only = jnp.arange(NULL_ROWS) == 0
    null_rows = jnp.where(first_only[:, None], null_heads[:, :, None], jnp.bfloat16(0))
    null_flip = jnp.where(first_only, null_heads[..., None], jnp.bfloat16(0))

    stacked, valid = lax.optimization_barrier((stacked, valid))
    near = swap_chip(stacked)

    wide_axes, deep_axes = ("z", "x"), ("yh", "yl", "core")
    q_held, g_held, *near_parts = prepare_call(video_query, out_grad, stacked, near, near_bias)
    attended, query_grad, far_grad, own_grad, near_grad, null_copies = heads_call(
        q_held, g_held, far, near_parts, null_rows, null_flip, bias, valid, lax.axis_size(wide_axes)
    )
    far_back = swap_link(far_grad)
    first = lax.all_to_all(null_copies.reshape(-1, 2 * HEADS, HEAD), wide_axes, 0, 0)
    partial = sum_peers(first).astype(jnp.bfloat16)
    copies = jnp.broadcast_to(partial[None], (lax.axis_size(deep_axes), *partial.shape))
    copies, near_grad = lax.optimization_barrier((copies, near_grad))
    near_back = swap_chip(near_grad)
    second = lax.all_to_all(copies, deep_axes, 0, 0)
    second, own_grad, far_back, near_back = lax.optimization_barrier(
        (second, own_grad, far_back, near_back)
    )
    grads = add_call(own_grad, far_back, near_back)
    null_grad = sum_peers(second).reshape(null_kv.shape)
    return (attended, query_grad, grads[0], grads[1], null_grad)


def solution(mesh):
    parts = CLIP_PARTS + SEQ_PARTS
    fine = Mesh(
        np.asarray(mesh.devices).reshape([size for _, size in parts]), [name for name, _ in parts]
    )
    rows = P(CLIP + SEQ, None)
    return jax.shard_map(
        body,
        mesh=fine,
        in_specs=(rows, rows, rows, P(), P(CLIP), P(CLIP, None), rows),
        out_specs=(rows, rows, rows, rows, P()),
        check_vma=False,
    )
```
